32 devices in a mesh: section: 2 (over x), dp: 16 (over z, y, core).
Axes of the slice: x: 2, y: 2, z: 4, core: 2. Of those that a mesh axis runs over, the one named last changes fastest.
Arguments:
- tokens: bfloat16 [8192, 768], P('dp'), may hold values from -6 to 6
- cotangent: bfloat16 [8192, 768], P('dp'), may hold values from -6 to 6
- heights: int32 [32], P('dp'), may hold values from 12 to 16
- widths: int32 [32], P('dp'), may hold values from 12 to 16
- qkv_weight: bfloat16 [2, 768, 2304], P('section', 'dp'), may hold values from -0.21875 to 0.21875
- out_weight: bfloat16 [2, 768, 768], P('section', 'dp'), may hold values from -0.875 to 0.875
- up_weight: bfloat16 [2, 768, 3072], P('section', 'dp'), may hold values from -0.21875 to 0.21875
- down_weight: bfloat16 [2, 3072, 768], P('section', 'dp'), may hold values from -0.109375 to 0.109375
- q_bias: bfloat16 [2, 768], P('section', 'dp'), may hold values from -1.5 to 1.5
- v_bias: bfloat16 [2, 768], P('section', 'dp'), may hold values from -1.5 to 1.5
- out_bias: bfloat16 [2, 768], P('section', 'dp'), may hold values from -1.5 to 1.5
- up_bias: bfloat16 [2, 3072], P('section', 'dp'), may hold values from -1.5 to 1.5
- down_bias: bfloat16 [2, 768], P('section', 'dp'), may hold values from -1.5 to 1.5
- gain_one: bfloat16 [2, 768], P('section', 'dp'), may hold values from 0.25 to 1.75
- shift_one: bfloat16 [2, 768], P('section', 'dp'), may hold values from -1.5 to 1.5
- gain_two: bfloat16 [2, 768], P('section', 'dp'), may hold values from 0.25 to 1.75
- shift_two: bfloat16 [2, 768], P('section', 'dp'), may hold values from -1.5 to 1.5
Outputs:
- layer_outputs: bfloat16 [2, 8192, 768], P('section', 'dp')
- input_grads: float32 [2, 8192, 768], P('section', 'dp')
- grad_qkv_weight: float32 [2, 768, 2304], P('section', 'dp')
- grad_out_weight: float32 [2, 768, 768], P('section', 'dp')
- grad_up_weight: float32 [2, 768, 3072], P('section', 'dp')
- grad_down_weight: float32 [2, 3072, 768], P('section', 'dp')
- grad_q_bias: float32 [2, 768], P('section', 'dp')
- grad_v_bias: float32 [2, 768], P('section', 'dp')
- grad_out_bias: float32 [2, 768], P('section', 'dp')
- grad_up_bias: float32 [2, 3072], P('section', 'dp')
- grad_down_bias: float32 [2, 768], P('section', 'dp')
- grad_gain_one: float32 [2, 768], P('section', 'dp')
- grad_shift_one: float32 [2, 768], P('section', 'dp')
- grad_gain_two: float32 [2, 768], P('section', 'dp')
- grad_shift_two: float32 [2, 768], P('section', 'dp')
The draws below stay inside these ranges and needn't reach their ends.
All inputs are finite; a program needn't handle non-finite values.
Results may differ from the reference program's by a relative error of at most 0.014.
Values may be sent and summed in bfloat16 or wider, within the bound.
No kernel may reach another device: no remote copies, remote signals or barrier semaphores. Data moves between devices by JAX's collectives and lax.ppermute only.
A program may use at most 256 MiB of HBM per device.

```python
import jax
import jax.numpy as jnp
from jax import lax

H = 16
HD = 48
D = 768
FF = 3072
GRID = 16
SLOTS = 256
IMAGES = 32
TOKENS = 8192


def plant(values, stream_key, smallest, top_value):
    shape = values.shape
    index_at = [jax.random.randint(jax.random.fold_in(stream_key, axis), (), 0, shape[axis]) for axis in range(len(shape))]
    values = values.at[tuple(index_at)].set(smallest)
    longest = shape.index(max(shape))
    index_at[longest] = (index_at[longest] + 1) % shape[longest]
    return values.at[tuple(index_at)].set(top_value)


def steps_of(stream_key, shape, cuts, smallest, top_value):
    def one(axis_at, shards_of):
        steps = jax.random.uniform(jax.random.fold_in(jax.random.fold_in(stream_key, 6), axis_at), (shards_of,), jnp.float32, smallest / len(cuts), top_value / len(cuts))
        return jnp.repeat(jnp.exp(steps), shape[axis_at] // shards_of).reshape((-1,) + (1,) * (len(shape) - axis_at - 1))

    factor_of = one(*cuts[0])
    for cut in cuts[1:]:
        factor_of = factor_of * one(*cut)
    return factor_of


def scatter_about(rng, extent, scale, most, split=(), kind=jnp.bfloat16):
    array = scale * jax.random.normal(rng, extent, jnp.float32)
    if split:
        array = array * steps_of(rng, extent, split, -0.22, 0.18)
    return jnp.clip(array, -most, most).astype(kind)


def setup_inputs(seed: int = 0) -> dict:
    arg_keys = jax.random.split(jax.random.key(seed), 18)
    return {
        "tokens": scatter_about(arg_keys[0], (TOKENS, D), 1.0, 6.0, ((0, 16),)),
        "cotangent": scatter_about(arg_keys[1], (TOKENS, D), 1.0, 6.0, ((0, 16),)),
        "heights": plant(jax.random.randint(arg_keys[2], (IMAGES,), GRID - GRID // 4, GRID + 1), jax.random.fold_in(arg_keys[2], 1), GRID - GRID // 4, GRID).astype(jnp.int32),
        "widths": plant(jax.random.randint(arg_keys[3], (IMAGES,), GRID - GRID // 4, GRID + 1), jax.random.fold_in(arg_keys[3], 1), GRID - GRID // 4, GRID).astype(jnp.int32),
        "qkv_weight": scatter_about(arg_keys[4], (2, D, 3 * D), D ** -0.5, 0.21875, ((0, 2), (1, 16))),
        "out_weight": scatter_about(arg_keys[5], (2, D, D), (D // 16) ** -0.5, 0.875, ((0, 2), (1, 16))),
        "up_weight": scatter_about(arg_keys[6], (2, D, FF), D ** -0.5, 0.21875, ((0, 2), (1, 16))),
        "down_weight": scatter_about(arg_keys[7], (2, FF, D), FF ** -0.5, 0.109375, ((0, 2), (1, 16))),
        "q_bias": scatter_about(arg_keys[8], (2, D), 0.3, 1.5, ((0, 2), (1, 16))),
        "v_bias": scatter_about(arg_keys[9], (2, D), 0.3, 1.5, ((0, 2), (1, 16))),
        "out_bias": scatter_about(arg_keys[10], (2, D), 0.3, 1.5, ((0, 2), (1, 16))),
        "up_bias": scatter_about(arg_keys[11], (2, FF), 0.3, 1.5, ((0, 2), (1, 16))),
        "down_bias": scatter_about(arg_keys[12], (2, D), 0.3, 1.5, ((0, 2), (1, 16))),
        "gain_one": jnp.clip(1.0 + 0.15 * jax.random.normal(arg_keys[13], (2, D), jnp.float32), 0.25, 1.75).astype(jnp.bfloat16),
        "shift_one": scatter_about(arg_keys[14], (2, D), 0.3, 1.5, ((0, 2), (1, 16))),
        "gain_two": jnp.clip(1.0 + 0.15 * jax.random.normal(arg_keys[15], (2, D), jnp.float32), 0.25, 1.75).astype(jnp.bfloat16),
        "shift_two": scatter_about(arg_keys[16], (2, D), 0.3, 1.5, ((0, 2), (1, 16))),
    }


precise = lax.Precision.HIGHEST
eps_norm = 1e-05

@jax.custom_vjp
def low(v):
    return lax.optimization_barrier(v.astype(jnp.bfloat16)).astype(jnp.float32)

@jax.custom_vjp
def low_back(v):
    return v

def low_keep(v):
    return (low(v), None)

def low_pass(kept, grad):
    return (grad,)

def back_keep(v):
    return (v, None)

def back_low(kept, grad):
    return (low(grad),)
low.defvjp(low_keep, low_pass)
low_back.defvjp(back_keep, back_low)

def layer_norm(values_in, gain_vec, offset_vec):
    average = lax.optimization_barrier(jnp.mean(values_in, axis=-1, keepdims=True))
    centred = values_in - average
    variance = lax.optimization_barrier(jnp.mean(centred * centred, axis=-1, keepdims=True))
    return centred * lax.rsqrt(variance + eps_norm) * gain_vec + offset_vec

def matmul(first_mat, second_mat):
    return jnp.dot(first_mat, second_mat, precision=precise)

def attend_image(element):
    queries, key_rows, values, valid_row = element
    score_scale = HD ** (-0.5)
    scores = jnp.einsum('qhd,khd->hqk', queries, key_rows, precision=precise) * score_scale
    scores = low_back(scores)
    scores = jnp.where(valid_row[None, None, :], scores, -1e+30)
    largest = lax.optimization_barrier(jnp.max(scores, axis=-1, keepdims=True))
    exponent = jnp.exp(scores - largest)
    soft_weights = low(exponent / lax.optimization_barrier(jnp.sum(exponent, axis=-1, keepdims=True)))
    return jnp.einsum('hqk,khd->qhd', soft_weights, values, precision=precise)

def one_layer(layer_input, params, valid_mask):
    qkv_w, out_w, up_w, down_w, bias_q, bias_v, bias_out, bias_up, bias_down, gain_a, offset_a, gain_b, offset_b = params
    row_count = layer_input.shape[0]
    images = row_count // SLOTS
    normed = low(layer_norm(layer_input, gain_a, offset_a))
    projected = matmul(normed, qkv_w)
    queries = low_back(low(projected[:, :D] + bias_q))
    key_rows = low_back(low(projected[:, D:2 * D]))
    values = low_back(low(projected[:, 2 * D:] + bias_v))
    head_shape = (images, SLOTS, H, HD)
    attended = lax.map(jax.checkpoint(attend_image), (queries.reshape(head_shape), key_rows.reshape(head_shape), values.reshape(head_shape), valid_mask))
    attended = low_back(low(attended.reshape(row_count, D)))
    branch = low_back(matmul(attended, out_w) + bias_out)
    middle = layer_input + branch
    second = low(layer_norm(middle, gain_b, offset_b))
    hidden_pre = low_back(matmul(second, up_w) + bias_up)
    activated = low(jax.nn.gelu(hidden_pre, approximate=False))
    mlp_out = low_back(matmul(activated, down_w) + bias_down)
    return middle + mlp_out

def both_layers(params, layer_input, bridge, valid_mask):
    first_params = tuple((weight[0] for weight in params))
    second_params = tuple((weight[1] for weight in params))
    result_one = one_layer(layer_input, first_params, valid_mask)
    inner_input = low_back(low(result_one)) + bridge
    result_two = one_layer(inner_input, second_params, valid_mask)
    return (result_one, result_two)

def reference(tokens, cotangent, heights, widths, qkv_weight, out_weight, up_weight, down_weight, q_bias, v_bias, out_bias, up_bias, down_bias, gain_one, shift_one, gain_two, shift_two):
    weights = tuple((weight.astype(jnp.float32) for weight in (qkv_weight, out_weight, up_weight, down_weight, q_bias, v_bias, out_bias, up_bias, down_bias, gain_one, shift_one, gain_two, shift_two)))
    position = jnp.arange(SLOTS, dtype=jnp.int32)
    valid = ((position // GRID)[None, :] < heights[:, None]) & ((position % GRID)[None, :] < widths[:, None])
    per_group = 16
    groups = IMAGES // per_group
    token_groups = tokens.reshape(groups, per_group * SLOTS, D)
    seed_groups = cotangent.reshape(groups, per_group * SLOTS, D)
    valid_groups = valid.reshape(groups, per_group, SLOTS)

    def step(carry, element):
        token_block, seed_block, valid_block = element
        layer_input = token_block.astype(jnp.float32)
        bridge = jnp.zeros_like(layer_input)

        def run_layers(params, start_values, bridge_values):
            return both_layers(params, start_values, bridge_values, valid_block)
        (result_one, result_two), pullback = jax.vjp(run_layers, weights, layer_input, bridge)
        gradients, grad_input, grad_bridge = pullback((jnp.zeros_like(result_one), seed_block.astype(jnp.float32)))
        carry = tuple((total + grad for total, grad in zip(carry, gradients)))
        return (carry, (result_one.astype(jnp.bfloat16), result_two.astype(jnp.bfloat16), grad_input, grad_bridge))
    initial = tuple((jnp.zeros(weight.shape, jnp.float32) for weight in weights))
    sums, (outs_one, outs_two, grads_one, grads_two) = lax.scan(step, initial, (token_groups, seed_groups, valid_groups))
    layer_outputs = jnp.stack([outs_one.reshape(TOKENS, D), outs_two.reshape(TOKENS, D)])
    input_grads = jnp.stack([grads_one.reshape(TOKENS, D), grads_two.reshape(TOKENS, D)])
    return (layer_outputs, input_grads, sums[0], sums[1], sums[2], sums[3], sums[4], sums[5], sums[6], sums[7], sums[8], sums[9], sums[10], sums[11], sums[12])
```

```python
import functools

import jax
import jax.numpy as jnp
from jax import lax
from jax.experimental import pallas as pl
from jax.experimental.pallas import tpu as pltpu
from jax.sharding import PartitionSpec as P

H = 16
GRID = 16
LEAD = 16
RING = 8
VEC_ROWS = 16

f32 = jnp.float32
bf16 = jnp.bfloat16
eps_norm = 1e-05


def layer_norm(values_in, gain_vec, offset_vec):
    average = jnp.mean(values_in, axis=-1, keepdims=True)
    centred = values_in - average
    variance = jnp.mean(centred * centred, axis=-1, keepdims=True)
    return centred * lax.rsqrt(variance + eps_norm) * gain_vec + offset_vec


def gelu_exact(values_in):
    return jax.nn.gelu(values_in, approximate=False)


def product(first_mat, second_mat):
    return jnp.dot(first_mat, second_mat, preferred_element_type=f32)


def outer_sum(first_mat, second_mat):
    return lax.dot_general(
        first_mat, second_mat, (((0,), (0,)), ((), ())), preferred_element_type=f32
    )


def back_product(first_mat, second_mat):
    return lax.dot_general(
        first_mat, second_mat, (((1,), (1,)), ((), ())), preferred_element_type=f32
    )


def chip_at(place):
    if isinstance(place, int):
        return 2 * place if place < 4 else 2 * (7 - place) + 1
    return jnp.where(place < 4, 2 * place, 2 * (7 - place) + 1)


def place_of(chip):
    if isinstance(chip, int):
        return chip // 2 if chip % 2 == 0 else 7 - chip // 2
    return jnp.where(chip % 2 == 0, chip // 2, 7 - chip // 2)


def ring_route(step):
    return [
        (2 * chip_at(place) + core, 2 * chip_at((place + step) % RING) + core)
        for place in range(RING)
        for core in range(2)
    ]


CORE_ROUTE = [(index, index ^ 1) for index in range(2 * RING)]


def onward(block):
    return lax.ppermute(block, "dp", ring_route(1))


def backward(block):
    return lax.ppermute(block, "dp", ring_route(-1))


def across(block):
    return lax.ppermute(block, "dp", CORE_ROUTE)


def ring_gather(shard):
    half = shard.shape[0] // 2
    here = {0: shard}
    up, down = shard, shard
    for step in range(1, RING // 2):
        up, down = onward(up), backward(down)
        here[RING - step], here[step] = up, down
    far = (onward(up[:half]), backward(down[half:]))
    blocks = []
    for place in range(RING):
        if place == RING // 2:
            blocks += [far[0], far[1], across(far[0]), across(far[1])]
        else:
            blocks += [here[place], across(here[place])]
    return blocks


def assemble(blocks):
    rows, width = blocks[0].shape
    half = rows // 2
    count = len(blocks)

    def kernel(*refs):
        blocks_in, out, sems = refs[:count], refs[count], refs[count + 1]
        me = lax.axis_index("dp")
        core, place = lax.rem(me, 2), place_of(lax.div(me, 2))
        copies = []
        at = 0
        for step in range(RING):
            chip = chip_at(lax.rem(place + step, RING))
            parts = ((0, half), (half, half)) if step == RING // 2 else ((0, rows),)
            for owner in (2 * chip + core, 2 * chip + 1 - core):
                for start, size in parts:
                    copies.append(
                        pltpu.make_async_copy(
                            blocks_in[at], out.at[owner, pl.ds(start, size)], sems.at[at]
                        )
                    )
                    at += 1
        for copy in copies:
            copy.start()
        for copy in copies:
            copy.wait()

    return pl.pallas_call(
        kernel,
        out_shape=jax.ShapeDtypeStruct((2 * RING, rows, width), blocks[0].dtype),
        in_specs=[pl.BlockSpec(memory_space=pl.ANY)] * count,
        out_specs=pl.BlockSpec(memory_space=pl.ANY),
        scratch_shapes=[pltpu.SemaphoreType.DMA((count,))],
        name="assemble",
    )(*blocks)


def dispatch(whole):
    count, rows, width = whole.shape

    def kernel(whole_ref, own_ref, peer_ref, sems):
        me = lax.axis_index("dp")
        core, place = lax.rem(me, 2), place_of(lax.div(me, 2))
        copies = []
        for step in range(RING):
            chip = chip_at(lax.rem(place + step, RING))
            copies.append(
                pltpu.make_async_copy(whole_ref.at[2 * chip + core], own_ref.at[step], sems.at[2 * step])
            )
            copies.append(
                pltpu.make_async_copy(
                    whole_ref.at[2 * chip + 1 - core], peer_ref.at[step], sems.at[2 * step + 1]
                )
            )
        for copy in copies:
            copy.start()
        for copy in copies:
            copy.wait()

    return pl.pallas_call(
        kernel,
        out_shape=[jax.ShapeDtypeStruct((RING, rows, width), whole.dtype)] * 2,
        in_specs=[pl.BlockSpec(memory_space=pl.ANY)],
        out_specs=[pl.BlockSpec(memory_space=pl.ANY)] * 2,
        scratch_shapes=[pltpu.SemaphoreType.DMA((2 * RING,))],
        name="dispatch",
    )(whole)


def ring_scatter(own, peer):
    rows = own.shape[1]
    half = rows // 2
    arrived = across(peer)

    def local(step, start=0, size=rows):
        return own[step, start : start + size].astype(f32) + arrived[step, start : start + size].astype(f32)

    far = RING // 2
    up = onward(local(far, 0, half).astype(bf16))
    down = backward(local(far, half, half).astype(bf16))
    joint_up = jnp.concatenate([local(far - 1, 0, half) + up.astype(f32), local(far - 1, half, half)], 0)
    joint_down = jnp.concatenate([local(far + 1, 0, half), local(far + 1, half, half) + down.astype(f32)], 0)
    up, down = onward(joint_up.astype(bf16)), backward(joint_down.astype(bf16))
    for step in range(far - 2, 0, -1):
        up = onward((local(step) + up.astype(f32)).astype(bf16))
        down = backward((local(RING - step) + down.astype(f32)).astype(bf16))
    return local(0) + up.astype(f32) + down.astype(f32)


def head_split(matrix, valid_mask):
    images, slots = valid_mask.shape
    return matrix.reshape(images, slots, H, matrix.shape[1] // H)


def attn_forward(layer_input, attn_w, vecs, valid_mask):
    width = layer_input.shape[1]
    images, slots = valid_mask.shape
    rows = width // LEAD
    w_of = lambda c: attn_w[:, c * rows : (c + 1) * rows].reshape(width, width)
    normed = layer_norm(layer_input, vecs["gain_one"], vecs["shift_one"]).astype(bf16)
    queries = (product(normed, w_of(0)) + vecs["q_bias"]).astype(bf16)
    key_rows = product(normed, w_of(1)).astype(bf16)
    values = (product(normed, w_of(2)) + vecs["v_bias"]).astype(bf16)
    scale = (width // H) ** (-0.5)
    q4, k4, v4 = (head_split(a, valid_mask) for a in (queries, key_rows, values))
    scores = jnp.einsum("iqhd,ikhd->ihqk", q4, k4, preferred_element_type=f32) * scale
    scores = jnp.where(valid_mask[:, None, None, :], scores, -1e30)
    exponent = jnp.exp(scores - jnp.max(scores, axis=-1, keepdims=True))
    probs = (exponent / jnp.sum(exponent, axis=-1, keepdims=True)).astype(bf16)
    attended = jnp.einsum("ihqk,ikhd->iqhd", probs, v4, preferred_element_type=f32)
    attended = attended.reshape(images * slots, -1).astype(bf16)
    middle = layer_input + (product(attended, w_of(3)) + vecs["out_bias"])
    second = layer_norm(middle, vecs["gain_two"], vecs["shift_two"]).astype(bf16)
    return middle, second, (normed, queries, key_rows, values, probs, attended)


def mlp_forward(middle, second, up_w, down_w, vecs):
    width = middle.shape[1]
    rows = width // LEAD
    chunks = up_w.shape[1] // rows
    up = jnp.concatenate([up_w[:, c * rows : (c + 1) * rows].reshape(width, width) for c in range(chunks)], 1)
    hidden_pre = product(second, up) + vecs["up_bias"]
    activated = gelu_exact(hidden_pre).astype(bf16)
    result = middle + (product(activated, down_w.reshape(-1, width)) + vecs["down_bias"])
    return result.astype(bf16), activated, hidden_pre


def mlp_backward(upstream, middle, hidden_pre, up_w, down_w, vecs):
    width = middle.shape[1]
    rows = width // LEAD
    chunks = up_w.shape[1] // rows
    up = jnp.concatenate([up_w[:, c * rows : (c + 1) * rows].reshape(width, width) for c in range(chunks)], 1)
    grad_act = back_product(upstream, down_w.reshape(-1, width))
    grad_pre = jax.vjp(gelu_exact, hidden_pre)[1](grad_act)[0].astype(bf16)
    grad_second = back_product(grad_pre, up)
    grad_mid, grad_gain, grad_offset = jax.vjp(layer_norm, middle, vecs["gain_two"], vecs["shift_two"])[1](
        grad_second
    )
    sums = {
        "down_bias": jnp.sum(upstream.astype(f32), axis=0),
        "up_bias": jnp.sum(grad_pre.astype(f32), axis=0),
        "gain_two": grad_gain,
        "shift_two": grad_offset,
    }
    return upstream.astype(f32) + grad_mid, grad_pre, sums


def attn_backward(grad_middle, layer_input, saved, attn_w, vecs, valid_mask):
    normed, queries, key_rows, values, probs, attended = saved
    width = layer_input.shape[1]
    images, slots = valid_mask.shape
    rows = width // LEAD
    w_of = lambda c: attn_w[:, c * rows : (c + 1) * rows].reshape(width, width)
    scale = (width // H) ** (-0.5)
    grad_branch = grad_middle.astype(bf16)
    grad_attended = back_product(grad_branch, w_of(3)).astype(bf16)
    q4, k4, v4, g4 = (head_split(a, valid_mask) for a in (queries, key_rows, values, grad_attended))
    grad_probs = jnp.einsum("iqhd,ikhd->ihqk", g4, v4, preferred_element_type=f32)
    grad_value = jnp.einsum("ihqk,iqhd->ikhd", probs, g4, preferred_element_type=f32)
    soft = probs.astype(f32)
    terms = jnp.sum(soft * grad_probs, axis=-1, keepdims=True)
    grad_scores = (soft * (grad_probs - terms)).astype(bf16)
    grad_query = jnp.einsum("ihqk,ikhd->iqhd", grad_scores, k4, preferred_element_type=f32) * scale
    grad_key = jnp.einsum("ihqk,iqhd->ikhd", grad_scores, q4, preferred_element_type=f32) * scale
    parts = [a.reshape(images * slots, -1).astype(bf16) for a in (grad_query, grad_key, grad_value)]
    grad_normed = sum(back_product(part, w_of(c)) for c, part in enumerate(parts))
    grad_in, grad_gain, grad_offset = jax.vjp(layer_norm, layer_input, vecs["gain_one"], vecs["shift_one"])[1](
        grad_normed
    )
    sums = {
        "out_bias": jnp.sum(grad_branch.astype(f32), axis=0),
        "q_bias": jnp.sum(parts[0].astype(f32), axis=0),
        "v_bias": jnp.sum(parts[2].astype(f32), axis=0),
        "gain_one": grad_gain,
        "shift_one": grad_offset,
    }
    return grad_middle + grad_in, grad_branch, parts, sums


VECS = ("q_bias", "v_bias", "out_bias", "down_bias", "gain_one", "shift_one", "gain_two", "shift_two", "up_bias")


def by_columns(weight, width):
    rows, columns = weight.shape
    return jnp.concatenate([weight[:, at : at + width] for at in range(0, columns, width)], 0)


def solution(mesh):
    dp_size = mesh.shape["dp"]
    ringed = dp_size == 2 * RING

    def gather_weights(qkv, out, up, down, vectors):
        width = out.shape[1]
        if ringed:
            vec_row = jnp.concatenate([vectors[name] for name in VECS])
            vec_count = vec_row.shape[0]
            vec_block = jnp.zeros((VEC_ROWS, width), bf16).at[0, :vec_count].set(vec_row)
            first = assemble(ring_gather(jnp.concatenate([by_columns(qkv, width), out, vec_block], 0)))
            up_w = assemble(ring_gather(by_columns(up, width)))
            down_w = assemble(ring_gather(down))
            vec_rows = first[:, first.shape[1] - VEC_ROWS, :vec_count]
            vecs, at = {}, 0
            for name in VECS:
                size = vectors[name].shape[0]
                vecs[name] = vec_rows[:, at : at + size].reshape(1, -1).astype(f32)
                at += size
            return first, up_w, down_w, vecs
        gathered = [lax.all_gather(w, "dp", axis=0, tiled=True) for w in (qkv, out, up, down)]
        blocked = [w.reshape(LEAD, -1, w.shape[1]) for w in gathered]
        fold = lambda w: w.reshape(LEAD, w.shape[1], -1, width).transpose(0, 2, 1, 3).reshape(LEAD, -1, width)
        first = jnp.concatenate([fold(blocked[0]), blocked[1], jnp.zeros((LEAD, VEC_ROWS, width), bf16)], 1)
        vecs = {
            name: lax.all_gather(vectors[name], "dp", axis=0, tiled=True).reshape(1, -1).astype(f32)
            for name in VECS
        }
        return first, fold(blocked[2]), blocked[3], vecs

    def scatter_gradients(grad_down, grad_up, grad_first, sums):
        width = grad_down.shape[2]
        rows = width // LEAD
        if ringed:
            row = jnp.concatenate([sums[name].reshape(LEAD, -1) for name in VECS], 1).astype(bf16)
            vec_count = row.shape[1]
            vec_block = jnp.zeros((LEAD, VEC_ROWS, width), bf16).at[:, 0, :vec_count].set(row)
            down = ring_scatter(*dispatch(grad_down))
            up = ring_scatter(*dispatch(grad_up))
            first = ring_scatter(*dispatch(jnp.concatenate([grad_first, vec_block], 1)))
            vec_row, at, vecs = first[4 * rows], 0, {}
            for name in VECS:
                size = sums[name].size // dp_size
                vecs[name] = vec_row[at : at + size]
                at += size
            unfold = lambda block: jnp.concatenate(
                [block[at : at + rows] for at in range(0, block.shape[0], rows)], 1
            )
            return unfold(first[: 3 * rows]), first[3 * rows : 4 * rows], unfold(up), down, vecs
        scatter = lambda a: lax.psum_scatter(a, "dp", scatter_dimension=0, tiled=True)
        unfold = lambda w: w.reshape(LEAD, -1, rows, width).transpose(0, 2, 1, 3).reshape(LEAD * rows, -1)
        vecs = {name: scatter(sums[name].reshape(-1)) for name in VECS}
        return (
            scatter(unfold(grad_first[:, : 3 * rows]).astype(f32)),
            scatter(grad_first[:, 3 * rows :].reshape(width, width).astype(f32)),
            scatter(unfold(grad_up).astype(f32)),
            scatter(grad_down.reshape(-1, width).astype(f32)),
            vecs,
        )

    def shards(
        tokens, cotangent, heights, widths, qkv_weight, out_weight, up_weight, down_weight,
        q_bias, v_bias, out_bias, up_bias, down_bias, gain_one, shift_one, gain_two, shift_two,
    ):
        leading = lax.axis_index("section") == 0
        vectors = dict(
            q_bias=q_bias[0], v_bias=v_bias[0], out_bias=out_bias[0], up_bias=up_bias[0], down_bias=down_bias[0],
            gain_one=gain_one[0], shift_one=shift_one[0], gain_two=gain_two[0], shift_two=shift_two[0],
        )
        attn_w, up_w, down_w, vecs = gather_weights(
            qkv_weight[0], out_weight[0], up_weight[0], down_weight[0], vectors
        )
        position = jnp.arange(GRID * GRID, dtype=jnp.int32)
        valid = ((position // GRID)[None, :] < heights[:, None]) & (
            (position % GRID)[None, :] < widths[:, None]
        )

        middle, second, _ = attn_forward(tokens.astype(f32), attn_w, vecs, valid)
        sent, _, _ = mlp_forward(middle, second, up_w, down_w, vecs)
        received = lax.ppermute(sent, "section", [(0, 1)])
        layer_input = jnp.where(leading, tokens, received).astype(f32)
        middle, second, saved = attn_forward(layer_input, attn_w, vecs, valid)
        result, activated, hidden_pre = mlp_forward(middle, second, up_w, down_w, vecs)

        grad_middle, _, _ = mlp_backward(cotangent, middle, hidden_pre, up_w, down_w, vecs)
        grad_input, _, _, _ = attn_backward(grad_middle, layer_input, saved, attn_w, vecs, valid)
        arriving = lax.ppermute(grad_input.astype(bf16), "section", [(1, 0)])
        upstream = jnp.where(leading, arriving, cotangent)
        grad_down = outer_sum(activated, upstream).astype(bf16)
        grad_middle, grad_pre, sums = mlp_backward(upstream, middle, hidden_pre, up_w, down_w, vecs)
        grad_up = outer_sum(second, grad_pre).astype(bf16)
        grad_input, grad_branch, parts, more = attn_backward(
            grad_middle, layer_input, saved, attn_w, vecs, valid
        )
        normed, attended = saved[0], saved[5]
        first = [outer_sum(normed, part) for part in parts] + [outer_sum(attended, grad_branch)]
        width = tokens.shape[1]
        grad_first = jnp.concatenate([g.reshape(LEAD, -1, width) for g in first], 1).astype(bf16)
        chunks = grad_up.shape[1] // width
        grad_up = jnp.concatenate(
            [grad_up[:, c * width : (c + 1) * width].reshape(LEAD, -1, width) for c in range(chunks)], 1
        )
        g_qkv, g_out, g_up, g_down, g_vecs = scatter_gradients(
            grad_down.reshape(LEAD, -1, width), grad_up, grad_first, {**sums, **more}
        )
        return (
            result[None], grad_input[None], g_qkv[None], g_out[None], g_up[None], g_down[None],
            *(
                g_vecs[name][None]
                for name in (
                    "q_bias", "v_bias", "out_bias", "up_bias", "down_bias",
                    "gain_one", "shift_one", "gain_two", "shift_two",
                )
            ),
        )

    rows = P("dp", None)
    three, two = P("section", "dp", None), P("section", "dp")
    return jax.shard_map(
        shards,
        mesh=mesh,
        in_specs=(rows, rows, P("dp"), P("dp")) + (three,) * 4 + (two,) * 9,
        out_specs=(three,) * 6 + (two,) * 9,
        check_vma=False,
    )
```

```python
import jax
import jax.numpy as jnp
from jax import lax
from jax.experimental import pallas as pl
from jax.experimental.pallas import tpu as pltpu
from jax.sharding import PartitionSpec as P

H = 16
GRID = 16
LEAD = 16
RING = 8
VEC_ROWS = 16

f32 = jnp.float32
bf16 = jnp.bfloat16
eps_norm = 1e-05


def chip_at(place):
    if isinstance(place, int):
        return 2 * place if place < 4 else 2 * (7 - place) + 1
    return jnp.where(place < 4, 2 * place, 2 * (7 - place) + 1)


def place_of(chip):
    if isinstance(chip, int):
        return chip // 2 if chip % 2 == 0 else 7 - chip // 2
    return jnp.where(chip % 2 == 0, chip // 2, 7 - chip // 2)


def ring_route(step):
    return [
        (2 * chip_at(place) + core, 2 * chip_at((place + step) % RING) + core)
        for place in range(RING)
        for core in range(2)
    ]


CORE_ROUTE = [(index, index ^ 1) for index in range(2 * RING)]


def onward(block):
    return lax.ppermute(block, "dp", ring_route(1))


def backward(block):
    return lax.ppermute(block, "dp", ring_route(-1))


def across(block):
    return lax.ppermute(block, "dp", CORE_ROUTE)


def ring_gather(shard):
    half = shard.shape[0] // 2
    here = {0: shard}
    up, down = shard, shard
    for step in range(1, RING // 2):
        up, down = onward(up), backward(down)
        here[RING - step], here[step] = up, down
    far = (onward(up[:half]), backward(down[half:]))
    blocks = []
    for place in range(RING):
        if place == RING // 2:
            blocks += [far[0], far[1], across(far[0]), across(far[1])]
        else:
            blocks += [here[place], across(here[place])]
    return blocks


def assemble(blocks):
    rows, width = blocks[0].shape
    half = rows // 2
    count = len(blocks)

    def kernel(*refs):
        blocks_in, out, sems = refs[:count], refs[count], refs[count + 1]
        me = lax.axis_index("dp")
        core, place = lax.rem(me, 2), place_of(lax.div(me, 2))
        copies = []
        at = 0
        for step in range(RING):
            chip = chip_at(lax.rem(place + step, RING))
            parts = ((0, half), (half, half)) if step == RING // 2 else ((0, rows),)
            for owner in (2 * chip + core, 2 * chip + 1 - core):
                for start, size in parts:
                    copies.append(
                        pltpu.make_async_copy(
                            blocks_in[at], out.at[owner, pl.ds(start, size)], sems.at[at]
                        )
                    )
                    at += 1
        for copy in copies:
            copy.start()
        for copy in copies:
            copy.wait()

    return pl.pallas_call(
        kernel,
        out_shape=jax.ShapeDtypeStruct((2 * RING, rows, width), blocks[0].dtype),
        in_specs=[pl.BlockSpec(memory_space=pl.ANY)] * count,
        out_specs=pl.BlockSpec(memory_space=pltpu.VMEM),
        scratch_shapes=[pltpu.SemaphoreType.DMA((count,))],
        compiler_params=pltpu.CompilerParams(vmem_limit_bytes=16 * 2**20),
        name="assemble",
    )(*blocks)


def ring_scatter(own, peer):
    rows = own.shape[1]
    half = rows // 2
    arrived = across(peer)

    def local(step, start=0, size=rows):
        return own[step, start : start + size].astype(f32) + arrived[step, start : start + size].astype(f32)

    far = RING // 2
    up = onward(local(far, 0, half).astype(bf16))
    down = backward(local(far, half, half).astype(bf16))
    joint_up = jnp.concatenate([local(far - 1, 0, half) + up.astype(f32), local(far - 1, half, half)], 0)
    joint_down = jnp.concatenate([local(far + 1, 0, half), local(far + 1, half, half) + down.astype(f32)], 0)
    up, down = onward(joint_up.astype(bf16)), backward(joint_down.astype(bf16))
    for step in range(far - 2, 0, -1):
        up = onward((local(step) + up.astype(f32)).astype(bf16))
        down = backward((local(RING - step) + down.astype(f32)).astype(bf16))
    return local(0) + up.astype(f32) + down.astype(f32)


VMEM_LIMIT = 48 * 2**20
MLP_CHUNK = 32
Q_BIAS, V_BIAS, OUT_BIAS, DOWN_BIAS, GAIN_ONE, SHIFT_ONE, GAIN_TWO, SHIFT_TWO, UP_BIAS = range(9)
NT = (((1,), (1,)), ((), ()))
TN = (((0,), (0,)), ((), ()))


def dot(first_mat, second_mat):
    return jnp.dot(first_mat, second_mat, preferred_element_type=f32)


def dot_nt(first_mat, second_mat):
    return lax.dot_general(first_mat, second_mat, NT, preferred_element_type=f32)


def dot_tn(first_mat, second_mat):
    return lax.dot_general(first_mat, second_mat, TN, preferred_element_type=f32)


def weight_part(w_ref, part):
    width = w_ref.shape[2]
    rows = width // LEAD
    return w_ref[:, part * rows : (part + 1) * rows, :].reshape(width, width)


def norm_parts(rows_in):
    average = jnp.mean(rows_in, axis=-1, keepdims=True)
    centred = rows_in - average
    inverse = lax.rsqrt(jnp.mean(centred * centred, axis=-1, keepdims=True) + eps_norm)
    return centred * inverse, inverse


def norm_back(rows_in, gain_row, grad_rows):
    unit, inverse = norm_parts(rows_in)
    scaled = grad_rows * gain_row
    mean_one = jnp.mean(scaled, axis=-1, keepdims=True)
    mean_two = jnp.mean(scaled * unit, axis=-1, keepdims=True)
    return (scaled - mean_one - unit * mean_two) * inverse, grad_rows * unit


def head_window(head, head_size, width):
    start = min(head * head_size // 128 * 128, width - 256)
    return start, head * head_size - start


def only_head(block, low, head_size):
    lane = lax.broadcasted_iota(jnp.int32, block.shape, 1)
    return jnp.where((lane >= low) & (lane < low + head_size), block, jnp.zeros_like(block))


def column_sum(rows_in):
    return jnp.sum(rows_in, axis=0, keepdims=True)


def attn_forward_kernel(
    heights_ref, widths_ref, x_ref, w_ref, vec_ref,
    middle_ref, second_ref, normed_ref, q_ref, k_ref, v_ref, probs_ref, attended_ref,
    vt_ref, at_ref,
):
    slots, width = x_ref.shape
    head_size = width // H
    step = 64
    for at in range(0, slots, step):
        unit, _ = norm_parts(x_ref[at : at + step, :].astype(f32))
        normed_ref[at : at + step, :] = (
            unit * vec_ref[GAIN_ONE : GAIN_ONE + 1, :] + vec_ref[SHIFT_ONE : SHIFT_ONE + 1, :]
        ).astype(bf16)
    normed = normed_ref[...]
    q_ref[...] = (dot(normed, weight_part(w_ref, 0)) + vec_ref[Q_BIAS : Q_BIAS + 1, :]).astype(bf16)
    k_ref[...] = dot(normed, weight_part(w_ref, 1)).astype(bf16)
    values = dot(normed, weight_part(w_ref, 2)) + vec_ref[V_BIAS : V_BIAS + 1, :]
    v_ref[...] = values.astype(bf16)
    vt_ref[...] = values.astype(bf16).T
    image = pl.program_id(0)
    slot = lax.broadcasted_iota(jnp.int32, (slots, 128), 0)
    valid = (slot // GRID < heights_ref[image]) & (slot % GRID < widths_ref[image])
    mask = jnp.where(valid, 0.0, -1e30).astype(f32)
    scale = head_size ** (-0.5)
    for head in range(H):
        start, low = head_window(head, head_size, width)
        queries = only_head(q_ref[:, start : start + 256], low, head_size)
        scores = dot_nt(k_ref[:, start : start + 256], queries)
        for at in range(0, slots, 128):
            part = scores[:, at : at + 128] * scale + mask
            exponent = jnp.exp(part - jnp.max(part, axis=0, keepdims=True))
            inverse = 1.0 / jnp.sum(exponent, axis=0, keepdims=True)
            probs_ref[head, :, at : at + 128] = (exponent * inverse).astype(bf16)
        here = slice(head * head_size, (head + 1) * head_size)
        at_ref[here, :] = dot(vt_ref[here, :], probs_ref[head])
    attended_ref[...] = at_ref[...].T.astype(bf16)
    branch = dot(attended_ref[...], weight_part(w_ref, 3))
    middle_ref[...] = x_ref[...].astype(f32) + (branch + vec_ref[OUT_BIAS : OUT_BIAS + 1, :])
    for at in range(0, slots, step):
        unit, _ = norm_parts(middle_ref[at : at + step, :])
        second_ref[at : at + step, :] = (
            unit * vec_ref[GAIN_TWO : GAIN_TWO + 1, :] + vec_ref[SHIFT_TWO : SHIFT_TWO + 1, :]
        ).astype(bf16)


def attn_forward(layer_input, attn_w, vecs, heights, widths):
    count, width = layer_input.shape
    images = heights.shape[0]
    slots = count // images
    rows = pl.BlockSpec((slots, width), lambda i, *_: (i, 0))
    wide = jax.ShapeDtypeStruct((count, width), f32)
    low = jax.ShapeDtypeStruct((count, width), bf16)
    flops = 8 * count * width * width + 4 * count * slots * width
    return pl.pallas_call(
        attn_forward_kernel,
        grid_spec=pltpu.PrefetchScalarGridSpec(
            num_scalar_prefetch=2,
            grid=(images,),
            in_specs=[
                rows,
                pl.BlockSpec(attn_w.shape, lambda i, *_: (0, 0, 0), pipeline_mode=pl.Buffered(1)),
                pl.BlockSpec(vecs.shape, lambda i, *_: (0, 0)),
            ],
            out_specs=[rows] * 6
            + [pl.BlockSpec((None, H, slots, slots), lambda i, *_: (i, 0, 0, 0)), rows],
            scratch_shapes=[pltpu.VMEM((width, slots), bf16), pltpu.VMEM((width, slots), f32)],
        ),
        out_shape=[wide, low, low, low, low, low, jax.ShapeDtypeStruct((images, H, slots, slots), bf16), low],
        compiler_params=pltpu.CompilerParams(vmem_limit_bytes=VMEM_LIMIT),
        cost_estimate=pl.CostEstimate(
            flops=flops, bytes_accessed=attn_w.size * 2 + count * width * 20, transcendentals=count * slots * H
        ),
        name="attn_forward",
    )(heights, widths, layer_input, attn_w, vecs)


def mlp_forward_kernel(
    middle_ref, second_ref, up_ref, down_ref, vec_ref, result_ref, act_ref, slope_ref, pre_ref, acc_ref
):
    index = pl.program_id(0)
    count, width = second_ref.shape
    pre_ref[...] = dot(second_ref[...], up_ref[...].reshape(width, width))
    bias = vec_ref[pl.ds(UP_BIAS + index, 1), :]

    def gelu_rows(at, _):
        here = pl.ds(at * MLP_CHUNK, MLP_CHUNK)
        pre = pre_ref[here, :] + bias
        below = 0.5 * (1.0 + lax.erf(pre * (0.5**0.5)))
        act_ref[here, :] = (pre * below).astype(bf16)
        bell = jnp.exp(-0.5 * pre * pre) * (0.5 / jnp.pi) ** 0.5
        slope_ref[here, :] = (below + pre * bell).astype(bf16)
        return 0

    lax.fori_loop(0, count // MLP_CHUNK, gelu_rows, 0)
    added = dot(act_ref[...], down_ref[...].reshape(width, width))

    @pl.when(index == 0)
    def _():
        acc_ref[...] = added

    @pl.when(index > 0)
    def _():
        acc_ref[...] += added

    @pl.when(index == pl.num_programs(0) - 1)
    def _():
        result_ref[...] = (
            middle_ref[...] + (acc_ref[...] + vec_ref[DOWN_BIAS : DOWN_BIAS + 1, :])
        ).astype(bf16)


def mlp_forward(middle, second, up_w, down_w, vecs):
    count, width = middle.shape
    parts = up_w.shape[1] * LEAD // width
    whole = pl.BlockSpec((count, width), lambda j: (0, 0))
    chunk = pl.BlockSpec((count, width), lambda j: (0, j))
    low = jax.ShapeDtypeStruct((count, width), bf16)
    hidden = jax.ShapeDtypeStruct((count, width * parts), bf16)
    return pl.pallas_call(
        mlp_forward_kernel,
        grid=(parts,),
        in_specs=[
            whole,
            whole,
            pl.BlockSpec((LEAD, width // LEAD, width), lambda j: (0, j, 0)),
            pl.BlockSpec((LEAD // parts, down_w.shape[1], width), lambda j: (j, 0, 0)),
            pl.BlockSpec(vecs.shape, lambda j: (0, 0)),
        ],
        out_specs=[whole, chunk, chunk],
        out_shape=[low, hidden, hidden],
        scratch_shapes=[pltpu.VMEM((count, width), f32)] * 2,
        compiler_params=pltpu.CompilerParams(vmem_limit_bytes=VMEM_LIMIT),
        cost_estimate=pl.CostEstimate(
            flops=4 * count * width * width * parts,
            bytes_accessed=up_w.size * 4 + count * width * (8 + 4 * parts),
            transcendentals=2 * count * width * parts,
        ),
        name="mlp_forward",
    )(middle, second, up_w, down_w, vecs)


def mlp_backward_kernel(
    upstream_ref, slope_ref, middle_ref, up_ref, down_ref, vec_ref,
    grad_middle_ref, grad_pre_ref, sums_ref, up_sum_ref, ga_ref, acc_ref,
):
    index = pl.program_id(0)
    count, width = upstream_ref.shape
    ga_ref[...] = dot_nt(upstream_ref[...], down_ref[...].reshape(width, width))
    sums = jnp.zeros((1, width), f32)
    for at in range(0, count, MLP_CHUNK):
        here = slice(at, at + MLP_CHUNK)
        pre = (ga_ref[here, :] * slope_ref[here, :].astype(f32)).astype(bf16)
        grad_pre_ref[here, :] = pre
        sums += column_sum(pre.astype(f32))
    up_sum_ref[0] = sums
    added = dot_nt(grad_pre_ref[...], up_ref[...].reshape(width, width))

    @pl.when(index == 0)
    def _():
        acc_ref[...] = added

    @pl.when(index > 0)
    def _():
        acc_ref[...] += added

    @pl.when(index == pl.num_programs(0) - 1)
    def _():
        gain = vec_ref[GAIN_TWO : GAIN_TWO + 1, :]
        down_sum = jnp.zeros((1, width), f32)
        gain_sum = jnp.zeros((1, width), f32)
        shift_sum = jnp.zeros((1, width), f32)
        for at in range(0, count, MLP_CHUNK):
            here = slice(at, at + MLP_CHUNK)
            upstream = upstream_ref[here, :].astype(f32)
            grad = acc_ref[here, :]
            grad_mid, gain_terms = norm_back(middle_ref[here, :], gain, grad)
            grad_middle_ref[here, :] = upstream + grad_mid
            down_sum += column_sum(upstream)
            gain_sum += column_sum(gain_terms)
            shift_sum += column_sum(grad)
        sums_ref[0:1, :] = down_sum
        sums_ref[1:2, :] = gain_sum
        sums_ref[2:3, :] = shift_sum


def mlp_backward(upstream, slope, middle, up_w, down_w, vecs):
    count, width = middle.shape
    parts = up_w.shape[1] * LEAD // width
    whole = pl.BlockSpec((count, width), lambda j: (0, 0))
    chunk = pl.BlockSpec((count, width), lambda j: (0, j))
    return pl.pallas_call(
        mlp_backward_kernel,
        grid=(parts,),
        in_specs=[
            whole,
            chunk,
            whole,
            pl.BlockSpec((LEAD, width // LEAD, width), lambda j: (0, j, 0)),
            pl.BlockSpec((LEAD // parts, down_w.shape[1], width), lambda j: (j, 0, 0)),
            pl.BlockSpec(vecs.shape, lambda j: (0, 0)),
        ],
        out_specs=[
            whole,
            chunk,
            pl.BlockSpec((8, width), lambda j: (0, 0)),
            pl.BlockSpec((1, 1, width), lambda j: (j, 0, 0)),
        ],
        out_shape=[
            jax.ShapeDtypeStruct((count, width), f32),
            jax.ShapeDtypeStruct((count, width * parts), bf16),
            jax.ShapeDtypeStruct((8, width), f32),
            jax.ShapeDtypeStruct((parts, 1, width), f32),
        ],
        scratch_shapes=[pltpu.VMEM((count, width), f32)] * 2,
        compiler_params=pltpu.CompilerParams(vmem_limit_bytes=VMEM_LIMIT),
        cost_estimate=pl.CostEstimate(
            flops=4 * count * width * width * parts,
            bytes_accessed=up_w.size * 4 + count * width * (10 + 4 * parts),
            transcendentals=0,
        ),
        name="mlp_backward",
    )(upstream, slope, middle, up_w, down_w, vecs)


def attn_backward_kernel(
    grad_middle_ref, x_ref, q_ref, k_ref, v_ref, probs_ref, w_ref, vec_ref,
    grad_in_ref, grad_low_ref, branch_ref, gq_ref, gk_ref, gv_ref, sums_ref,
    ga_ref, gat_ref, qt_ref, kt_ref, gqt_ref, gkt_ref, gvt_ref,
):
    slots, width = x_ref.shape
    head_size = width // H
    scale = head_size ** (-0.5)
    branch_ref[...] = grad_middle_ref[...].astype(bf16)
    ga = dot_nt(branch_ref[...], weight_part(w_ref, 3)).astype(bf16)
    ga_ref[...] = ga
    gat_ref[...] = ga.T
    qt_ref[...] = q_ref[...].T
    kt_ref[...] = k_ref[...].T
    for head in range(H):
        start, low = head_window(head, head_size, width)
        here = slice(head * head_size, (head + 1) * head_size)
        own = only_head(ga_ref[:, start : start + 256], low, head_size)
        grad_probs = dot_nt(v_ref[:, start : start + 256], own)
        pieces = []
        for at in range(0, slots, 128):
            probs = probs_ref[head, :, at : at + 128].astype(f32)
            grad = grad_probs[:, at : at + 128]
            total = jnp.sum(probs * grad, axis=0, keepdims=True)
            pieces.append((probs * (grad - total)).astype(bf16))
        grad_scores = jnp.concatenate(pieces, axis=1)
        gvt_ref[here, :] = dot_nt(gat_ref[here, :], probs_ref[head])
        gqt_ref[here, :] = dot(kt_ref[here, :], grad_scores) * scale
        gkt_ref[here, :] = dot_nt(qt_ref[here, :], grad_scores) * scale
    gq_ref[...] = gqt_ref[...].T.astype(bf16)
    gk_ref[...] = gkt_ref[...].T.astype(bf16)
    gv_ref[...] = gvt_ref[...].T.astype(bf16)
    grad_normed = dot_nt(gq_ref[...], weight_part(w_ref, 0))
    grad_normed += dot_nt(gk_ref[...], weight_part(w_ref, 1))
    grad_normed += dot_nt(gv_ref[...], weight_part(w_ref, 2))
    grad_in_ref[...] = grad_normed
    gain = vec_ref[GAIN_ONE : GAIN_ONE + 1, :]
    sums = [jnp.zeros((1, width), f32)] * 5
    for at in range(0, slots, MLP_CHUNK):
        rows = slice(at, at + MLP_CHUNK)
        grad = grad_in_ref[rows, :]
        grad_norm, gain_terms = norm_back(x_ref[rows, :].astype(f32), gain, grad)
        total = grad_middle_ref[rows, :] + grad_norm
        grad_in_ref[rows, :] = total
        grad_low_ref[rows, :] = total.astype(bf16)
        terms = (
            gq_ref[rows, :].astype(f32), gv_ref[rows, :].astype(f32), branch_ref[rows, :].astype(f32),
            gain_terms, grad,
        )
        sums = [old + column_sum(new) for old, new in zip(sums, terms)]

    first = pl.program_id(0) == 0
    for row, value in enumerate(sums):
        sums_ref[row : row + 1, :] = value + jnp.where(first, 0.0, sums_ref[row : row + 1, :])


def attn_backward(grad_middle, layer_input, saved, attn_w, vecs, images):
    queries, key_rows, values, probs = saved
    count, width = layer_input.shape
    slots = count // images
    rows = pl.BlockSpec((slots, width), lambda i: (i, 0))
    low = jax.ShapeDtypeStruct((count, width), bf16)
    flipped = pltpu.VMEM((width, slots), bf16)
    flipped_wide = pltpu.VMEM((width, slots), f32)
    return pl.pallas_call(
        attn_backward_kernel,
        grid=(images,),
        in_specs=[rows] * 5
        + [
            pl.BlockSpec((None, H, slots, slots), lambda i: (i, 0, 0, 0)),
            pl.BlockSpec(attn_w.shape, lambda i: (0, 0, 0), pipeline_mode=pl.Buffered(1)),
            pl.BlockSpec(vecs.shape, lambda i: (0, 0)),
        ],
        out_specs=[rows] * 6 + [pl.BlockSpec((8, width), lambda i: (0, 0))],
        out_shape=[jax.ShapeDtypeStruct((count, width), f32)] + [low] * 5 + [jax.ShapeDtypeStruct((8, width), f32)],
        scratch_shapes=[pltpu.VMEM((slots, width), bf16)] + [flipped] * 3 + [flipped_wide] * 3,
        compiler_params=pltpu.CompilerParams(vmem_limit_bytes=VMEM_LIMIT),
        cost_estimate=pl.CostEstimate(
            flops=8 * count * width * width + 8 * count * slots * width,
            bytes_accessed=attn_w.size * 2 + count * width * 30,
            transcendentals=0,
        ),
        name="attn_backward",
    )(grad_middle, layer_input, queries, key_rows, values, probs, attn_w, vecs)


def ring_slot(owner, me):
    there, here = place_of(lax.div(owner, 2)), place_of(lax.div(me, 2))
    return lax.rem(there - here + RING, RING)


def store_block(own_ref, peer_ref, owner, core, rows, value):
    me = lax.axis_index("dp")
    slot = ring_slot(owner, me)

    @pl.when(lax.rem(me, 2) == core)
    def _():
        own_ref[slot, rows, :] = value

    @pl.when(lax.rem(me, 2) != core)
    def _():
        peer_ref[slot, rows, :] = value


def scatter_shapes(rows, width):
    return [jax.ShapeDtypeStruct((RING, rows, width), bf16)] * 2


def grad_down_kernel(act_ref, upstream_ref, own_ref, peer_ref):
    index = pl.program_id(0)
    rows = own_ref.shape[1]
    value = dot_tn(act_ref[...], upstream_ref[...]).astype(bf16)
    for at in range(value.shape[0] // rows):
        owner = index * (value.shape[0] // rows) + at
        store_block(own_ref, peer_ref, owner, at % 2, slice(None), value[at * rows : (at + 1) * rows])


def grad_down_blocks(activated, upstream):
    count, width = upstream.shape
    hidden = activated.shape[1]
    parts = hidden // width
    rows = hidden // LEAD
    return pl.pallas_call(
        grad_down_kernel,
        grid=(parts,),
        in_specs=[
            pl.BlockSpec((count, width), lambda j: (0, j)),
            pl.BlockSpec((count, width), lambda j: (0, 0)),
        ],
        out_specs=[pl.BlockSpec((RING, rows, width), lambda j: (0, 0, 0))] * 2,
        out_shape=scatter_shapes(rows, width),
        compiler_params=pltpu.CompilerParams(vmem_limit_bytes=VMEM_LIMIT),
        cost_estimate=pl.CostEstimate(
            flops=2 * count * width * hidden, bytes_accessed=count * hidden * 2 + hidden * width * 2, transcendentals=0
        ),
        name="grad_down",
    )(activated, upstream)


def grad_up_kernel(second_ref, pre_ref, own_ref, peer_ref, flip_ref):
    index = pl.program_id(0)
    width = second_ref.shape[1]
    rows = width // LEAD

    @pl.when(index == 0)
    def _():
        flip_ref[...] = second_ref[...].T

    value = dot(flip_ref[...], pre_ref[...]).astype(bf16)
    for owner in range(LEAD):
        here = pl.ds(pl.multiple_of(index * rows, rows), rows)
        store_block(own_ref, peer_ref, owner, owner % 2, here, value[owner * rows : (owner + 1) * rows])


def grad_up_blocks(second, grad_pre):
    count, width = second.shape
    hidden = grad_pre.shape[1]
    parts = hidden // width
    rows = hidden // LEAD
    return pl.pallas_call(
        grad_up_kernel,
        grid=(parts,),
        in_specs=[
            pl.BlockSpec((count, width), lambda j: (0, 0)),
            pl.BlockSpec((count, width), lambda j: (0, j)),
        ],
        out_specs=[pl.BlockSpec((RING, rows, width), lambda j: (0, 0, 0))] * 2,
        out_shape=scatter_shapes(rows, width),
        scratch_shapes=[pltpu.VMEM((width, count), bf16)],
        compiler_params=pltpu.CompilerParams(vmem_limit_bytes=VMEM_LIMIT),
        cost_estimate=pl.CostEstimate(
            flops=2 * count * width * hidden, bytes_accessed=count * hidden * 2 + hidden * width * 2, transcendentals=0
        ),
        name="grad_up",
    )(second, grad_pre)


def grad_first_kernel(
    normed_ref, attended_ref, gq_ref, gk_ref, gv_ref, branch_ref, vec_ref, own_ref, peer_ref, flip_ref
):
    width = normed_ref.shape[1]
    rows = width // LEAD
    flip_ref[...] = normed_ref[...].T
    for part, right in enumerate((gq_ref, gk_ref, gv_ref, branch_ref)):
        if part == 3:
            flip_ref[...] = attended_ref[...].T
        value = dot(flip_ref[...], right[...]).astype(bf16)
        for owner in range(LEAD):
            here = slice(part * rows, (part + 1) * rows)
            store_block(own_ref, peer_ref, owner, owner % 2, here, value[owner * rows : (owner + 1) * rows])
    for owner in range(LEAD):
        here = slice(4 * rows, 4 * rows + VEC_ROWS)
        store_block(own_ref, peer_ref, owner, owner % 2, here, vec_ref[owner])


def grad_first_blocks(normed, attended, gq, gk, gv, branch, vec_block):
    count, width = normed.shape
    rows = 4 * width // LEAD + VEC_ROWS
    return pl.pallas_call(
        grad_first_kernel,
        in_specs=[pl.BlockSpec(memory_space=pltpu.VMEM)] * 7,
        out_specs=[pl.BlockSpec(memory_space=pltpu.VMEM)] * 2,
        out_shape=scatter_shapes(rows, width),
        scratch_shapes=[pltpu.VMEM((width, count), bf16)],
        compiler_params=pltpu.CompilerParams(vmem_limit_bytes=VMEM_LIMIT),
        cost_estimate=pl.CostEstimate(
            flops=8 * count * width * width, bytes_accessed=count * width * 12 + 8 * width * width, transcendentals=0
        ),
        name="grad_first",
    )(normed, attended, gq, gk, gv, branch, vec_block)


VECS = ("q_bias", "v_bias", "out_bias", "down_bias", "gain_one", "shift_one", "gain_two", "shift_two")


def by_columns(weight, width):
    columns = weight.shape[1]
    return jnp.concatenate([weight[:, at : at + width] for at in range(0, columns, width)], 0)


def back_by_columns(block, rows):
    return jnp.concatenate([block[at : at + rows] for at in range(0, block.shape[0], rows)], 1)


def solution(mesh):
    dp_size = mesh.shape["dp"]
    ringed = dp_size == 2 * RING

    def gather_weights(qkv, out, up, down, vectors):
        width = out.shape[1]
        if ringed:
            rows = out.shape[0]
            vec_rows = jnp.concatenate([jnp.stack([vectors[name] for name in VECS]), vectors["up_bias"].reshape(-1, rows)])
            vec_block = jnp.pad(vec_rows, ((0, VEC_ROWS - vec_rows.shape[0]), (0, width - rows)))
            first = assemble(ring_gather(jnp.concatenate([by_columns(qkv, width), out, vec_block], 0)))
            up_w = assemble(ring_gather(by_columns(up, width)))
            down_w = assemble(ring_gather(down))
            vec_all = first[:, first.shape[1] - VEC_ROWS :, :rows]
            count = len(VECS)
            vecs = vec_all[:, :count].transpose(1, 0, 2).reshape(count, width)
            ups = vec_all[:, count : vec_rows.shape[0]].reshape(-1, width)
        else:
            gathered = [lax.all_gather(w, "dp", axis=0, tiled=True) for w in (qkv, out, up, down)]
            blocked = [w.reshape(LEAD, -1, w.shape[1]) for w in gathered]
            fold = lambda w: w.reshape(LEAD, w.shape[1], -1, width).transpose(0, 2, 1, 3).reshape(LEAD, -1, width)
            first = jnp.concatenate([fold(blocked[0]), blocked[1], jnp.zeros((LEAD, VEC_ROWS, width), bf16)], 1)
            up_w, down_w = fold(blocked[2]), blocked[3]
            whole = lambda name: lax.all_gather(vectors[name], "dp", axis=0, tiled=True)
            vecs = jnp.stack([whole(name) for name in VECS])
            ups = whole("up_bias").reshape(-1, width)
        vecs = jnp.concatenate([vecs, ups], 0).astype(f32)
        return first, up_w, down_w, jnp.pad(vecs, ((0, VEC_ROWS - vecs.shape[0]), (0, 0)))

    def shards(
        tokens, cotangent, heights, widths, qkv_weight, out_weight, up_weight, down_weight,
        q_bias, v_bias, out_bias, up_bias, down_bias, gain_one, shift_one, gain_two, shift_two,
    ):
        leading = lax.axis_index("section") == 0
        width = tokens.shape[1]
        images = heights.shape[0]
        rows = width // LEAD
        vectors = dict(
            q_bias=q_bias[0], v_bias=v_bias[0], out_bias=out_bias[0], up_bias=up_bias[0], down_bias=down_bias[0],
            gain_one=gain_one[0], shift_one=shift_one[0], gain_two=gain_two[0], shift_two=shift_two[0],
        )
        attn_w, up_w, down_w, vecs = gather_weights(
            qkv_weight[0], out_weight[0], up_weight[0], down_weight[0], vectors
        )

        middle, second = attn_forward(tokens, attn_w, vecs, heights, widths)[:2]
        sent = mlp_forward(middle, second, up_w, down_w, vecs)[0]
        received = lax.ppermute(sent, "section", [(0, 1)])
        layer_input = jnp.where(leading, tokens, received)
        middle, second, normed, queries, key_rows, values, probs, attended = attn_forward(
            layer_input, attn_w, vecs, heights, widths
        )
        result, activated, slope = mlp_forward(middle, second, up_w, down_w, vecs)

        saved = (queries, key_rows, values, probs)
        grad_middle = mlp_backward(cotangent, slope, middle, up_w, down_w, vecs)[0]
        to_send = attn_backward(grad_middle, layer_input, saved, attn_w, vecs, images)[1]
        arriving = lax.ppermute(to_send, "section", [(1, 0)])
        upstream = jnp.where(leading, arriving, cotangent)
        if ringed:
            g_down = ring_scatter(*grad_down_blocks(activated, upstream))
        grad_middle, grad_pre, mlp_sums, up_sums = mlp_backward(upstream, slope, middle, up_w, down_w, vecs)
        if ringed:
            g_up = back_by_columns(ring_scatter(*grad_up_blocks(second, grad_pre)), rows)
        grad_input, _, branch, gq, gk, gv, attn_sums = attn_backward(
            grad_middle, layer_input, saved, attn_w, vecs, images
        )
        sums = jnp.concatenate([attn_sums[:3], mlp_sums[:1], attn_sums[3:5], mlp_sums[1:3]], 0)
        count = len(VECS)
        if ringed:
            parts = up_sums.shape[0]
            blocks = jnp.concatenate(
                [sums.reshape(count, LEAD, rows).transpose(1, 0, 2), up_sums.reshape(LEAD, parts, rows)], 1
            )
            blocks = jnp.pad(blocks, ((0, 0), (0, VEC_ROWS - count - parts), (0, width - rows))).astype(bf16)
            g_first = ring_scatter(*grad_first_blocks(normed, attended, gq, gk, gv, branch, blocks))
            g_qkv = back_by_columns(g_first[: 3 * rows], rows)
            g_out = g_first[3 * rows : 4 * rows]
            vec_rows = g_first[4 * rows :, :rows]
            g_vecs = {name: vec_rows[at] for at, name in enumerate(VECS)}
            g_vecs["up_bias"] = vec_rows[count : count + parts].reshape(-1)
        else:
            scatter = lambda a: lax.psum_scatter(a, "dp", scatter_dimension=0, tiled=True)
            outer = lambda a, b: lax.dot_general(a, b, TN, preferred_element_type=f32)
            g_down = scatter(outer(activated, upstream))
            g_up = scatter(outer(second, grad_pre))
            g_qkv = scatter(outer(normed, jnp.concatenate([gq, gk, gv], 1)))
            g_out = scatter(outer(attended, branch))
            g_vecs = {name: scatter(sums[at]) for at, name in enumerate(VECS)}
            g_vecs["up_bias"] = scatter(up_sums.reshape(-1))
        return (
            result[None], grad_input[None], g_qkv[None], g_out[None], g_up[None], g_down[None],
            *(
                g_vecs[name][None]
                for name in (
                    "q_bias", "v_bias", "out_bias", "up_bias", "down_bias",
                    "gain_one", "shift_one", "gain_two", "shift_two",
                )
            ),
        )

    rows_spec = P("dp", None)
    three, two = P("section", "dp", None), P("section", "dp")
    return jax.shard_map(
        shards,
        mesh=mesh,
        in_specs=(rows_spec, rows_spec, P("dp"), P("dp")) + (three,) * 4 + (two,) * 9,
        out_specs=(three,) * 6 + (two,) * 9,
        check_vma=False,
    )
```

```python
import functools

import jax
import jax.numpy as jnp
from jax import lax
from jax.experimental import pallas as pl
from jax.experimental.pallas import tpu as pltpu
from jax.sharding import PartitionSpec as P

H = 16
GRID = 16
LEAD = 16
RING = 8
VEC_ROWS = 16

f32 = jnp.float32
bf16 = jnp.bfloat16
eps_norm = 1e-05


def chip_at(place):
    if isinstance(place, int):
        return 2 * place if place < 4 else 2 * (7 - place) + 1
    return jnp.where(place < 4, 2 * place, 2 * (7 - place) + 1)


def place_of(chip):
    if isinstance(chip, int):
        return chip // 2 if chip % 2 == 0 else 7 - chip // 2
    return jnp.where(chip % 2 == 0, chip // 2, 7 - chip // 2)


def ring_route(step):
    return [
        (2 * chip_at(place) + core, 2 * chip_at((place + step) % RING) + core)
        for place in range(RING)
        for core in range(2)
    ]


CORE_ROUTE = [(index, index ^ 1) for index in range(2 * RING)]


def onward(block):
    return lax.ppermute(block, "dp", ring_route(1))


def backward(block):
    return lax.ppermute(block, "dp", ring_route(-1))


def across(block):
    return lax.ppermute(block, "dp", CORE_ROUTE)


def tie(*values):
    leaves, tree = jax.tree.flatten(values)
    arrays = iter(lax.optimization_barrier([leaf for leaf in leaves if isinstance(leaf, jax.Array)]))
    held = jax.tree.unflatten(tree, [next(arrays) if isinstance(leaf, jax.Array) else leaf for leaf in leaves])
    return held if len(held) > 1 else held[0]


def pack_first(qkv, out, vectors, ups):
    rows, width = out.shape
    chunks = qkv.shape[1] // width
    names, size = vectors.shape[0], ups.shape[1]

    def kernel(qkv_ref, out_ref, vec_ref, up_ref, packed_ref):
        me = lax.axis_index("dp")
        for chunk in range(chunks):
            packed_ref[chunk * rows : (chunk + 1) * rows, :] = qkv_ref[:, chunk * width : (chunk + 1) * width]
        packed_ref[chunks * rows : (chunks + 1) * rows, :] = out_ref[...]
        lane = lax.broadcasted_iota(jnp.int32, (names, width), 1)
        spread = jnp.concatenate([vec_ref[...].astype(f32)] * (width // rows), axis=1)
        small = jnp.where((lane >= me * rows) & (lane < (me + 1) * rows), spread, 0.0)
        lane = lax.broadcasted_iota(jnp.int32, (VEC_ROWS - names, width), 1)
        row = lax.broadcasted_iota(jnp.int32, (VEC_ROWS - names, width), 0)
        spread = jnp.concatenate([up_ref[...].astype(f32)] * (width // size), axis=1)
        at = row * width + lane
        last = jnp.where((at >= me * size) & (at < (me + 1) * size), spread, 0.0)
        packed_ref[(chunks + 1) * rows :, :] = jnp.concatenate([small, last], axis=0).astype(bf16)

    return pl.pallas_call(
        kernel,
        out_shape=jax.ShapeDtypeStruct(((chunks + 1) * rows + VEC_ROWS, width), bf16),
        compiler_params=pltpu.CompilerParams(vmem_limit_bytes=2 * 2**20),
        name="pack_first",
    )(qkv, out, vectors, ups)


def pack_second(up, down):
    rows, width = up.shape[0], down.shape[1]
    chunks = up.shape[1] // width

    def kernel(up_ref, down_ref, packed_ref):
        for chunk in range(chunks):
            packed_ref[chunk * rows : (chunk + 1) * rows, :] = up_ref[:, chunk * width : (chunk + 1) * width]
        packed_ref[chunks * rows :, :] = down_ref[...]

    return pl.pallas_call(
        kernel,
        out_shape=jax.ShapeDtypeStruct((chunks * rows + down.shape[0], width), bf16),
        compiler_params=pltpu.CompilerParams(vmem_limit_bytes=2 * 2**20),
        name="pack_second",
    )(up, down)


def half_of(rows):
    return rows // 32 * 16


def gather_start(shard):
    return {"step": 0, "here": {0: shard}, "peer": {}, "up": shard, "down": shard}


def gather_step(state):
    step = state["step"] + 1
    up, down = state["up"], state["down"]
    here, peer = dict(state["here"]), dict(state["peer"])
    if step < RING // 2:
        up, down = onward(up), backward(down)
    else:
        half = half_of(up.shape[0])
        up, down = onward(up[:half]), backward(down[half:])
    for place in here:
        if place not in peer:
            peer[place] = across(here[place])
    if step < RING // 2:
        here[RING - step], here[step] = up, down
    return {"step": step, "here": here, "peer": peer, "up": up, "down": down}


def gather_blocks(state):
    here, peer = state["here"], state["peer"]
    far = [state["up"], state["down"]]
    blocks = []
    for place in range(RING):
        if place == RING // 2:
            blocks += far + [across(block) for block in far]
        else:
            blocks += [here[place], peer[place]]
    return blocks


def assemble(blocks, vectors=False):
    rows, width = blocks[0].shape
    half = half_of(rows)
    count = len(blocks)

    def kernel(*refs):
        blocks_in, out, sems = refs[:count], refs[count], refs[-1]
        me = lax.axis_index("dp")
        core, place = lax.rem(me, 2), place_of(lax.div(me, 2))
        copies = []
        at = 0
        for step in range(RING):
            chip = chip_at(lax.rem(place + step, RING))
            parts = ((0, half), (half, rows - half)) if step == RING // 2 else ((0, rows),)
            for owner in (2 * chip + core, 2 * chip + 1 - core):
                for start, size in parts:
                    copies.append(
                        pltpu.make_async_copy(
                            blocks_in[at], out.at[owner, pl.ds(start, size)], sems.at[at]
                        )
                    )
                    at += 1
        for copy in copies:
            copy.start()
        for copy in copies:
            copy.wait()
        if vectors:
            total = jnp.zeros((VEC_ROWS, width), f32)
            for owner in range(2 * RING):
                total += out[owner, rows - VEC_ROWS :, :].astype(f32)
            refs[count + 1][...] = total

    shapes = [jax.ShapeDtypeStruct((2 * RING, rows, width), blocks[0].dtype)]
    if vectors:
        shapes.append(jax.ShapeDtypeStruct((VEC_ROWS, width), f32))
    outs = pl.pallas_call(
        kernel,
        out_shape=shapes,
        in_specs=[pl.BlockSpec(memory_space=pl.ANY)] * count,
        out_specs=[pl.BlockSpec(memory_space=pltpu.VMEM)] * len(shapes),
        scratch_shapes=[pltpu.SemaphoreType.DMA((count,))],
        compiler_params=pltpu.CompilerParams(vmem_limit_bytes=2**20),
        name="assemble",
    )(*blocks)
    return outs if vectors else outs[0]


def scatter_start(own, peer):
    return {"step": 0, "own": own, "peer": peer}


def hop_kernel(step, half, *refs):
    own_up, peer_up, own_down, peer_down = refs[:4]
    up_out, down_out = refs[-2:]
    top, bottom = slice(0, half), slice(half, None)
    local_up = lambda rows: own_up[0, rows, :].astype(f32) + peer_up[0, rows, :].astype(f32)
    local_down = lambda rows: own_down[0, rows, :].astype(f32) + peer_down[0, rows, :].astype(f32)
    if step == 1:
        up_out[...] = local_up(top).astype(bf16)
        down_out[...] = local_down(bottom).astype(bf16)
        return
    up_in, down_in = refs[4], refs[5]
    if step == 2:
        up_out[top, :] = (local_up(top) + up_in[...].astype(f32)).astype(bf16)
        up_out[bottom, :] = local_up(bottom).astype(bf16)
        down_out[top, :] = local_down(top).astype(bf16)
        down_out[bottom, :] = (local_down(bottom) + down_in[...].astype(f32)).astype(bf16)
        return
    up_out[...] = (local_up(slice(None)) + up_in[...].astype(f32)).astype(bf16)
    down_out[...] = (local_down(slice(None)) + down_in[...].astype(f32)).astype(bf16)


def scatter_step(state, held=()):
    step = state["step"]
    own, peer = state["own"], state["peer"]
    if step == 0:
        peer, held = tie(peer, held)
        return {"step": 1, "own": own, "peer": across(peer)}, held
    rows, width = own.shape[1:]
    half, far = half_of(rows), RING // 2
    at = lambda place: pl.BlockSpec((1, rows, width), lambda i: (place, 0, 0))
    whole = lambda size: pl.BlockSpec((size, width), lambda i: (0, 0))
    up_place, down_place = far + 1 - step, far - 1 + step
    before = [] if step == 1 else [state["up"], state["down"]]
    sizes = (half, rows - half) if step == 1 else (rows, rows)
    up, down = pl.pallas_call(
        functools.partial(hop_kernel, step, half),
        grid=(1,),
        in_specs=[at(up_place), at(up_place), at(down_place), at(down_place)] + [whole(b.shape[0]) for b in before],
        out_specs=[whole(size) for size in sizes],
        out_shape=[jax.ShapeDtypeStruct((size, width), bf16) for size in sizes],
        compiler_params=pltpu.CompilerParams(vmem_limit_bytes=8 * 2**20),
        name="hop",
    )(own, peer, own, peer, *before)
    up, down, held = tie(up, down, held)
    return {"step": step + 1, "own": own, "peer": peer, "up": onward(up), "down": backward(down)}, held


def scatter_sum(state, cuts):
    own, peer = state["own"], state["peer"]
    rows, width = own.shape[1:]
    shapes = [jax.ShapeDtypeStruct((count, chunks * width), f32) for _, count, chunks in cuts]

    def kernel(own_ref, peer_ref, up_ref, down_ref, *outs):
        for (first, count, chunks), out in zip(cuts, outs):
            for chunk in range(chunks):
                here = slice(first + chunk * count, first + (chunk + 1) * count)
                both = own_ref[0, here, :].astype(f32) + peer_ref[0, here, :].astype(f32)
                sent = up_ref[here, :].astype(f32) + down_ref[here, :].astype(f32)
                out[:, chunk * width : (chunk + 1) * width] = both + sent

    at = pl.BlockSpec((1, rows, width), lambda i: (0, 0, 0))
    whole = pl.BlockSpec((rows, width), lambda i: (0, 0))
    return pl.pallas_call(
        kernel,
        grid=(1,),
        in_specs=[at, at, whole, whole],
        out_specs=[pl.BlockSpec(shape.shape, lambda i: (0, 0)) for shape in shapes],
        out_shape=shapes,
        compiler_params=pltpu.CompilerParams(vmem_limit_bytes=12 * 2**20),
        name="scatter_sum",
    )(own, peer, state["up"], state["down"])


VMEM_LIMIT = 24 * 2**20
MLP_CHUNK = 32
ATTN_COST, MLP_COST = 24, 6
Q_BIAS, V_BIAS, OUT_BIAS, DOWN_BIAS, GAIN_ONE, SHIFT_ONE, GAIN_TWO, SHIFT_TWO, UP_BIAS = range(9)
NT = (((1,), (1,)), ((), ()))
TN = (((0,), (0,)), ((), ()))


def dot(first_mat, second_mat):
    return jnp.dot(first_mat, second_mat, preferred_element_type=f32)


def dot_nt(first_mat, second_mat):
    return lax.dot_general(first_mat, second_mat, NT, preferred_element_type=f32)


def dot_tn(first_mat, second_mat):
    return lax.dot_general(first_mat, second_mat, TN, preferred_element_type=f32)


def weight_part(w_ref, part):
    width = w_ref.shape[2]
    rows = width // LEAD
    return w_ref[:, part * rows : (part + 1) * rows, :].reshape(width, width)


def norm_parts(rows_in):
    average = jnp.mean(rows_in, axis=-1, keepdims=True)
    centred = rows_in - average
    inverse = lax.rsqrt(jnp.mean(centred * centred, axis=-1, keepdims=True) + eps_norm)
    return centred * inverse, inverse


def norm_back(rows_in, gain_row, grad_rows):
    unit, inverse = norm_parts(rows_in)
    scaled = grad_rows * gain_row
    mean_one = jnp.mean(scaled, axis=-1, keepdims=True)
    mean_two = jnp.mean(scaled * unit, axis=-1, keepdims=True)
    return (scaled - mean_one - unit * mean_two) * inverse, grad_rows * unit


def head_window(head, head_size, width):
    start = min(head * head_size // 128 * 128, width - 256)
    return start, head * head_size - start


def only_head(block, low, head_size):
    lane = lax.broadcasted_iota(jnp.int32, block.shape, 1)
    return jnp.where((lane >= low) & (lane < low + head_size), block, jnp.zeros_like(block))


def column_sum(rows_in):
    return jnp.sum(rows_in, axis=0, keepdims=True)


def attn_forward_kernel(
    image, heights_ref, widths_ref, x_ref, w_ref, vec_ref,
    middle_ref, second_ref, normed_ref, q_ref, k_ref, v_ref, probs_ref, attended_ref,
    vt_ref, at_ref,
):
    slots, width = x_ref.shape
    head_size = width // H
    step = 64
    for at in range(0, slots, step):
        unit, _ = norm_parts(x_ref[at : at + step, :].astype(f32))
        normed_ref[at : at + step, :] = (
            unit * vec_ref[GAIN_ONE : GAIN_ONE + 1, :] + vec_ref[SHIFT_ONE : SHIFT_ONE + 1, :]
        ).astype(bf16)
    normed = normed_ref[...]
    q_ref[...] = (dot(normed, weight_part(w_ref, 0)) + vec_ref[Q_BIAS : Q_BIAS + 1, :]).astype(bf16)
    k_ref[...] = dot(normed, weight_part(w_ref, 1)).astype(bf16)
    values = dot(normed, weight_part(w_ref, 2)) + vec_ref[V_BIAS : V_BIAS + 1, :]
    v_ref[...] = values.astype(bf16)
    vt_ref[...] = values.astype(bf16).T
    slot = lax.broadcasted_iota(jnp.int32, (slots, 128), 0)
    valid = (slot // GRID < heights_ref[image]) & (slot % GRID < widths_ref[image])
    mask = jnp.where(valid, 0.0, -1e30).astype(f32)
    scale = head_size ** (-0.5)
    for head in range(H):
        start, low = head_window(head, head_size, width)
        queries = only_head(q_ref[:, start : start + 256], low, head_size)
        scores = dot_nt(k_ref[:, start : start + 256], queries)
        for at in range(0, slots, 128):
            part = scores[:, at : at + 128] * scale + mask
            exponent = jnp.exp(part - jnp.max(part, axis=0, keepdims=True))
            inverse = 1.0 / jnp.sum(exponent, axis=0, keepdims=True)
            probs_ref[head, :, at : at + 128] = (exponent * inverse).astype(bf16)
        here = slice(head * head_size, (head + 1) * head_size)
        at_ref[here, :] = dot(vt_ref[here, :], probs_ref[head])
    attended_ref[...] = at_ref[...].T.astype(bf16)
    branch = dot(attended_ref[...], weight_part(w_ref, 3))
    middle_ref[...] = x_ref[...].astype(f32) + (branch + vec_ref[OUT_BIAS : OUT_BIAS + 1, :])
    for at in range(0, slots, step):
        unit, _ = norm_parts(middle_ref[at : at + step, :])
        second_ref[at : at + step, :] = (
            unit * vec_ref[GAIN_TWO : GAIN_TWO + 1, :] + vec_ref[SHIFT_TWO : SHIFT_TWO + 1, :]
        ).astype(bf16)


def attn_forward(layer_input, attn_w, vecs, heights, widths, image):
    slots, width = layer_input.shape
    wide = jax.ShapeDtypeStruct((slots, width), f32)
    low = jax.ShapeDtypeStruct((slots, width), bf16)
    here = pl.BlockSpec(memory_space=pltpu.VMEM)
    return pl.pallas_call(
        functools.partial(attn_forward_kernel, image),
        in_specs=[pl.BlockSpec(memory_space=pltpu.SMEM)] * 2 + [here] * 3,
        out_specs=[here] * 8,
        scratch_shapes=[pltpu.VMEM((width, slots), bf16), pltpu.VMEM((width, slots), f32)],
        out_shape=[wide, low, low, low, low, low, jax.ShapeDtypeStruct((H, slots, slots), bf16), low],
        compiler_params=pltpu.CompilerParams(vmem_limit_bytes=6 * 2**20),
        cost_estimate=pl.CostEstimate(
            flops=ATTN_COST * slots * width * width, bytes_accessed=attn_w.size * 2, transcendentals=slots * slots * H
        ),
        name="attn_forward",
    )(heights, widths, layer_input, attn_w, vecs)


def mlp_up_kernel(keep_slope, pieces, *refs):
    second_refs, (up_ref, vec_ref, act_ref) = refs[:pieces], refs[pieces : pieces + 3]
    slope_ref = refs[pieces + 3] if keep_slope else None
    pre_ref = refs[-1]
    index = pl.program_id(0)
    slots, width = second_refs[0].shape
    weight = up_ref[...].reshape(width, width)
    for piece, second_ref in enumerate(second_refs):
        pre_ref[piece * slots : (piece + 1) * slots, :] = dot(second_ref[...], weight)
    bias = vec_ref[pl.ds(UP_BIAS + index, 1), :]

    def gelu_rows(at, _):
        here = pl.ds(at * MLP_CHUNK, MLP_CHUNK)
        pre = pre_ref[here, :] + bias
        below = 0.5 * (1.0 + lax.erf(pre * (0.5**0.5)))
        act_ref[here, :] = (pre * below).astype(bf16)
        if keep_slope:
            bell = jnp.exp(-0.5 * pre * pre) * (0.5 / jnp.pi) ** 0.5
            slope_ref[here, :] = (below + pre * bell).astype(bf16)
        return 0

    lax.fori_loop(0, pre_ref.shape[0] // MLP_CHUNK, gelu_rows, 0)


def mlp_up(second, mlp_w, vecs, keep_slope):
    slots, width = second[0].shape
    count = slots * len(second)
    parts = mlp_w.shape[1] * LEAD // (2 * width)
    outs = 2 if keep_slope else 1
    return pl.pallas_call(
        functools.partial(mlp_up_kernel, keep_slope, len(second)),
        grid=(parts,),
        in_specs=[pl.BlockSpec((slots, width), lambda j: (0, 0))] * len(second)
        + [
            pl.BlockSpec((LEAD, width // LEAD, width), lambda j: (0, j, 0)),
            pl.BlockSpec(vecs.shape, lambda j: (0, 0)),
        ],
        out_specs=[pl.BlockSpec((count, width), lambda j: (0, j))] * outs,
        out_shape=[jax.ShapeDtypeStruct((count, width * parts), bf16)] * outs,
        scratch_shapes=[pltpu.VMEM((count, width), f32)],
        compiler_params=pltpu.CompilerParams(vmem_limit_bytes=14 * 2**20),
        cost_estimate=pl.CostEstimate(
            flops=MLP_COST * count * width * width * parts,
            bytes_accessed=mlp_w.size + count * width * 4 * parts,
            transcendentals=2 * count * width * parts,
        ),
        name="mlp_up",
    )(*second, mlp_w, vecs)


def mlp_down_kernel(pieces, act_ref, *refs):
    middle_refs, (down_ref, vec_ref, result_ref, acc_ref) = refs[:pieces], refs[pieces:]
    index = pl.program_id(0)
    slots, width = middle_refs[0].shape
    added = dot(act_ref[...], down_ref[...].reshape(width, width))

    @pl.when(index == 0)
    def _():
        for piece, middle_ref in enumerate(middle_refs):
            here = slice(piece * slots, (piece + 1) * slots)
            acc_ref[here, :] = added[here] + (middle_ref[...] + vec_ref[DOWN_BIAS : DOWN_BIAS + 1, :])

    @pl.when(index > 0)
    def _():
        acc_ref[...] += added

    @pl.when(index == pl.num_programs(0) - 1)
    def _():
        result_ref[...] = acc_ref[...].astype(bf16)


def mlp_down(activated, middle, mlp_w, vecs, image=0):
    slots, width = middle[0].shape
    count = slots * len(middle)
    parts = activated.shape[1] // width
    return pl.pallas_call(
        functools.partial(mlp_down_kernel, len(middle)),
        grid=(parts,),
        in_specs=[pl.BlockSpec((count, width), lambda j: (image, j))]
        + [pl.BlockSpec((slots, width), lambda j: (0, 0))] * len(middle)
        + [
            pl.BlockSpec((LEAD // parts, mlp_w.shape[1] // 2, width), lambda j: (j, 1, 0)),
            pl.BlockSpec(vecs.shape, lambda j: (0, 0)),
        ],
        out_specs=pl.BlockSpec((count, width), lambda j: (0, 0)),
        out_shape=jax.ShapeDtypeStruct((count, width), bf16),
        scratch_shapes=[pltpu.VMEM((count, width), f32)],
        compiler_params=pltpu.CompilerParams(vmem_limit_bytes=12 * 2**20),
        cost_estimate=pl.CostEstimate(
            flops=MLP_COST * count * width * width * parts,
            bytes_accessed=mlp_w.size + count * width * 10,
            transcendentals=0,
        ),
        name="mlp_down",
    )(activated, *middle, mlp_w, vecs)


def mlp_backward_kernel(pieces, slope_ref, *refs):
    upstream_refs, middle_refs, refs = refs[:pieces], refs[pieces : 2 * pieces], refs[2 * pieces :]
    (up_ref, down_ref, vec_ref), refs = refs[:3], refs[3:]
    grad_middle_refs, branch_refs, refs = refs[:pieces], refs[pieces : 2 * pieces], refs[2 * pieces :]
    grad_pre_ref, sums_ref, up_sum_ref, ga_ref, acc_ref = refs
    index = pl.program_id(0)
    slots, width = upstream_refs[0].shape
    count = slots * pieces
    weight = down_ref[...].reshape(width, width)
    for piece, upstream_ref in enumerate(upstream_refs):
        ga_ref[piece * slots : (piece + 1) * slots, :] = dot_nt(upstream_ref[...], weight)
    sums = jnp.zeros((1, width), f32)
    for at in range(0, count, MLP_CHUNK):
        here = slice(at, at + MLP_CHUNK)
        pre = (ga_ref[here, :] * slope_ref[here, :].astype(f32)).astype(bf16)
        grad_pre_ref[here, :] = pre
        sums += column_sum(pre.astype(f32))
    up_sum_ref[0] = sums
    added = dot_nt(grad_pre_ref[...], up_ref[...].reshape(width, width))

    @pl.when(index == 0)
    def _():
        acc_ref[...] = added

    @pl.when(index > 0)
    def _():
        acc_ref[...] += added

    @pl.when(index == pl.num_programs(0) - 1)
    def _():
        gain = vec_ref[GAIN_TWO : GAIN_TWO + 1, :]
        sums = [jnp.zeros((1, width), f32)] * 3
        for piece in range(pieces):
            for at in range(0, slots, MLP_CHUNK):
                here = slice(at, at + MLP_CHUNK)
                upstream = upstream_refs[piece][here, :].astype(f32)
                grad = acc_ref[piece * slots + at : piece * slots + at + MLP_CHUNK, :]
                grad_mid, gain_terms = norm_back(middle_refs[piece][here, :], gain, grad)
                total = upstream + grad_mid
                grad_middle_refs[piece][here, :] = total
                branch_refs[piece][here, :] = total.astype(bf16)
                sums = [old + column_sum(new) for old, new in zip(sums, (upstream, gain_terms, grad))]
        for row, value in enumerate(sums):
            sums_ref[row : row + 1, :] = value


def mlp_backward(upstream, slope, middle, mlp_w, vecs, image=0):
    slots, width = middle[0].shape
    pieces = len(middle)
    count = slots * pieces
    parts = mlp_w.shape[1] * LEAD // (2 * width)
    whole = pl.BlockSpec((slots, width), lambda j: (0, 0))
    chunk = pl.BlockSpec((count, width), lambda j: (0, j))
    outs = pl.pallas_call(
        functools.partial(mlp_backward_kernel, pieces),
        grid=(parts,),
        in_specs=[pl.BlockSpec((count, width), lambda j: (image, j))]
        + [whole] * 2 * pieces
        + [
            pl.BlockSpec((LEAD, width // LEAD, width), lambda j: (0, j, 0)),
            pl.BlockSpec((LEAD // parts, mlp_w.shape[1] // 2, width), lambda j: (j, 1, 0)),
            pl.BlockSpec(vecs.shape, lambda j: (0, 0)),
        ],
        out_specs=[whole] * 2 * pieces
        + [
            chunk,
            pl.BlockSpec((8, width), lambda j: (0, 0)),
            pl.BlockSpec((1, 1, width), lambda j: (j, 0, 0)),
        ],
        out_shape=[jax.ShapeDtypeStruct((slots, width), f32)] * pieces
        + [jax.ShapeDtypeStruct((slots, width), bf16)] * pieces
        + [
            jax.ShapeDtypeStruct((count, width * parts), bf16),
            jax.ShapeDtypeStruct((8, width), f32),
            jax.ShapeDtypeStruct((parts, 1, width), f32),
        ],
        scratch_shapes=[pltpu.VMEM((count, width), f32)] * 2,
        compiler_params=pltpu.CompilerParams(vmem_limit_bytes=20 * 2**20),
        cost_estimate=pl.CostEstimate(
            flops=2 * MLP_COST * count * width * width * parts,
            bytes_accessed=mlp_w.size * 2 + count * width * (10 + 4 * parts),
            transcendentals=0,
        ),
        name="mlp_backward",
    )(slope, *upstream, *middle, mlp_w, mlp_w, vecs)
    return outs[:pieces], outs[pieces : 2 * pieces], *outs[2 * pieces :]


def attn_backward_kernel(
    grad_middle_ref, branch_ref, x_ref, q_ref, k_ref, v_ref, probs_ref, w_ref, vec_ref,
    grad_in_ref, grad_low_ref, gq_ref, gk_ref, gv_ref, sums_ref,
    ga_ref, gat_ref, qt_ref, kt_ref, gqt_ref, gkt_ref, gvt_ref,
):
    slots, width = x_ref.shape
    head_size = width // H
    scale = head_size ** (-0.5)
    ga = dot_nt(branch_ref[...], weight_part(w_ref, 3)).astype(bf16)
    ga_ref[...] = ga
    gat_ref[...] = ga.T
    qt_ref[...] = q_ref[...].T
    kt_ref[...] = k_ref[...].T
    for head in range(H):
        start, low = head_window(head, head_size, width)
        here = slice(head * head_size, (head + 1) * head_size)
        own = only_head(ga_ref[:, start : start + 256], low, head_size)
        grad_probs = dot_nt(v_ref[:, start : start + 256], own)
        pieces = []
        for at in range(0, slots, 128):
            probs = probs_ref[head, :, at : at + 128].astype(f32)
            grad = grad_probs[:, at : at + 128]
            total = jnp.sum(probs * grad, axis=0, keepdims=True)
            pieces.append((probs * (grad - total)).astype(bf16))
        grad_scores = jnp.concatenate(pieces, axis=1)
        gvt_ref[here, :] = dot_nt(gat_ref[here, :], probs_ref[head])
        gqt_ref[here, :] = dot(kt_ref[here, :], grad_scores) * scale
        gkt_ref[here, :] = dot_nt(qt_ref[here, :], grad_scores) * scale
    gq_ref[...] = gqt_ref[...].T.astype(bf16)
    gk_ref[...] = gkt_ref[...].T.astype(bf16)
    gv_ref[...] = gvt_ref[...].T.astype(bf16)
    grad_normed = dot_nt(gq_ref[...], weight_part(w_ref, 0))
    grad_normed += dot_nt(gk_ref[...], weight_part(w_ref, 1))
    grad_normed += dot_nt(gv_ref[...], weight_part(w_ref, 2))
    grad_in_ref[...] = grad_normed
    gain = vec_ref[GAIN_ONE : GAIN_ONE + 1, :]
    sums = [jnp.zeros((1, width), f32)] * 5
    for at in range(0, slots, MLP_CHUNK):
        rows = slice(at, at + MLP_CHUNK)
        grad = grad_in_ref[rows, :]
        grad_norm, gain_terms = norm_back(x_ref[rows, :].astype(f32), gain, grad)
        total = grad_middle_ref[rows, :] + grad_norm
        grad_in_ref[rows, :] = total
        grad_low_ref[rows, :] = total.astype(bf16)
        terms = (
            gq_ref[rows, :].astype(f32), gv_ref[rows, :].astype(f32), branch_ref[rows, :].astype(f32),
            gain_terms, grad,
        )
        sums = [old + column_sum(new) for old, new in zip(sums, terms)]

    for row, value in enumerate(sums):
        sums_ref[row : row + 1, :] = value


def attn_backward(grad_middle, branch, layer_input, saved, attn_w, vecs):
    queries, key_rows, values, probs = saved
    slots, width = layer_input.shape
    low = jax.ShapeDtypeStruct((slots, width), bf16)
    here = pl.BlockSpec(memory_space=pltpu.VMEM)
    flipped = pltpu.VMEM((width, slots), bf16)
    flipped_wide = pltpu.VMEM((width, slots), f32)
    return pl.pallas_call(
        attn_backward_kernel,
        in_specs=[here] * 9,
        out_specs=[here] * 6,
        out_shape=[jax.ShapeDtypeStruct((slots, width), f32)] + [low] * 4 + [jax.ShapeDtypeStruct((8, width), f32)],
        scratch_shapes=[pltpu.VMEM((slots, width), bf16)] + [flipped] * 3 + [flipped_wide] * 3,
        compiler_params=pltpu.CompilerParams(vmem_limit_bytes=8 * 2**20),
        cost_estimate=pl.CostEstimate(
            flops=ATTN_COST * slots * width * width, bytes_accessed=attn_w.size * 2, transcendentals=0
        ),
        name="attn_backward",
    )(grad_middle, branch, layer_input, queries, key_rows, values, probs, attn_w, vecs)


def ring_slot(owner, me):
    there, here = place_of(lax.div(owner, 2)), place_of(lax.div(me, 2))
    return lax.rem(there - here + RING, RING)


def store_block(own_ref, peer_ref, owner, core, rows, value):
    me = lax.axis_index("dp")
    slot = ring_slot(owner, me)

    @pl.when(lax.rem(me, 2) == core)
    def _():
        own_ref[slot, rows, :] = value

    @pl.when(lax.rem(me, 2) != core)
    def _():
        peer_ref[slot, rows, :] = value


def scatter_shapes(rows, width):
    return [jax.ShapeDtypeStruct((RING, rows, width), bf16)] * 2


def joined(refs, scratch_ref):
    slots = refs[0].shape[0]
    for piece, ref in enumerate(refs):
        scratch_ref[piece * slots : (piece + 1) * slots, :] = ref[...]


def flipped(refs, scratch_ref):
    slots = refs[0].shape[0]
    for piece, ref in enumerate(refs):
        scratch_ref[:, piece * slots : (piece + 1) * slots] = ref[...].T


def grad_down_kernel(pieces, act_ref, *refs):
    upstream_refs, (own_ref, peer_ref, right_ref) = refs[:pieces], refs[pieces:]
    index = pl.program_id(0)
    rows = own_ref.shape[1]

    @pl.when(index == 0)
    def _():
        joined(upstream_refs, right_ref)

    value = dot_tn(act_ref[...], right_ref[...]).astype(bf16)
    for at in range(value.shape[0] // rows):
        owner = index * (value.shape[0] // rows) + at
        store_block(own_ref, peer_ref, owner, at % 2, slice(None), value[at * rows : (at + 1) * rows])


def grad_down_blocks(activated, upstream):
    slots, width = upstream[0].shape
    count, hidden = activated.shape
    parts = hidden // width
    rows = hidden // LEAD
    return pl.pallas_call(
        functools.partial(grad_down_kernel, len(upstream)),
        grid=(parts,),
        in_specs=[pl.BlockSpec((count, width), lambda j: (0, j))]
        + [pl.BlockSpec((slots, width), lambda j: (0, 0))] * len(upstream),
        out_specs=[pl.BlockSpec((RING, rows, width), lambda j: (0, 0, 0))] * 2,
        out_shape=scatter_shapes(rows, width),
        scratch_shapes=[pltpu.VMEM((count, width), bf16)],
        compiler_params=pltpu.CompilerParams(vmem_limit_bytes=18 * 2**20),
        cost_estimate=pl.CostEstimate(
            flops=MLP_COST * count * width * hidden, bytes_accessed=count * hidden * 2 + hidden * width * 2, transcendentals=0
        ),
        name="grad_down",
    )(activated, *upstream)


def grad_up_kernel(pieces, *refs):
    pre_refs, second_refs, attended_refs, branch_refs, (own_ref, peer_ref, left_ref, right_ref) = (
        *(refs[at * pieces : (at + 1) * pieces] for at in range(4)), refs[4 * pieces :]
    )
    index = pl.program_id(0)
    rows = second_refs[0].shape[1] // LEAD

    @pl.when(index == 0)
    def _():
        flipped(second_refs, left_ref)

    joined(pre_refs, right_ref)
    value = dot(left_ref[...], right_ref[...]).astype(bf16)
    for owner in range(LEAD):
        here = pl.ds(pl.multiple_of(index * rows, rows), rows)
        store_block(own_ref, peer_ref, owner, owner % 2, here, value[owner * rows : (owner + 1) * rows])

    @pl.when(index == pl.num_programs(0) - 1)
    def _():
        flipped(attended_refs, left_ref)
        joined(branch_refs, right_ref)
        last = dot(left_ref[...], right_ref[...]).astype(bf16)
        for owner in range(LEAD):
            here = pl.ds(own_ref.shape[1] - rows, rows)
            store_block(own_ref, peer_ref, owner, owner % 2, here, last[owner * rows : (owner + 1) * rows])


def grad_up_blocks(second, grad_pre, attended, branch):
    slots, width = second[0].shape
    count, hidden = slots * len(second), grad_pre[0].shape[1]
    parts = hidden // width
    rows = (hidden + width) // LEAD
    whole = [pl.BlockSpec((slots, width), lambda j: (0, 0))] * len(second)
    return pl.pallas_call(
        functools.partial(grad_up_kernel, len(second)),
        grid=(parts,),
        in_specs=[pl.BlockSpec((slots, width), lambda j: (0, j))] * len(second) + whole * 3,
        out_specs=[pl.BlockSpec((RING, rows, width), lambda j: (0, 0, 0))] * 2,
        out_shape=scatter_shapes(rows, width),
        scratch_shapes=[pltpu.VMEM((width, count), bf16), pltpu.VMEM((count, width), bf16)],
        compiler_params=pltpu.CompilerParams(vmem_limit_bytes=24 * 2**20),
        cost_estimate=pl.CostEstimate(
            flops=MLP_COST * count * width * hidden, bytes_accessed=count * hidden * 2 + hidden * width * 2, transcendentals=0
        ),
        name="grad_up",
    )(*grad_pre, *second, *attended, *branch)


def grad_qkv_kernel(pieces, *refs):
    left_refs, rights = refs[:pieces], refs[pieces : 4 * pieces]
    attn_sums, mlp_sums, up_sums = (refs[at * pieces : (at + 1) * pieces] for at in (4, 5, 6))
    own_ref, peer_ref, left_ref, right_ref, vec_ref = refs[7 * pieces :]
    width = left_refs[0].shape[1]
    rows = width // LEAD
    flipped(left_refs, left_ref)
    for part in range(3):
        joined(rights[part * pieces : (part + 1) * pieces], right_ref)
        value = dot(left_ref[...], right_ref[...]).astype(bf16)
        for owner in range(LEAD):
            here = slice(part * rows, (part + 1) * rows)
            store_block(own_ref, peer_ref, owner, owner % 2, here, value[owner * rows : (owner + 1) * rows])
    vec_ref[...] = jnp.zeros_like(vec_ref)
    for name, refs_of, row in (
        (Q_BIAS, attn_sums, 0), (V_BIAS, attn_sums, 1), (OUT_BIAS, attn_sums, 2), (DOWN_BIAS, mlp_sums, 0),
        (GAIN_ONE, attn_sums, 3), (SHIFT_ONE, attn_sums, 4), (GAIN_TWO, mlp_sums, 1), (SHIFT_TWO, mlp_sums, 2),
    ):
        vec_ref[name : name + 1, :] = sum(ref[row : row + 1, :] for ref in refs_of)
    for part in range(up_sums[0].shape[0]):
        vec_ref[UP_BIAS + part : UP_BIAS + part + 1, :] = sum(ref[part] for ref in up_sums)
    vectors = vec_ref[...].astype(bf16)
    here = slice(3 * rows, 3 * rows + VEC_ROWS)
    for slot in range(RING):
        own_ref[slot, here, :] = vectors
        peer_ref[slot, here, :] = vectors


def grad_qkv_blocks(normed, rights, attn_sums, mlp_sums, up_sums):
    slots, width = normed[0].shape
    count = slots * len(normed)
    arrays = [*normed, *(piece for right in rights for piece in right), *attn_sums, *mlp_sums, *up_sums]
    rows = 3 * width // LEAD + VEC_ROWS
    return pl.pallas_call(
        functools.partial(grad_qkv_kernel, len(normed)),
        in_specs=[pl.BlockSpec(memory_space=pltpu.VMEM)] * len(arrays),
        out_specs=[pl.BlockSpec(memory_space=pltpu.VMEM)] * 2,
        out_shape=scatter_shapes(rows, width),
        scratch_shapes=[
            pltpu.VMEM((width, count), bf16), pltpu.VMEM((count, width), bf16), pltpu.VMEM((VEC_ROWS, width), f32)
        ],
        compiler_params=pltpu.CompilerParams(vmem_limit_bytes=6 * 2**20),
        cost_estimate=pl.CostEstimate(
            flops=3 * MLP_COST * count * width * width, bytes_accessed=len(arrays) * slots * width * 2, transcendentals=0
        ),
        name="grad_qkv",
    )(*arrays)


VECS = ("q_bias", "v_bias", "out_bias", "down_bias", "gain_one", "shift_one", "gain_two", "shift_two")


def solution(mesh):
    dp_size = mesh.shape["dp"]
    ringed = dp_size == 2 * RING

    def gathered_whole(qkv, out, up, down, vectors):
        width = out.shape[1]
        gathered = [lax.all_gather(w, "dp", axis=0, tiled=True) for w in (qkv, out, up, down)]
        blocked = [w.reshape(LEAD, -1, w.shape[1]) for w in gathered]
        fold = lambda w: w.reshape(LEAD, w.shape[1], -1, width).transpose(0, 2, 1, 3).reshape(LEAD, -1, width)
        first = jnp.concatenate([fold(blocked[0]), blocked[1], jnp.zeros((LEAD, VEC_ROWS, width), bf16)], 1)
        whole = lambda name: lax.all_gather(vectors[name], "dp", axis=0, tiled=True)
        vecs = jnp.concatenate([jnp.stack([whole(name) for name in VECS]), whole("up_bias").reshape(-1, width)])
        vecs = jnp.pad(vecs.astype(f32), ((0, VEC_ROWS - vecs.shape[0]), (0, 0)))
        return first, jnp.concatenate([fold(blocked[2]), blocked[3]], 1), vecs

    def own_vectors(block):
        me = lax.axis_index("dp")
        width = block.shape[1]
        rows = width // LEAD
        small = lax.dynamic_slice(block, (0, me * rows), (len(VECS), rows))
        parts = (3 * LEAD + LEAD) * rows // width
        size = parts * rows
        in_row = width // size
        own = {name: small[at] for at, name in enumerate(VECS)}
        own["up_bias"] = lax.dynamic_slice(block, (len(VECS) + me // in_row, me % in_row * size), (1, size))[0]
        return own

    def shards(
        tokens, cotangent, heights, widths, qkv_weight, out_weight, up_weight, down_weight,
        q_bias, v_bias, out_bias, up_bias, down_bias, gain_one, shift_one, gain_two, shift_two,
    ):
        leading = lax.axis_index("section") == 0
        width = tokens.shape[1]
        images = heights.shape[0]
        each = range(images)
        rows = width // LEAD
        cut = lambda array: jnp.split(array, images)
        vectors = dict(
            q_bias=q_bias[0], v_bias=v_bias[0], out_bias=out_bias[0], up_bias=up_bias[0], down_bias=down_bias[0],
            gain_one=gain_one[0], shift_one=shift_one[0], gain_two=gain_two[0], shift_two=shift_two[0],
        )
        inputs, cotangents = cut(tokens), cut(cotangent)

        attention = lambda x, image: attn_forward(x, attn_w, vecs, heights, widths, image)
        if ringed:
            small = jnp.stack([vectors[name] for name in VECS])
            g = gather_start(pack_first(qkv_weight[0], out_weight[0], small, vectors["up_bias"][None]))
            m = gather_start(pack_second(up_weight[0], down_weight[0]))
            for _ in range(RING // 2 - 1):
                g, m = tie(gather_step(g), m)
            g, m = gather_step(g), gather_step(m)
            attn_w, vecs = assemble(gather_blocks(g), True)
            m, attn_w, vecs = tie(m, attn_w, vecs)
            m = gather_step(m)
            front = [attention(inputs[image], image)[:2] for image in each]
            m, front = tie(m, front)
            for _ in range(m["step"], RING // 2):
                m = gather_step(m)
            mlp_w = assemble(gather_blocks(m))
        else:
            attn_w, mlp_w, vecs = gathered_whole(
                qkv_weight[0], out_weight[0], up_weight[0], down_weight[0], vectors
            )
            front = [attention(inputs[image], image)[:2] for image in each]
        received = []
        for image in each:
            (activated,) = mlp_up(front[image][1:], mlp_w, vecs, False)
            sent = mlp_down(activated, front[image][:1], mlp_w, vecs)
            front, sent = tie(front, sent)
            received.append(lax.ppermute(sent, "section", [(0, 1)]))

        layer_input, kept = [], []
        for image in each:
            layer_input.append(jnp.where(leading, inputs[image], received[image]))
            kept.append(attention(layer_input[image], image))
            kept, received = tie(kept, received)
        middle, second, normed, queries, key_rows, values, probs, attended = zip(*kept)
        activated, slope = mlp_up(second, mlp_w, vecs, True)

        back_attn = lambda grad, branch, image: attn_backward(
            grad[image], branch[image], layer_input[image],
            (queries[image], key_rows[image], values[image], probs[image]), attn_w, vecs,
        )
        grad_middle, branch = mlp_backward(cotangents, slope, middle, mlp_w, vecs)[:2]
        arriving = []
        for image in each:
            to_send = back_attn(grad_middle, branch, image)[1]
            grad_middle, branch, activated, to_send = tie(grad_middle, branch, activated, to_send)
            arriving.append(lax.ppermute(to_send, "section", [(1, 0)]))
        upstream, back = [], []

        def back_one(image):
            upstream.append(jnp.where(leading, arriving[image], cotangents[image]))
            back.append(mlp_backward(upstream[image:], slope, middle[image : image + 1], mlp_w, vecs, image))

        back_one(0)
        back, arriving, activated = tie(back, arriving, activated)
        result = mlp_down(activated, middle, mlp_w, vecs)
        result, arriving, activated = tie(result, arriving, activated)
        if ringed:
            rest = [jnp.where(leading, arriving[image], cotangents[image]) for image in each[1:]]
            d = scatter_start(*grad_down_blocks(activated, upstream + rest))
            d, arriving = scatter_step(d, arriving)
            for image in each[1:]:
                back_one(image)
            d, back = tie(d, back)
            d, back = scatter_step(d, back)
            grad_middle, branch, grad_pre, mlp_sums, up_sums = zip(*back)
            grad_middle, branch = [g for (g,) in grad_middle], [g for (g,) in branch]
            u = scatter_start(*grad_up_blocks(second, grad_pre, attended, branch))
            d, u = tie(d, u)
            held = (grad_middle, branch)
            attn_back = []
            for image in each:
                if image < 2:
                    d, held = scatter_step(d, held)
                    u, held = scatter_step(u, held)
                attn_back.append(back_attn(*held, image))
                d, u, attn_back, held = tie(d, u, attn_back, held)
            d, attn_back = scatter_step(d, attn_back)
            u, attn_back = scatter_step(u, attn_back)
        else:
            for image in each[1:]:
                back_one(image)
            grad_middle, branch, grad_pre, mlp_sums, up_sums = zip(*back)
            grad_middle, branch = [g for (g,) in grad_middle], [g for (g,) in branch]
            attn_back = [back_attn(grad_middle, branch, image) for image in each]
        grad_input, _, gq, gk, gv, attn_sums = zip(*attn_back)
        if ringed:
            q = scatter_start(*grad_qkv_blocks(normed, (gq, gk, gv), attn_sums, mlp_sums, up_sums))
            parts = mlp_w.shape[1] // rows - 4
            ends = RING // 2 + 1
            q = scatter_step(scatter_step(q)[0])[0]
            d, q = tie(d, q)
            while min(d["step"], u["step"], q["step"]) < ends:
                d, u, q = (state if state["step"] == ends else scatter_step(state)[0] for state in (d, u, q))
            (g_down,) = scatter_sum(d, [(0, d["own"].shape[1], 1)])
            g_up, g_out = scatter_sum(u, [(0, rows, parts), (parts * rows, rows, 1)])
            g_qkv, vec_sums = scatter_sum(q, [(0, rows, 3), (3 * rows, VEC_ROWS, 1)])
            g_vecs = own_vectors(vec_sums)
        else:
            attn_sums = sum(attn_sums)
            sums = dict(zip(("q_bias", "v_bias", "out_bias", "gain_one", "shift_one"), attn_sums))
            sums |= dict(zip(("down_bias", "gain_two", "shift_two"), sum(mlp_sums)))
            sums["up_bias"] = sum(up_sums).reshape(-1)
            scatter = lambda a: lax.psum_scatter(a, "dp", scatter_dimension=0, tiled=True)
            whole = lambda pieces: jnp.concatenate(pieces)
            outer = lambda a, b: lax.dot_general(a, b, TN, preferred_element_type=f32)
            g_down = scatter(outer(activated, whole(upstream)))
            g_up = scatter(outer(whole(second), whole(grad_pre)))
            g_qkv = scatter(jnp.concatenate([outer(whole(normed), whole(part)) for part in (gq, gk, gv)], 1))
            g_out = scatter(outer(whole(attended), whole(branch)))
            g_vecs = {name: scatter(value) for name, value in sums.items()}
        return (
            result[None], jnp.concatenate(grad_input)[None],
            g_qkv[None], g_out[None], g_up[None], g_down[None],
            *(
                g_vecs[name][None]
                for name in (
                    "q_bias", "v_bias", "out_bias", "up_bias", "down_bias",
                    "gain_one", "shift_one", "gain_two", "shift_two",
                )
            ),
        )

    rows_spec = P("dp", None)
    three, two = P("section", "dp", None), P("section", "dp")
    return jax.shard_map(
        shards,
        mesh=mesh,
        in_specs=(rows_spec, rows_spec, P("dp"), P("dp")) + (three,) * 4 + (two,) * 9,
        out_specs=(three,) * 6 + (two,) * 9,
        check_vma=False,
    )
```

```python
import functools

import jax
import jax.numpy as jnp
from jax import lax
from jax.experimental import pallas as pl
from jax.experimental.pallas import tpu as pltpu
from jax.sharding import PartitionSpec as P

H = 16
GRID = 16
LEAD = 16
RING = 8
VEC_ROWS = 16

f32 = jnp.float32
bf16 = jnp.bfloat16
eps_norm = 1e-05


def chip_at(place):
    if isinstance(place, int):
        return 2 * place if place < 4 else 2 * (7 - place) + 1
    return jnp.where(place < 4, 2 * place, 2 * (7 - place) + 1)


def place_of(chip):
    if isinstance(chip, int):
        return chip // 2 if chip % 2 == 0 else 7 - chip // 2
    return jnp.where(chip % 2 == 0, chip // 2, 7 - chip // 2)


def ring_route(step):
    return [
        (2 * chip_at(place) + core, 2 * chip_at((place + step) % RING) + core)
        for place in range(RING)
        for core in range(2)
    ]


CORE_ROUTE = [(index, index ^ 1) for index in range(2 * RING)]


def onward(block):
    return lax.ppermute(block, "dp", ring_route(1))


def backward(block):
    return lax.ppermute(block, "dp", ring_route(-1))


def across(block):
    return lax.ppermute(block, "dp", CORE_ROUTE)


def around(block):
    route = [(2 * chip_at(p) + core, 2 * chip_at((p + (-1) ** core) % RING) + core) for p in range(RING) for core in (0, 1)]
    return lax.ppermute(block, "dp", route)


def tie(*values):
    leaves, tree = jax.tree.flatten(values)
    arrays = iter(lax.optimization_barrier([leaf for leaf in leaves if isinstance(leaf, jax.Array)]))
    held = jax.tree.unflatten(tree, [next(arrays) if isinstance(leaf, jax.Array) else leaf for leaf in leaves])
    return held if len(held) > 1 else held[0]


def pack_first(qkv, out, vectors, ups):
    rows, width = out.shape
    chunks = qkv.shape[1] // width
    names, size = vectors.shape[0], ups.shape[1]

    def kernel(qkv_ref, out_ref, vec_ref, up_ref, one_ref, two_ref):
        me = lax.axis_index("dp")
        for chunk in range(chunks):
            packed_ref, at = (one_ref, chunk) if chunk < 2 else (two_ref, chunk - 2)
            packed_ref[at * rows : (at + 1) * rows, :] = qkv_ref[:, chunk * width : (chunk + 1) * width]
        two_ref[(chunks - 2) * rows : (chunks - 1) * rows, :] = out_ref[...]
        lane = lax.broadcasted_iota(jnp.int32, (names, width), 1)
        spread = jnp.concatenate([vec_ref[...].astype(f32)] * (width // rows), axis=1)
        small = jnp.where((lane >= me * rows) & (lane < (me + 1) * rows), spread, 0.0)
        lane = lax.broadcasted_iota(jnp.int32, (VEC_ROWS - names, width), 1)
        row = lax.broadcasted_iota(jnp.int32, (VEC_ROWS - names, width), 0)
        spread = jnp.concatenate([up_ref[...].astype(f32)] * (width // size), axis=1)
        at = row * width + lane
        last = jnp.where((at >= me * size) & (at < (me + 1) * size), spread, 0.0)
        two_ref[(chunks - 1) * rows :, :] = jnp.concatenate([small, last], axis=0).astype(bf16)

    return pl.pallas_call(
        kernel,
        out_shape=[
            jax.ShapeDtypeStruct((2 * rows, width), bf16),
            jax.ShapeDtypeStruct(((chunks - 1) * rows + VEC_ROWS, width), bf16),
        ],
        compiler_params=pltpu.CompilerParams(vmem_limit_bytes=4 * 2**20),
        name="pack_first",
    )(qkv, out, vectors, ups)


def pack_columns(weight, width):
    rows, columns = weight.shape
    chunks = columns // width

    def kernel(weight_ref, packed_ref):
        for chunk in range(chunks):
            packed_ref[chunk * rows : (chunk + 1) * rows, :] = weight_ref[:, chunk * width : (chunk + 1) * width]

    return pl.pallas_call(
        kernel,
        out_shape=jax.ShapeDtypeStruct((chunks * rows, width), bf16),
        compiler_params=pltpu.CompilerParams(vmem_limit_bytes=4 * 2**20),
        name="pack_columns",
    )(weight)


def half_of(rows):
    return rows // 32 * 16


def gather_start(shard):
    return {"step": 0, "rows": shard.shape[0], "mine": [jnp.concatenate([shard, across(shard)])], "theirs": []}


def gather_step(state):
    step, rows = state["step"] + 1, state["rows"]
    mine, theirs = list(state["mine"]), list(state["theirs"])
    if step > 2:
        mine[-1], theirs[-2] = tie(mine[-1], theirs[-2])
    came = around(mine[-1] if step < RING // 2 else mine[-1][:rows])
    return {"step": step, "rows": rows, "mine": [*mine, came], "theirs": [*theirs, across(came)]}


def assemble(states, vectors=False):
    width = states[0]["mine"][0].shape[1]
    arrays = [array for state in states for array in state["mine"] + state["theirs"]]
    count = len(arrays)
    total_rows = sum(state["rows"] for state in states)

    def kernel(*refs):
        blocks, out = refs[:count], refs[count]
        me = lax.axis_index("dp")
        core, place = lax.rem(me, 2), place_of(lax.div(me, 2))
        way = 1 - 2 * core
        at, start = 0, 0
        for state in states:
            rows = state["rows"]
            for steps, own_first in ((range(RING // 2 + 1), 1), (range(1, RING // 2 + 1), 0)):
                for step in steps:
                    toward = step * way if not own_first else -step * way
                    chip = chip_at(lax.rem(place + toward + RING, RING))
                    first = core if own_first else 1 - core
                    out[2 * chip + first, start : start + rows, :] = blocks[at][:rows, :]
                    if step < RING // 2:
                        out[2 * chip + 1 - first, start : start + rows, :] = blocks[at][rows:, :]
                    at += 1
            start += rows
        if vectors:
            total = jnp.zeros((VEC_ROWS, width), f32)
            for owner in range(2 * RING):
                total += out[owner, total_rows - VEC_ROWS :, :].astype(f32)
            refs[count + 1][...] = total

    shapes = [jax.ShapeDtypeStruct((2 * RING, total_rows, width), bf16)]
    if vectors:
        shapes.append(jax.ShapeDtypeStruct((VEC_ROWS, width), f32))
    outs = pl.pallas_call(
        kernel,
        out_shape=shapes,
        in_specs=[pl.BlockSpec(memory_space=pltpu.VMEM)] * count,
        out_specs=[pl.BlockSpec(memory_space=pltpu.VMEM)] * len(shapes),
        compiler_params=pltpu.CompilerParams(vmem_limit_bytes=2 * RING * total_rows * width + 2**21),
        name="assemble",
    )(*arrays)
    return outs if vectors else outs[0]


def scatter_start(own, peer):
    return {"step": 0, "own": own, "peer": peer}


def hop_kernel(step, half, *refs):
    own_up, peer_up, own_down, peer_down = refs[:4]
    up_out, down_out = refs[-2:]
    top, bottom = slice(0, half), slice(half, None)
    local_up = lambda rows: own_up[0, rows, :].astype(f32) + peer_up[0, rows, :].astype(f32)
    local_down = lambda rows: own_down[0, rows, :].astype(f32) + peer_down[0, rows, :].astype(f32)
    if step == 1:
        up_out[...] = local_up(top).astype(bf16)
        down_out[...] = local_down(bottom).astype(bf16)
        return
    up_in, down_in = refs[4], refs[5]
    if step == 2:
        up_out[top, :] = (local_up(top) + up_in[...].astype(f32)).astype(bf16)
        up_out[bottom, :] = local_up(bottom).astype(bf16)
        down_out[top, :] = local_down(top).astype(bf16)
        down_out[bottom, :] = (local_down(bottom) + down_in[...].astype(f32)).astype(bf16)
        return
    up_out[...] = (local_up(slice(None)) + up_in[...].astype(f32)).astype(bf16)
    down_out[...] = (local_down(slice(None)) + down_in[...].astype(f32)).astype(bf16)


def scatter_step(state, held=()):
    step = state["step"]
    own, peer = state["own"], state["peer"]
    if step == 0:
        peer, held = tie(peer, held)
        return {"step": 1, "own": own, "peer": across(peer)}, held
    rows, width = own.shape[1:]
    half, far = half_of(rows), RING // 2
    at = lambda place: pl.BlockSpec((1, rows, width), lambda i: (place, 0, 0))
    whole = lambda size: pl.BlockSpec((size, width), lambda i: (0, 0))
    up_place, down_place = far + 1 - step, far - 1 + step
    before = [] if step == 1 else [state["up"], state["down"]]
    sizes = (half, rows - half) if step == 1 else (rows, rows)
    up, down = pl.pallas_call(
        functools.partial(hop_kernel, step, half),
        grid=(1,),
        in_specs=[at(up_place), at(up_place), at(down_place), at(down_place)] + [whole(b.shape[0]) for b in before],
        out_specs=[whole(size) for size in sizes],
        out_shape=[jax.ShapeDtypeStruct((size, width), bf16) for size in sizes],
        compiler_params=pltpu.CompilerParams(vmem_limit_bytes=8 * 2**20),
        name="hop",
    )(own, peer, own, peer, *before)
    up, down, held = tie(up, down, held)
    return {"step": step + 1, "own": own, "peer": peer, "up": onward(up), "down": backward(down)}, held


def scatter_sum(state, cuts):
    own, peer = state["own"], state["peer"]
    rows, width = own.shape[1:]
    shapes = [jax.ShapeDtypeStruct((count, chunks * width), f32) for _, count, chunks in cuts]

    def kernel(own_ref, peer_ref, up_ref, down_ref, *outs):
        for (first, count, chunks), out in zip(cuts, outs):
            for chunk in range(chunks):
                here = slice(first + chunk * count, first + (chunk + 1) * count)
                both = own_ref[0, here, :].astype(f32) + peer_ref[0, here, :].astype(f32)
                sent = up_ref[here, :].astype(f32) + down_ref[here, :].astype(f32)
                out[:, chunk * width : (chunk + 1) * width] = both + sent

    at = pl.BlockSpec((1, rows, width), lambda i: (0, 0, 0))
    whole = pl.BlockSpec((rows, width), lambda i: (0, 0))
    return pl.pallas_call(
        kernel,
        grid=(1,),
        in_specs=[at, at, whole, whole],
        out_specs=[pl.BlockSpec(shape.shape, lambda i: (0, 0)) for shape in shapes],
        out_shape=shapes,
        compiler_params=pltpu.CompilerParams(vmem_limit_bytes=12 * 2**20),
        name="scatter_sum",
    )(own, peer, state["up"], state["down"])


VMEM_LIMIT = 24 * 2**20
MLP_CHUNK = 32
TILE = 256
LOG2_E = 1.4426950408889634
ATTN_COST, MLP_COST = 24, 6
Q_BIAS, V_BIAS, OUT_BIAS, DOWN_BIAS, GAIN_ONE, SHIFT_ONE, GAIN_TWO, SHIFT_TWO, UP_BIAS = range(9)
NT = (((1,), (1,)), ((), ()))
TN = (((0,), (0,)), ((), ()))


def dot(first_mat, second_mat):
    return jnp.dot(first_mat, second_mat, preferred_element_type=f32)


def dot_nt(first_mat, second_mat):
    return lax.dot_general(first_mat, second_mat, NT, preferred_element_type=f32)


def dot_tn(first_mat, second_mat):
    return lax.dot_general(first_mat, second_mat, TN, preferred_element_type=f32)


def weight_part(w_ref, part):
    width = w_ref.shape[2]
    rows = width // LEAD
    return w_ref[:, part * rows : (part + 1) * rows, :].reshape(width, width)


def norm_parts(rows_in):
    average = jnp.mean(rows_in, axis=-1, keepdims=True)
    centred = rows_in - average
    inverse = lax.rsqrt(jnp.mean(centred * centred, axis=-1, keepdims=True) + eps_norm)
    return centred * inverse, inverse


def norm_back(rows_in, gain_row, grad_rows):
    unit, inverse = norm_parts(rows_in)
    scaled = grad_rows * gain_row
    mean_one = jnp.mean(scaled, axis=-1, keepdims=True)
    mean_two = jnp.mean(scaled * unit, axis=-1, keepdims=True)
    return (scaled - mean_one - unit * mean_two) * inverse, grad_rows * unit


def head_window(head, head_size, width):
    start = min(head * head_size // 128 * 128, width - 256)
    return start, head * head_size - start


def only_head(block, low, head_size):
    lane = lax.broadcasted_iota(jnp.int32, block.shape, 1)
    return jnp.where((lane >= low) & (lane < low + head_size), block, jnp.zeros_like(block))


def column_sum(rows_in):
    return jnp.sum(rows_in, axis=0, keepdims=True)


def attn_forward_kernel(
    image, heights_ref, widths_ref, x_ref, w_ref, vec_ref,
    middle_ref, second_ref, normed_ref, q_ref, k_ref, v_ref, probs_ref, attended_ref,
    vt_ref, at_ref,
):
    kept_heads = probs_ref.shape[0]
    slots, width = x_ref.shape
    head_size = width // H
    step = 64
    for at in range(0, slots, step):
        unit, _ = norm_parts(x_ref[at : at + step, :].astype(f32))
        normed_ref[at : at + step, :] = (
            unit * vec_ref[GAIN_ONE : GAIN_ONE + 1, :] + vec_ref[SHIFT_ONE : SHIFT_ONE + 1, :]
        ).astype(bf16)
    normed = normed_ref[...]
    q_ref[...] = (dot(normed, weight_part(w_ref, 0)) + vec_ref[Q_BIAS : Q_BIAS + 1, :]).astype(bf16)
    k_ref[...] = dot(normed, weight_part(w_ref, 1)).astype(bf16)
    values = dot(normed, weight_part(w_ref, 2)) + vec_ref[V_BIAS : V_BIAS + 1, :]
    v_ref[...] = values.astype(bf16)
    vt_ref[...] = values.astype(bf16).T
    slot = lax.broadcasted_iota(jnp.int32, (slots, 128), 0)
    valid = (slot // GRID < heights_ref[image]) & (slot % GRID < widths_ref[image])
    mask = jnp.where(valid, 0.0, -1e30).astype(f32)
    scale = head_size ** (-0.5)
    for head in range(H):
        start, low = head_window(head, head_size, width)
        queries = only_head(q_ref[:, start : start + 256], low, head_size)
        scores = dot_nt(k_ref[:, start : start + 256], queries)
        for at in range(0, slots, 128):
            part = scores[:, at : at + 128] * scale + mask
            exponent = jnp.exp(part - jnp.max(part, axis=0, keepdims=True))
            inverse = 1.0 / jnp.sum(exponent, axis=0, keepdims=True)
            probs_ref[head % kept_heads, :, at : at + 128] = (exponent * inverse).astype(bf16)
        here = slice(head * head_size, (head + 1) * head_size)
        at_ref[here, :] = dot(vt_ref[here, :], probs_ref[head % kept_heads])
    attended_ref[...] = at_ref[...].T.astype(bf16)
    branch = dot(attended_ref[...], weight_part(w_ref, 3))
    middle_ref[...] = x_ref[...].astype(f32) + (branch + vec_ref[OUT_BIAS : OUT_BIAS + 1, :])
    for at in range(0, slots, step):
        unit, _ = norm_parts(middle_ref[at : at + step, :])
        second_ref[at : at + step, :] = (
            unit * vec_ref[GAIN_TWO : GAIN_TWO + 1, :] + vec_ref[SHIFT_TWO : SHIFT_TWO + 1, :]
        ).astype(bf16)


def attn_forward(layer_input, attn_w, vecs, heights, widths, image, keep):
    slots, width = layer_input.shape
    wide = jax.ShapeDtypeStruct((slots, width), f32)
    low = jax.ShapeDtypeStruct((slots, width), bf16)
    probs = jax.ShapeDtypeStruct((H if keep else 4, slots, slots), bf16)
    here = pl.BlockSpec(memory_space=pltpu.VMEM)
    results = [wide, low, low, low, low, low, probs, low]
    outs = len(results) if keep else 2
    return pl.pallas_call(
        functools.partial(attn_forward_kernel, image),
        in_specs=[pl.BlockSpec(memory_space=pltpu.SMEM)] * 2 + [here] * 3,
        out_specs=[here] * outs,
        scratch_shapes=[pltpu.VMEM(r.shape, r.dtype) for r in results[outs:]]
        + [pltpu.VMEM((width, slots), bf16), pltpu.VMEM((width, slots), f32)],
        out_shape=results[:outs],
        compiler_params=pltpu.CompilerParams(vmem_limit_bytes=6 * 2**20),
        cost_estimate=pl.CostEstimate(
            flops=ATTN_COST * slots * width * width, bytes_accessed=attn_w.size * 2, transcendentals=slots * slots * H
        ),
        name="attn_forward",
    )(heights, widths, layer_input, attn_w, vecs)


def gelu_parts(pre):
    bell = jnp.exp2(pre * pre * (-0.5 * LOG2_E))
    scaled = 1.0 + jnp.abs(pre) * (0.3275911 * 0.5**0.5)
    near = pl.reciprocal(scaled, approx=True)
    near = near * (2.0 - scaled * near)
    tail = near * (0.5 * 1.061405429) - 0.5 * 1.453152027
    for coefficient in (1.421413741, -0.284496736, 0.254829592):
        tail = tail * near + 0.5 * coefficient
    tail = tail * near * bell
    return jnp.where(pre < 0.0, tail, 1.0 - tail), bell


def up_columns(w_ref, at):
    width = w_ref.shape[2]
    rows = width // LEAD
    chunk, column = at // width, at % width
    return w_ref[:, chunk * rows : (chunk + 1) * rows, column : column + TILE].reshape(width, TILE)


def mlp_up_kernel(keep_slope, pieces, *refs):
    second_refs, (w_ref, vec_ref, act_ref) = refs[:pieces], refs[pieces : pieces + 3]
    slope_ref = refs[pieces + 3] if keep_slope else None
    pre_refs = refs[-2:]
    slots, width = second_refs[0].shape
    hidden = act_ref.shape[1]

    def multiply(at):
        weight = up_columns(w_ref, at)
        for piece, second_ref in enumerate(second_refs):
            pre_refs[at // TILE % 2][piece * slots : (piece + 1) * slots, :] = dot(second_ref[...], weight)

    multiply(0)
    for at in range(0, hidden, TILE):
        if at + TILE < hidden:
            multiply(at + TILE)
        columns = slice(at, at + TILE)
        row = UP_BIAS + at // width
        bias = vec_ref[row : row + 1, at % width : at % width + TILE]
        for start in range(0, slots * pieces, MLP_CHUNK):
            here = slice(start, start + MLP_CHUNK)
            pre = pre_refs[at // TILE % 2][here, :] + bias
            below, bell = gelu_parts(pre)
            act_ref[here, columns] = (pre * below).astype(bf16)
            if keep_slope:
                slope_ref[here, columns] = (below + pre * bell * (0.5 / jnp.pi) ** 0.5).astype(bf16)


def mlp_up(second, mlp_w, vecs, keep_slope):
    slots, width = second[0].shape
    count = slots * len(second)
    hidden = mlp_w.shape[1] * LEAD // 2
    outs = 2 if keep_slope else 1
    here = pl.BlockSpec(memory_space=pltpu.VMEM)
    return pl.pallas_call(
        functools.partial(mlp_up_kernel, keep_slope, len(second)),
        in_specs=[here] * (len(second) + 2),
        out_specs=[here] * outs,
        out_shape=[jax.ShapeDtypeStruct((count, hidden), bf16)] * outs,
        scratch_shapes=[pltpu.VMEM((count, TILE), f32)] * 2,
        compiler_params=pltpu.CompilerParams(vmem_limit_bytes=6 * 2**20),
        cost_estimate=pl.CostEstimate(
            flops=MLP_COST * count * width * hidden,
            bytes_accessed=mlp_w.size + count * hidden * 4,
            transcendentals=2 * count * hidden,
        ),
        name="mlp_up",
    )(*second, mlp_w, vecs)


def mlp_down_kernel(pieces, act_ref, *refs):
    middle_refs, (w_ref, vec_ref, result_ref) = refs[:pieces], refs[pieces:]
    slots, width = middle_refs[0].shape
    hidden = act_ref.shape[1]
    bias = vec_ref[DOWN_BIAS : DOWN_BIAS + 1, :]
    for column in range(0, width, TILE):
        columns = slice(column, column + TILE)
        weight = w_ref[:, w_ref.shape[1] // 2 :, columns].reshape(hidden, TILE)
        for piece, middle_ref in enumerate(middle_refs):
            here = slice(piece * slots, (piece + 1) * slots)
            added = dot(act_ref[here, :], weight)
            result_ref[here, columns] = (added + (middle_ref[:, columns] + bias[:, columns])).astype(bf16)


def mlp_down(activated, middle, mlp_w, vecs):
    slots, width = middle[0].shape
    count = slots * len(middle)
    here = pl.BlockSpec(memory_space=pltpu.VMEM)
    return pl.pallas_call(
        functools.partial(mlp_down_kernel, len(middle)),
        in_specs=[here] * (len(middle) + 3),
        out_specs=here,
        out_shape=jax.ShapeDtypeStruct((count, width), bf16),
        compiler_params=pltpu.CompilerParams(vmem_limit_bytes=4 * 2**20),
        cost_estimate=pl.CostEstimate(
            flops=MLP_COST * count * width * activated.shape[1],
            bytes_accessed=mlp_w.size + count * width * 10,
            transcendentals=0,
        ),
        name="mlp_down",
    )(activated, *middle, mlp_w, vecs)


def mlp_backward_kernel(pieces, first, slope_ref, *refs):
    upstream_refs, middle_refs, refs = refs[:pieces], refs[pieces : 2 * pieces], refs[2 * pieces :]
    (w_ref, vec_ref), refs = refs[:2], refs[2:]
    grad_middle_refs, branch_refs, refs = refs[:pieces], refs[pieces : 2 * pieces], refs[2 * pieces :]
    grad_pre_ref, sums_ref, up_sum_ref, ga_refs = refs[0], refs[1], refs[2], refs[3:]
    slots, width = upstream_refs[0].shape
    hidden = slope_ref.shape[1]
    half = w_ref.shape[1] // 2

    step = LEAD // 4 * half

    def multiply(at):
        weight = w_ref[at // half : (at + step) // half, half:, :].reshape(step, width)
        for piece, upstream_ref in enumerate(upstream_refs):
            ga_refs[at // step % 2][piece * slots : (piece + 1) * slots, :] = dot_nt(upstream_ref[...], weight)

    multiply(0)
    for at in range(0, hidden, step):
        if at + step < hidden:
            multiply(at + step)
        sums = jnp.zeros((1, step), f32)
        for start in range(0, slots * pieces, MLP_CHUNK):
            here = slice(start, start + MLP_CHUNK)
            slope = slope_ref[first * slots + start : first * slots + start + MLP_CHUNK, at : at + step]
            pre = (ga_refs[at // step % 2][here, :] * slope.astype(f32)).astype(bf16)
            grad_pre_ref[here, at : at + step] = pre
            sums += column_sum(pre.astype(f32))
        up_sum_ref[at // width, :, at % width : at % width + step] = sums
    gain = vec_ref[GAIN_TWO : GAIN_TWO + 1, :]
    sums = [jnp.zeros((1, width), f32)] * 3
    for piece in range(pieces):
        rows = slice(piece * slots, (piece + 1) * slots)
        total = None
        for chunk in range(hidden // width):
            weight = w_ref[:, chunk * width // LEAD : (chunk + 1) * width // LEAD, :].reshape(width, width)
            added = dot_nt(grad_pre_ref[rows, chunk * width : (chunk + 1) * width], weight)
            total = added if total is None else total + added
        ga_refs[piece % 2][:slots, :] = total
        for at in range(0, slots, MLP_CHUNK):
            here = slice(at, at + MLP_CHUNK)
            upstream = upstream_refs[piece][here, :].astype(f32)
            grad = ga_refs[piece % 2][here, :]
            grad_mid, gain_terms = norm_back(middle_refs[piece][here, :], gain, grad)
            whole = upstream + grad_mid
            grad_middle_refs[piece][here, :] = whole
            branch_refs[piece][here, :] = whole.astype(bf16)
            sums = [old + column_sum(new) for old, new in zip(sums, (upstream, gain_terms, grad))]
    for row, value in enumerate(sums):
        sums_ref[row : row + 1, :] = value


def mlp_backward(upstream, slope, middle, mlp_w, vecs, image=0):
    slots, width = middle[0].shape
    pieces = len(middle)
    count = slots * pieces
    parts = mlp_w.shape[1] * LEAD // (2 * width)
    here = pl.BlockSpec(memory_space=pltpu.VMEM)
    outs = pl.pallas_call(
        functools.partial(mlp_backward_kernel, pieces, image),
        in_specs=[here] * (2 * pieces + 3),
        out_specs=[here] * (2 * pieces + 3),
        out_shape=[jax.ShapeDtypeStruct((slots, width), f32)] * pieces
        + [jax.ShapeDtypeStruct((slots, width), bf16)] * pieces
        + [
            jax.ShapeDtypeStruct((count, width * parts), bf16),
            jax.ShapeDtypeStruct((8, width), f32),
            jax.ShapeDtypeStruct((parts, 1, width), f32),
        ],
        scratch_shapes=[pltpu.VMEM((count, width), f32)] * 2,
        compiler_params=pltpu.CompilerParams(vmem_limit_bytes=8 * 2**20),
        cost_estimate=pl.CostEstimate(
            flops=2 * MLP_COST * count * width * width * parts,
            bytes_accessed=mlp_w.size * 2 + count * width * (10 + 4 * parts),
            transcendentals=0,
        ),
        name="mlp_backward",
    )(slope, *upstream, *middle, mlp_w, vecs)
    return outs[:pieces], outs[pieces : 2 * pieces], *outs[2 * pieces :]


def attn_backward_kernel(
    grad_middle_ref, branch_ref, x_ref, q_ref, k_ref, v_ref, probs_ref, w_ref, vec_ref,
    grad_in_ref, grad_low_ref, gq_ref, gk_ref, gv_ref, sums_ref,
    ga_ref, gat_ref, qt_ref, kt_ref, gqt_ref, gkt_ref, gvt_ref,
):
    slots, width = x_ref.shape
    head_size = width // H
    scale = head_size ** (-0.5)
    ga = dot_nt(branch_ref[...], weight_part(w_ref, 3)).astype(bf16)
    ga_ref[...] = ga
    gat_ref[...] = ga.T
    qt_ref[...] = q_ref[...].T
    kt_ref[...] = k_ref[...].T
    for head in range(H):
        start, low = head_window(head, head_size, width)
        here = slice(head * head_size, (head + 1) * head_size)
        own = only_head(ga_ref[:, start : start + 256], low, head_size)
        grad_probs = dot_nt(v_ref[:, start : start + 256], own)
        pieces = []
        for at in range(0, slots, 128):
            probs = probs_ref[head, :, at : at + 128].astype(f32)
            grad = grad_probs[:, at : at + 128]
            total = jnp.sum(probs * grad, axis=0, keepdims=True)
            pieces.append((probs * (grad - total)).astype(bf16))
        grad_scores = jnp.concatenate(pieces, axis=1)
        gvt_ref[here, :] = dot_nt(gat_ref[here, :], probs_ref[head])
        gqt_ref[here, :] = dot(kt_ref[here, :], grad_scores) * scale
        gkt_ref[here, :] = dot_nt(qt_ref[here, :], grad_scores) * scale
    gq_ref[...] = gqt_ref[...].T.astype(bf16)
    gk_ref[...] = gkt_ref[...].T.astype(bf16)
    gv_ref[...] = gvt_ref[...].T.astype(bf16)
    grad_normed = dot_nt(gq_ref[...], weight_part(w_ref, 0))
    grad_normed += dot_nt(gk_ref[...], weight_part(w_ref, 1))
    grad_normed += dot_nt(gv_ref[...], weight_part(w_ref, 2))
    grad_in_ref[...] = grad_normed
    gain = vec_ref[GAIN_ONE : GAIN_ONE + 1, :]
    sums = [jnp.zeros((1, width), f32)] * 5
    for at in range(0, slots, MLP_CHUNK):
        rows = slice(at, at + MLP_CHUNK)
        grad = grad_in_ref[rows, :]
        grad_norm, gain_terms = norm_back(x_ref[rows, :].astype(f32), gain, grad)
        total = grad_middle_ref[rows, :] + grad_norm
        grad_in_ref[rows, :] = total
        grad_low_ref[rows, :] = total.astype(bf16)
        terms = (
            gq_ref[rows, :].astype(f32), gv_ref[rows, :].astype(f32), branch_ref[rows, :].astype(f32),
            gain_terms, grad,
        )
        sums = [old + column_sum(new) for old, new in zip(sums, terms)]

    for row, value in enumerate(sums):
        sums_ref[row : row + 1, :] = value


def attn_backward(grad_middle, branch, layer_input, saved, attn_w, vecs):
    queries, key_rows, values, probs = saved
    slots, width = layer_input.shape
    low = jax.ShapeDtypeStruct((slots, width), bf16)
    here = pl.BlockSpec(memory_space=pltpu.VMEM)
    flipped = pltpu.VMEM((width, slots), bf16)
    flipped_wide = pltpu.VMEM((width, slots), f32)
    return pl.pallas_call(
        attn_backward_kernel,
        in_specs=[here] * 9,
        out_specs=[here] * 6,
        out_shape=[jax.ShapeDtypeStruct((slots, width), f32)] + [low] * 4 + [jax.ShapeDtypeStruct((8, width), f32)],
        scratch_shapes=[pltpu.VMEM((slots, width), bf16)] + [flipped] * 3 + [flipped_wide] * 3,
        compiler_params=pltpu.CompilerParams(vmem_limit_bytes=8 * 2**20),
        cost_estimate=pl.CostEstimate(
            flops=ATTN_COST * slots * width * width, bytes_accessed=attn_w.size * 2, transcendentals=0
        ),
        name="attn_backward",
    )(grad_middle, branch, layer_input, queries, key_rows, values, probs, attn_w, vecs)


def ring_slot(owner, me):
    there, here = place_of(lax.div(owner, 2)), place_of(lax.div(me, 2))
    return lax.rem(there - here + RING, RING)


def store_block(own_ref, peer_ref, owner, core, rows, value):
    me = lax.axis_index("dp")
    slot = ring_slot(owner, me)

    @pl.when(lax.rem(me, 2) == core)
    def _():
        own_ref[slot, rows, :] = value

    @pl.when(lax.rem(me, 2) != core)
    def _():
        peer_ref[slot, rows, :] = value


def scatter_shapes(rows, width):
    return [jax.ShapeDtypeStruct((RING, rows, width), bf16)] * 2


def joined(refs, scratch_ref):
    slots = refs[0].shape[0]
    for piece, ref in enumerate(refs):
        scratch_ref[piece * slots : (piece + 1) * slots, :] = ref[...]


def flipped(refs, scratch_ref):
    slots = refs[0].shape[0]
    for piece, ref in enumerate(refs):
        scratch_ref[:, piece * slots : (piece + 1) * slots] = ref[...].T


def grad_down_kernel(pieces, act_ref, *refs):
    upstream_refs, (own_ref, peer_ref, right_ref) = refs[:pieces], refs[pieces:]
    index = pl.program_id(0)
    rows = own_ref.shape[1]

    @pl.when(index == 0)
    def _():
        joined(upstream_refs, right_ref)

    value = dot_tn(act_ref[...], right_ref[...]).astype(bf16)
    for at in range(value.shape[0] // rows):
        owner = index * (value.shape[0] // rows) + at
        store_block(own_ref, peer_ref, owner, at % 2, slice(None), value[at * rows : (at + 1) * rows])


def grad_down_blocks(activated, upstream):
    slots, width = upstream[0].shape
    count, hidden = activated.shape
    parts = hidden // width
    rows = hidden // LEAD
    return pl.pallas_call(
        functools.partial(grad_down_kernel, len(upstream)),
        grid=(parts,),
        in_specs=[pl.BlockSpec((count, width), lambda j: (0, j))]
        + [pl.BlockSpec((slots, width), lambda j: (0, 0))] * len(upstream),
        out_specs=[pl.BlockSpec((RING, rows, width), lambda j: (0, 0, 0))] * 2,
        out_shape=scatter_shapes(rows, width),
        scratch_shapes=[pltpu.VMEM((count, width), bf16)],
        compiler_params=pltpu.CompilerParams(vmem_limit_bytes=18 * 2**20),
        cost_estimate=pl.CostEstimate(
            flops=MLP_COST * count * width * hidden, bytes_accessed=count * hidden * 2 + hidden * width * 2, transcendentals=0
        ),
        name="grad_down",
    )(activated, *upstream)


def grad_up_kernel(pieces, *refs):
    pre_refs, second_refs, attended_refs, branch_refs, (own_ref, peer_ref, left_ref, right_ref) = (
        *(refs[at * pieces : (at + 1) * pieces] for at in range(4)), refs[4 * pieces :]
    )
    index = pl.program_id(0)
    rows = second_refs[0].shape[1] // LEAD

    @pl.when(index == 0)
    def _():
        flipped(second_refs, left_ref)

    joined(pre_refs, right_ref)
    value = dot(left_ref[...], right_ref[...]).astype(bf16)
    for owner in range(LEAD):
        here = pl.ds(pl.multiple_of(index * rows, rows), rows)
        store_block(own_ref, peer_ref, owner, owner % 2, here, value[owner * rows : (owner + 1) * rows])

    @pl.when(index == pl.num_programs(0) - 1)
    def _():
        flipped(attended_refs, left_ref)
        joined(branch_refs, right_ref)
        last = dot(left_ref[...], right_ref[...]).astype(bf16)
        for owner in range(LEAD):
            here = pl.ds(own_ref.shape[1] - rows, rows)
            store_block(own_ref, peer_ref, owner, owner % 2, here, last[owner * rows : (owner + 1) * rows])


def grad_up_blocks(second, grad_pre, attended, branch):
    slots, width = second[0].shape
    count, hidden = slots * len(second), grad_pre[0].shape[1]
    parts = hidden // width
    rows = (hidden + width) // LEAD
    whole = [pl.BlockSpec((slots, width), lambda j: (0, 0))] * len(second)
    return pl.pallas_call(
        functools.partial(grad_up_kernel, len(second)),
        grid=(parts,),
        in_specs=[pl.BlockSpec((slots, width), lambda j: (0, j))] * len(second) + whole * 3,
        out_specs=[pl.BlockSpec((RING, rows, width), lambda j: (0, 0, 0))] * 2,
        out_shape=scatter_shapes(rows, width),
        scratch_shapes=[pltpu.VMEM((width, count), bf16), pltpu.VMEM((count, width), bf16)],
        compiler_params=pltpu.CompilerParams(vmem_limit_bytes=24 * 2**20),
        cost_estimate=pl.CostEstimate(
            flops=MLP_COST * count * width * hidden, bytes_accessed=count * hidden * 2 + hidden * width * 2, transcendentals=0
        ),
        name="grad_up",
    )(*grad_pre, *second, *attended, *branch)


def grad_qkv_kernel(pieces, *refs):
    left_refs, rights = refs[:pieces], refs[pieces : 4 * pieces]
    attn_sums, mlp_sums, up_sums = (refs[at * pieces : (at + 1) * pieces] for at in (4, 5, 6))
    own_ref, peer_ref, left_ref, right_ref, vec_ref = refs[7 * pieces :]
    width = left_refs[0].shape[1]
    rows = width // LEAD
    flipped(left_refs, left_ref)
    for part in range(3):
        joined(rights[part * pieces : (part + 1) * pieces], right_ref)
        value = dot(left_ref[...], right_ref[...]).astype(bf16)
        for owner in range(LEAD):
            here = slice(part * rows, (part + 1) * rows)
            store_block(own_ref, peer_ref, owner, owner % 2, here, value[owner * rows : (owner + 1) * rows])
    vec_ref[...] = jnp.zeros_like(vec_ref)
    for name, refs_of, row in (
        (Q_BIAS, attn_sums, 0), (V_BIAS, attn_sums, 1), (OUT_BIAS, attn_sums, 2), (DOWN_BIAS, mlp_sums, 0),
        (GAIN_ONE, attn_sums, 3), (SHIFT_ONE, attn_sums, 4), (GAIN_TWO, mlp_sums, 1), (SHIFT_TWO, mlp_sums, 2),
    ):
        vec_ref[name : name + 1, :] = sum(ref[row : row + 1, :] for ref in refs_of)
    for part in range(up_sums[0].shape[0]):
        vec_ref[UP_BIAS + part : UP_BIAS + part + 1, :] = sum(ref[part] for ref in up_sums)
    vectors = vec_ref[...].astype(bf16)
    here = slice(3 * rows, 3 * rows + VEC_ROWS)
    for slot in range(RING):
        own_ref[slot, here, :] = vectors
        peer_ref[slot, here, :] = vectors


def grad_qkv_blocks(normed, rights, attn_sums, mlp_sums, up_sums):
    slots, width = normed[0].shape
    count = slots * len(normed)
    arrays = [*normed, *(piece for right in rights for piece in right), *attn_sums, *mlp_sums, *up_sums]
    rows = 3 * width // LEAD + VEC_ROWS
    return pl.pallas_call(
        functools.partial(grad_qkv_kernel, len(normed)),
        in_specs=[pl.BlockSpec(memory_space=pltpu.VMEM)] * len(arrays),
        out_specs=[pl.BlockSpec(memory_space=pltpu.VMEM)] * 2,
        out_shape=scatter_shapes(rows, width),
        scratch_shapes=[
            pltpu.VMEM((width, count), bf16), pltpu.VMEM((count, width), bf16), pltpu.VMEM((VEC_ROWS, width), f32)
        ],
        compiler_params=pltpu.CompilerParams(vmem_limit_bytes=6 * 2**20),
        cost_estimate=pl.CostEstimate(
            flops=3 * MLP_COST * count * width * width, bytes_accessed=len(arrays) * slots * width * 2, transcendentals=0
        ),
        name="grad_qkv",
    )(*arrays)


VECS = ("q_bias", "v_bias", "out_bias", "down_bias", "gain_one", "shift_one", "gain_two", "shift_two")


def solution(mesh):
    dp_size = mesh.shape["dp"]
    ringed = dp_size == 2 * RING

    def gathered_whole(qkv, out, up, down, vectors):
        width = out.shape[1]
        gathered = [lax.all_gather(w, "dp", axis=0, tiled=True) for w in (qkv, out, up, down)]
        blocked = [w.reshape(LEAD, -1, w.shape[1]) for w in gathered]
        fold = lambda w: w.reshape(LEAD, w.shape[1], -1, width).transpose(0, 2, 1, 3).reshape(LEAD, -1, width)
        first = jnp.concatenate([fold(blocked[0]), blocked[1], jnp.zeros((LEAD, VEC_ROWS, width), bf16)], 1)
        whole = lambda name: lax.all_gather(vectors[name], "dp", axis=0, tiled=True)
        vecs = jnp.concatenate([jnp.stack([whole(name) for name in VECS]), whole("up_bias").reshape(-1, width)])
        vecs = jnp.pad(vecs.astype(f32), ((0, VEC_ROWS - vecs.shape[0]), (0, 0)))
        return first, jnp.concatenate([fold(blocked[2]), blocked[3]], 1), vecs

    def own_vectors(block):
        me = lax.axis_index("dp")
        width = block.shape[1]
        rows = width // LEAD
        small = lax.dynamic_slice(block, (0, me * rows), (len(VECS), rows))
        parts = (3 * LEAD + LEAD) * rows // width
        size = parts * rows
        in_row = width // size
        own = {name: small[at] for at, name in enumerate(VECS)}
        own["up_bias"] = lax.dynamic_slice(block, (len(VECS) + me // in_row, me % in_row * size), (1, size))[0]
        return own

    def shards(
        tokens, cotangent, heights, widths, qkv_weight, out_weight, up_weight, down_weight,
        q_bias, v_bias, out_bias, up_bias, down_bias, gain_one, shift_one, gain_two, shift_two,
    ):
        leading = lax.axis_index("section") == 0
        width = tokens.shape[1]
        images = heights.shape[0]
        each = range(images)
        rows = width // LEAD
        cut = lambda array: jnp.split(array, images)
        vectors = dict(
            q_bias=q_bias[0], v_bias=v_bias[0], out_bias=out_bias[0], up_bias=up_bias[0], down_bias=down_bias[0],
            gain_one=gain_one[0], shift_one=shift_one[0], gain_two=gain_two[0], shift_two=shift_two[0],
        )
        inputs, cotangents = cut(tokens), cut(cotangent)

        attention = lambda x, image, keep: attn_forward(x, attn_w, vecs, heights, widths, image, keep)
        if ringed:
            small = jnp.stack([vectors[name] for name in VECS])
            one, two = pack_first(qkv_weight[0], out_weight[0], small, vectors["up_bias"][None])
            g, h = gather_start(one), gather_start(two)
            u, d = gather_start(pack_columns(up_weight[0], width)), gather_start(down_weight[0])
            for _ in range(RING // 2 - 1):
                g, h = gather_step(g), gather_step(h)
            g["mine"], u["mine"] = tie(g["mine"], u["mine"])
            h["mine"], d["mine"] = tie(h["mine"], d["mine"])
            g, h, u, d = (gather_step(state) for state in (g, h, u, d))
            attn_w, vecs = assemble([g, h], True)
            front = [attention(inputs[0], 0, False)]
            attn_w, front, u["mine"], d["mine"] = tie(attn_w, front, u["mine"], d["mine"])
            u, d = gather_step(u), gather_step(d)
            front += [attention(inputs[image], image, False) for image in each[1:]]
            front, u["mine"], d["mine"] = tie(front, u["mine"], d["mine"])
            for _ in range(u["step"], RING // 2):
                u, d = gather_step(u), gather_step(d)
            mlp_w = assemble([u, d])
        else:
            attn_w, mlp_w, vecs = gathered_whole(
                qkv_weight[0], out_weight[0], up_weight[0], down_weight[0], vectors
            )
            front = [attention(inputs[image], image, False) for image in each]
        received = []
        for image in each:
            (activated,) = mlp_up(front[image][1:], mlp_w, vecs, False)
            sent = mlp_down(activated, front[image][:1], mlp_w, vecs)
            front, sent = tie(front, sent)
            received.append(lax.ppermute(sent, "section", [(0, 1)]))

        layer_input, kept = [], []
        for image in each:
            layer_input.append(jnp.where(leading, inputs[image], received[image]))
            kept.append(attention(layer_input[image], image, True))
            kept, received = tie(kept, received)
        middle, second, normed, queries, key_rows, values, probs, attended = zip(*kept)
        activated, slope = mlp_up(second, mlp_w, vecs, True)

        back_attn = lambda grad, branch, image: attn_backward(
            grad[image], branch[image], layer_input[image],
            (queries[image], key_rows[image], values[image], probs[image]), attn_w, vecs,
        )
        grad_middle, branch = mlp_backward(cotangents, slope, middle, mlp_w, vecs)[:2]
        arriving = []
        for image in each:
            to_send = back_attn(grad_middle, branch, image)[1]
            grad_middle, branch, activated, to_send = tie(grad_middle, branch, activated, to_send)
            arriving.append(lax.ppermute(to_send, "section", [(1, 0)]))
        upstream, back = [], []

        def back_one(image):
            upstream.append(jnp.where(leading, arriving[image], cotangents[image]))
            back.append(mlp_backward(upstream[image:], slope, middle[image : image + 1], mlp_w, vecs, image))

        back_one(0)
        back, arriving, activated = tie(back, arriving, activated)
        result = mlp_down(activated, middle, mlp_w, vecs)
        result, arriving, activated = tie(result, arriving, activated)
        if ringed:
            rest = [jnp.where(leading, arriving[image], cotangents[image]) for image in each[1:]]
            d = scatter_start(*grad_down_blocks(activated, upstream + rest))
            d, arriving = scatter_step(d, arriving)
            for image in each[1:]:
                back_one(image)
            d, back = tie(d, back)
            d, back = scatter_step(d, back)
            grad_middle, branch, grad_pre, mlp_sums, up_sums = zip(*back)
            grad_middle, branch = [g for (g,) in grad_middle], [g for (g,) in branch]
            u = scatter_start(*grad_up_blocks(second, grad_pre, attended, branch))
            d, u = tie(d, u)
            held = (grad_middle, branch)
            attn_back = []
            for image in each:
                if image < 2:
                    d, held = scatter_step(d, held)
                    u, held = scatter_step(u, held)
                attn_back.append(back_attn(*held, image))
                d, u, attn_back, held = tie(d, u, attn_back, held)
            d, attn_back = scatter_step(d, attn_back)
            u, attn_back = scatter_step(u, attn_back)
        else:
            for image in each[1:]:
                back_one(image)
            grad_middle, branch, grad_pre, mlp_sums, up_sums = zip(*back)
            grad_middle, branch = [g for (g,) in grad_middle], [g for (g,) in branch]
            attn_back = [back_attn(grad_middle, branch, image) for image in each]
        grad_input, _, gq, gk, gv, attn_sums = zip(*attn_back)
        if ringed:
            q = scatter_start(*grad_qkv_blocks(normed, (gq, gk, gv), attn_sums, mlp_sums, up_sums))
            parts = mlp_w.shape[1] // rows - 4
            ends = RING // 2 + 1
            q = scatter_step(scatter_step(q)[0])[0]
            d, q = tie(d, q)
            while min(d["step"], u["step"], q["step"]) < ends:
                d, u, q = (state if state["step"] == ends else scatter_step(state)[0] for state in (d, u, q))
            (g_down,) = scatter_sum(d, [(0, d["own"].shape[1], 1)])
            g_up, g_out = scatter_sum(u, [(0, rows, parts), (parts * rows, rows, 1)])
            g_qkv, vec_sums = scatter_sum(q, [(0, rows, 3), (3 * rows, VEC_ROWS, 1)])
            g_vecs = own_vectors(vec_sums)
        else:
            attn_sums = sum(attn_sums)
            sums = dict(zip(("q_bias", "v_bias", "out_bias", "gain_one", "shift_one"), attn_sums))
            sums |= dict(zip(("down_bias", "gain_two", "shift_two"), sum(mlp_sums)))
            sums["up_bias"] = sum(up_sums).reshape(-1)
            scatter = lambda a: lax.psum_scatter(a, "dp", scatter_dimension=0, tiled=True)
            whole = lambda pieces: jnp.concatenate(pieces)
            outer = lambda a, b: lax.dot_general(a, b, TN, preferred_element_type=f32)
            g_down = scatter(outer(activated, whole(upstream)))
            g_up = scatter(outer(whole(second), whole(grad_pre)))
            g_qkv = scatter(jnp.concatenate([outer(whole(normed), whole(part)) for part in (gq, gk, gv)], 1))
            g_out = scatter(outer(whole(attended), whole(branch)))
            g_vecs = {name: scatter(value) for name, value in sums.items()}
        return (
            result[None], jnp.concatenate(grad_input)[None],
            g_qkv[None], g_out[None], g_up[None], g_down[None],
            *(
                g_vecs[name][None]
                for name in (
                    "q_bias", "v_bias", "out_bias", "up_bias", "down_bias",
                    "gain_one", "shift_one", "gain_two", "shift_two",
                )
            ),
        )

    rows_spec = P("dp", None)
    three, two = P("section", "dp", None), P("section", "dp")
    return jax.shard_map(
        shards,
        mesh=mesh,
        in_specs=(rows_spec, rows_spec, P("dp"), P("dp")) + (three,) * 4 + (two,) * 9,
        out_specs=(three,) * 6 + (two,) * 9,
        check_vma=False,
    )
```

```python
import functools

import jax
import jax.numpy as jnp
from jax import lax
from jax.experimental import pallas as pl
from jax.experimental.pallas import tpu as pltpu
from jax.sharding import PartitionSpec as P

H = 16
GRID = 16
LEAD = 16
RING = 8
VEC_ROWS = 16

f32 = jnp.float32
bf16 = jnp.bfloat16
eps_norm = 1e-05


def chip_at(place):
    if isinstance(place, int):
        return 2 * place if place < 4 else 2 * (7 - place) + 1
    return jnp.where(place < 4, 2 * place, 2 * (7 - place) + 1)


def place_of(chip):
    if isinstance(chip, int):
        return chip // 2 if chip % 2 == 0 else 7 - chip // 2
    return jnp.where(chip % 2 == 0, chip // 2, 7 - chip // 2)


def ring_route(step):
    return [
        (2 * chip_at(place) + core, 2 * chip_at((place + step) % RING) + core)
        for place in range(RING)
        for core in range(2)
    ]


CORE_ROUTE = [(index, index ^ 1) for index in range(2 * RING)]


def onward(block):
    return lax.ppermute(block, "dp", ring_route(1))


def backward(block):
    return lax.ppermute(block, "dp", ring_route(-1))


def across(block):
    return lax.ppermute(block, "dp", CORE_ROUTE)


def around(block):
    route = [(2 * chip_at(p) + core, 2 * chip_at((p + (-1) ** core) % RING) + core) for p in range(RING) for core in (0, 1)]
    return lax.ppermute(block, "dp", route)


def tie(*values):
    leaves, tree = jax.tree.flatten(values)
    arrays = iter(lax.optimization_barrier([leaf for leaf in leaves if isinstance(leaf, jax.Array)]))
    held = jax.tree.unflatten(tree, [next(arrays) if isinstance(leaf, jax.Array) else leaf for leaf in leaves])
    return held if len(held) > 1 else held[0]


def pack_first(qkv, out, vectors, ups):
    rows, width = out.shape
    chunks = qkv.shape[1] // width
    names, size = vectors.shape[0], ups.shape[1]

    def kernel(qkv_ref, out_ref, vec_ref, up_ref, one_ref, two_ref):
        me = lax.axis_index("dp")
        for chunk in range(chunks):
            packed_ref, at = (one_ref, chunk) if chunk < 2 else (two_ref, chunk - 2)
            packed_ref[at * rows : (at + 1) * rows, :] = qkv_ref[:, chunk * width : (chunk + 1) * width]
        two_ref[(chunks - 2) * rows : (chunks - 1) * rows, :] = out_ref[...]
        lane = lax.broadcasted_iota(jnp.int32, (names, width), 1)
        spread = jnp.concatenate([vec_ref[...].astype(f32)] * (width // rows), axis=1)
        small = jnp.where((lane >= me * rows) & (lane < (me + 1) * rows), spread, 0.0)
        lane = lax.broadcasted_iota(jnp.int32, (VEC_ROWS - names, width), 1)
        row = lax.broadcasted_iota(jnp.int32, (VEC_ROWS - names, width), 0)
        spread = jnp.concatenate([up_ref[...].astype(f32)] * (width // size), axis=1)
        at = row * width + lane
        last = jnp.where((at >= me * size) & (at < (me + 1) * size), spread, 0.0)
        two_ref[(chunks - 1) * rows :, :] = jnp.concatenate([small, last], axis=0).astype(bf16)

    return pl.pallas_call(
        kernel,
        out_shape=[
            jax.ShapeDtypeStruct((2 * rows, width), bf16),
            jax.ShapeDtypeStruct(((chunks - 1) * rows + VEC_ROWS, width), bf16),
        ],
        compiler_params=pltpu.CompilerParams(vmem_limit_bytes=4 * 2**20),
        name="pack_first",
    )(qkv, out, vectors, ups)


def pack_columns(weight, width):
    rows, columns = weight.shape
    chunks = columns // width

    def kernel(weight_ref, packed_ref):
        for chunk in range(chunks):
            packed_ref[chunk * rows : (chunk + 1) * rows, :] = weight_ref[:, chunk * width : (chunk + 1) * width]

    return pl.pallas_call(
        kernel,
        out_shape=jax.ShapeDtypeStruct((chunks * rows, width), bf16),
        compiler_params=pltpu.CompilerParams(vmem_limit_bytes=4 * 2**20),
        name="pack_columns",
    )(weight)


def half_of(rows):
    return rows // 32 * 16


def gather_start(shard):
    return {"step": 0, "rows": shard.shape[0], "mine": [jnp.concatenate([shard, across(shard)])], "theirs": []}


def gather_step(state):
    step, rows = state["step"] + 1, state["rows"]
    mine, theirs = list(state["mine"]), list(state["theirs"])
    if step > 2:
        mine[-1], theirs[-2] = tie(mine[-1], theirs[-2])
    came = around(mine[-1] if step < RING // 2 else mine[-1][:rows])
    return {"step": step, "rows": rows, "mine": [*mine, came], "theirs": [*theirs, across(came)]}


def assemble(states, vectors=False):
    width = states[0]["mine"][0].shape[1]
    arrays = [array for state in states for array in state["mine"] + state["theirs"]]
    count = len(arrays)
    total_rows = sum(state["rows"] for state in states)

    def kernel(*refs):
        blocks, out = refs[:count], refs[count]
        me = lax.axis_index("dp")
        core, place = lax.rem(me, 2), place_of(lax.div(me, 2))
        way = 1 - 2 * core
        at, start = 0, 0
        for state in states:
            rows = state["rows"]
            for steps, own_first in ((range(RING // 2 + 1), 1), (range(1, RING // 2 + 1), 0)):
                for step in steps:
                    toward = step * way if not own_first else -step * way
                    chip = chip_at(lax.rem(place + toward + RING, RING))
                    first = core if own_first else 1 - core
                    out[2 * chip + first, start : start + rows, :] = blocks[at][:rows, :]
                    if step < RING // 2:
                        out[2 * chip + 1 - first, start : start + rows, :] = blocks[at][rows:, :]
                    at += 1
            start += rows
        if vectors:
            total = jnp.zeros((VEC_ROWS, width), f32)
            for owner in range(2 * RING):
                total += out[owner, total_rows - VEC_ROWS :, :].astype(f32)
            refs[count + 1][...] = total

    shapes = [jax.ShapeDtypeStruct((2 * RING, total_rows, width), bf16)]
    if vectors:
        shapes.append(jax.ShapeDtypeStruct((VEC_ROWS, width), f32))
    outs = pl.pallas_call(
        kernel,
        out_shape=shapes,
        in_specs=[pl.BlockSpec(memory_space=pltpu.VMEM)] * count,
        out_specs=[pl.BlockSpec(memory_space=pltpu.VMEM)] * len(shapes),
        compiler_params=pltpu.CompilerParams(vmem_limit_bytes=2 * RING * total_rows * width + 2**21),
        name="assemble",
    )(*arrays)
    return outs if vectors else outs[0]


def scatter_start(own, peer=None):
    return {"step": 1 if peer is None else 0, "own": own, "peer": peer}


def hop_kernel(step, half, both, *refs):
    count = 2 if both else 1
    last = step == RING // 2
    ups, downs, befores = refs[:count], refs[count : 2 * count], refs[2 * count : -2]
    up_out, down_out = refs[-2:]
    if last:
        homes, befores, local_out = befores[:count], befores[count : count + 2], refs[-1]
        up_out, down_out = refs[-3:-1]
    top, bottom = slice(0, half), slice(half, None)

    def local(blocks, rows):
        return sum(block[0, rows, :].astype(f32) for block in blocks)

    if step == 1:
        up_out[...] = local(ups, top).astype(bf16)
        down_out[...] = local(downs, bottom).astype(bf16)
        return
    up_in, down_in = befores
    if step == 2:
        up_out[top, :] = (local(ups, top) + up_in[...].astype(f32)).astype(bf16)
        up_out[bottom, :] = local(ups, bottom).astype(bf16)
        down_out[top, :] = local(downs, top).astype(bf16)
        down_out[bottom, :] = (local(downs, bottom) + down_in[...].astype(f32)).astype(bf16)
        return
    up_out[...] = (local(ups, slice(None)) + up_in[...].astype(f32)).astype(bf16)
    down_out[...] = (local(downs, slice(None)) + down_in[...].astype(f32)).astype(bf16)
    if last:
        local_out[...] = local(homes, slice(None))


def scatter_step(state, held=()):
    step = state["step"]
    own, peer = state["own"], state["peer"]
    if step == 0:
        peer, held = tie(peer, held)
        return {"step": 1, "own": own, "peer": across(peer)}, held
    rows, width = own.shape[1:]
    half, far = half_of(rows), RING // 2
    at = lambda place: pl.BlockSpec((1, rows, width), lambda i: (place, 0, 0))
    whole = lambda size: pl.BlockSpec((size, width), lambda i: (0, 0))
    up_place, down_place = far + 1 - step, far - 1 + step
    before = [] if step == 1 else [state["up"], state["down"]]
    sizes = (half, rows - half) if step == 1 else (rows, rows)
    both = [own] if peer is None else [own, peer]
    places = [up_place, down_place]
    shapes = [jax.ShapeDtypeStruct((size, width), bf16) for size in sizes]
    if step == far:
        places.append(0)
        shapes.append(jax.ShapeDtypeStruct((rows, width), f32))
    outs = pl.pallas_call(
        functools.partial(hop_kernel, step, half, peer is not None),
        grid=(1,),
        in_specs=[at(place) for place in places for _ in both] + [whole(b.shape[0]) for b in before],
        out_specs=[whole(shape.shape[0]) for shape in shapes],
        out_shape=shapes,
        compiler_params=pltpu.CompilerParams(vmem_limit_bytes=8 * 2**20),
        name="hop",
    )(*both * len(places), *before)
    up, down, held = tie(*outs[:2], held)
    state = {"step": step + 1, "own": own, "peer": peer, "up": onward(up), "down": backward(down)}
    if step == far:
        state["local"] = outs[2]
    return state, held


def scatter_sum(state, cuts):
    rows, width = state["local"].shape
    shapes = [jax.ShapeDtypeStruct((count, chunks * width), f32) for _, count, chunks in cuts]

    def kernel(local_ref, up_ref, down_ref, *outs):
        for (first, count, chunks), out in zip(cuts, outs):
            for chunk in range(chunks):
                here = slice(first + chunk * count, first + (chunk + 1) * count)
                sent = up_ref[here, :].astype(f32) + down_ref[here, :].astype(f32)
                out[:, chunk * width : (chunk + 1) * width] = local_ref[here, :] + sent

    here = pl.BlockSpec(memory_space=pltpu.VMEM)
    return pl.pallas_call(
        kernel,
        in_specs=[here] * 3,
        out_specs=[here] * len(shapes),
        out_shape=shapes,
        compiler_params=pltpu.CompilerParams(vmem_limit_bytes=12 * 2**20),
        cost_estimate=pl.CostEstimate(flops=rows * width * 2000, bytes_accessed=rows * width * 10, transcendentals=0),
        name="scatter_sum",
    )(state["local"], state["up"], state["down"])


VMEM_LIMIT = 24 * 2**20
MLP_CHUNK = 32
TILE = 256
LOG2_E = 1.4426950408889634
ATTN_COST, MLP_COST = 24, 6
Q_BIAS, V_BIAS, OUT_BIAS, DOWN_BIAS, GAIN_ONE, SHIFT_ONE, GAIN_TWO, SHIFT_TWO, UP_BIAS = range(9)
NT = (((1,), (1,)), ((), ()))
TN = (((0,), (0,)), ((), ()))


def dot(first_mat, second_mat):
    return jnp.dot(first_mat, second_mat, preferred_element_type=f32)


def dot_nt(first_mat, second_mat):
    return lax.dot_general(first_mat, second_mat, NT, preferred_element_type=f32)


def dot_tn(first_mat, second_mat):
    return lax.dot_general(first_mat, second_mat, TN, preferred_element_type=f32)


def weight_part(w_ref, part):
    width = w_ref.shape[2]
    rows = width // LEAD
    return w_ref[:, part * rows : (part + 1) * rows, :].reshape(width, width)


def norm_parts(rows_in):
    average = jnp.mean(rows_in, axis=-1, keepdims=True)
    centred = rows_in - average
    inverse = lax.rsqrt(jnp.mean(centred * centred, axis=-1, keepdims=True) + eps_norm)
    return centred * inverse, inverse


def norm_back(rows_in, gain_row, grad_rows):
    unit, inverse = norm_parts(rows_in)
    scaled = grad_rows * gain_row
    mean_one = jnp.mean(scaled, axis=-1, keepdims=True)
    mean_two = jnp.mean(scaled * unit, axis=-1, keepdims=True)
    return (scaled - mean_one - unit * mean_two) * inverse, grad_rows * unit


def head_window(head, head_size, width):
    start = min(head * head_size // 128 * 128, width - 256)
    return start, head * head_size - start


def only_head(block, low, head_size):
    lane = lax.broadcasted_iota(jnp.int32, block.shape, 1)
    return jnp.where((lane >= low) & (lane < low + head_size), block, jnp.zeros_like(block))


def column_sum(rows_in):
    return jnp.sum(rows_in, axis=0, keepdims=True)


def attn_forward_kernel(
    image, heights_ref, widths_ref, x_ref, w_ref, vec_ref,
    middle_ref, second_ref, normed_ref, q_ref, k_ref, v_ref, probs_ref, attended_ref,
    vt_ref, at_ref,
):
    kept_heads = probs_ref.shape[0]
    slots, width = x_ref.shape
    head_size = width // H
    step = 64
    for at in range(0, slots, step):
        unit, _ = norm_parts(x_ref[at : at + step, :].astype(f32))
        normed_ref[at : at + step, :] = (
            unit * vec_ref[GAIN_ONE : GAIN_ONE + 1, :] + vec_ref[SHIFT_ONE : SHIFT_ONE + 1, :]
        ).astype(bf16)
    normed = normed_ref[...]
    q_ref[...] = (dot(normed, weight_part(w_ref, 0)) + vec_ref[Q_BIAS : Q_BIAS + 1, :]).astype(bf16)
    k_ref[...] = dot(normed, weight_part(w_ref, 1)).astype(bf16)
    values = dot(normed, weight_part(w_ref, 2)) + vec_ref[V_BIAS : V_BIAS + 1, :]
    v_ref[...] = values.astype(bf16)
    vt_ref[...] = values.astype(bf16).T
    slot = lax.broadcasted_iota(jnp.int32, (slots, 128), 0)
    valid = (slot // GRID < heights_ref[image]) & (slot % GRID < widths_ref[image])
    mask = jnp.where(valid, 0.0, -1e30).astype(f32)
    scale = head_size ** (-0.5)
    for head in range(H):
        start, low = head_window(head, head_size, width)
        queries = only_head(q_ref[:, start : start + 256], low, head_size)
        scores = dot_nt(k_ref[:, start : start + 256], queries)
        for at in range(0, slots, 128):
            part = scores[:, at : at + 128] * scale + mask
            exponent = jnp.exp(part - jnp.max(part, axis=0, keepdims=True))
            inverse = 1.0 / jnp.sum(exponent, axis=0, keepdims=True)
            probs_ref[head % kept_heads, :, at : at + 128] = (exponent * inverse).astype(bf16)
        here = slice(head * head_size, (head + 1) * head_size)
        at_ref[here, :] = dot(vt_ref[here, :], probs_ref[head % kept_heads])
    attended_ref[...] = at_ref[...].T.astype(bf16)
    branch = dot(attended_ref[...], weight_part(w_ref, 3))
    middle_ref[...] = x_ref[...].astype(f32) + (branch + vec_ref[OUT_BIAS : OUT_BIAS + 1, :])
    for at in range(0, slots, step):
        unit, _ = norm_parts(middle_ref[at : at + step, :])
        second_ref[at : at + step, :] = (
            unit * vec_ref[GAIN_TWO : GAIN_TWO + 1, :] + vec_ref[SHIFT_TWO : SHIFT_TWO + 1, :]
        ).astype(bf16)


def attn_forward(layer_input, attn_w, vecs, heights, widths, image, keep):
    slots, width = layer_input.shape
    wide = jax.ShapeDtypeStruct((slots, width), f32)
    low = jax.ShapeDtypeStruct((slots, width), bf16)
    probs = jax.ShapeDtypeStruct((H if keep else 4, slots, slots), bf16)
    here = pl.BlockSpec(memory_space=pltpu.VMEM)
    results = [wide, low, low, low, low, low, probs, low]
    outs = len(results) if keep else 2
    return pl.pallas_call(
        functools.partial(attn_forward_kernel, image),
        in_specs=[pl.BlockSpec(memory_space=pltpu.SMEM)] * 2 + [here] * 3,
        out_specs=[here] * outs,
        scratch_shapes=[pltpu.VMEM(r.shape, r.dtype) for r in results[outs:]]
        + [pltpu.VMEM((width, slots), bf16), pltpu.VMEM((width, slots), f32)],
        out_shape=results[:outs],
        compiler_params=pltpu.CompilerParams(vmem_limit_bytes=6 * 2**20),
        cost_estimate=pl.CostEstimate(
            flops=ATTN_COST * slots * width * width, bytes_accessed=attn_w.size * 2, transcendentals=slots * slots * H
        ),
        name="attn_forward",
    )(heights, widths, layer_input, attn_w, vecs)


def gelu_parts(pre):
    bell = jnp.exp2(pre * pre * (-0.5 * LOG2_E))
    scaled = 1.0 + jnp.abs(pre) * (0.3275911 * 0.5**0.5)
    near = pl.reciprocal(scaled, approx=True)
    near = near * (2.0 - scaled * near)
    tail = near * (0.5 * 1.061405429) - 0.5 * 1.453152027
    for coefficient in (1.421413741, -0.284496736, 0.254829592):
        tail = tail * near + 0.5 * coefficient
    tail = tail * near * bell
    return jnp.where(pre < 0.0, tail, 1.0 - tail), bell


def up_columns(w_ref, at):
    width = w_ref.shape[2]
    rows = width // LEAD
    chunk, column = at // width, at % width
    return w_ref[:, chunk * rows : (chunk + 1) * rows, column : column + TILE].reshape(width, TILE)


def mlp_up_kernel(keep_slope, pieces, *refs):
    second_refs, (w_ref, vec_ref, act_ref) = refs[:pieces], refs[pieces : pieces + 3]
    slope_ref = refs[pieces + 3] if keep_slope else None
    pre_refs = refs[-2:]
    slots, width = second_refs[0].shape
    hidden = act_ref.shape[1]

    def multiply(at):
        weight = up_columns(w_ref, at)
        for piece, second_ref in enumerate(second_refs):
            pre_refs[at // TILE % 2][piece * slots : (piece + 1) * slots, :] = dot(second_ref[...], weight)

    multiply(0)
    for at in range(0, hidden, TILE):
        if at + TILE < hidden:
            multiply(at + TILE)
        columns = slice(at, at + TILE)
        row = UP_BIAS + at // width
        bias = vec_ref[row : row + 1, at % width : at % width + TILE]
        for start in range(0, slots * pieces, MLP_CHUNK):
            here = slice(start, start + MLP_CHUNK)
            pre = pre_refs[at // TILE % 2][here, :] + bias
            below, bell = gelu_parts(pre)
            act_ref[here, columns] = (pre * below).astype(bf16)
            if keep_slope:
                slope_ref[here, columns] = (below + pre * bell * (0.5 / jnp.pi) ** 0.5).astype(bf16)


def mlp_up(second, mlp_w, vecs, keep_slope):
    slots, width = second[0].shape
    count = slots * len(second)
    hidden = mlp_w.shape[1] * LEAD // 2
    outs = 2 if keep_slope else 1
    here = pl.BlockSpec(memory_space=pltpu.VMEM)
    return pl.pallas_call(
        functools.partial(mlp_up_kernel, keep_slope, len(second)),
        in_specs=[here] * (len(second) + 2),
        out_specs=[here] * outs,
        out_shape=[jax.ShapeDtypeStruct((count, hidden), bf16)] * outs,
        scratch_shapes=[pltpu.VMEM((count, TILE), f32)] * 2,
        compiler_params=pltpu.CompilerParams(vmem_limit_bytes=6 * 2**20),
        cost_estimate=pl.CostEstimate(
            flops=MLP_COST * count * width * hidden,
            bytes_accessed=mlp_w.size + count * hidden * 4,
            transcendentals=2 * count * hidden,
        ),
        name="mlp_up",
    )(*second, mlp_w, vecs)


def mlp_down_kernel(pieces, act_ref, *refs):
    middle_refs, (w_ref, vec_ref, result_ref) = refs[:pieces], refs[pieces:]
    slots, width = middle_refs[0].shape
    hidden = act_ref.shape[1]
    bias = vec_ref[DOWN_BIAS : DOWN_BIAS + 1, :]
    for column in range(0, width, TILE):
        columns = slice(column, column + TILE)
        weight = w_ref[:, w_ref.shape[1] // 2 :, columns].reshape(hidden, TILE)
        for piece, middle_ref in enumerate(middle_refs):
            here = slice(piece * slots, (piece + 1) * slots)
            added = dot(act_ref[here, :], weight)
            result_ref[here, columns] = (added + (middle_ref[:, columns] + bias[:, columns])).astype(bf16)


def mlp_down(activated, middle, mlp_w, vecs):
    slots, width = middle[0].shape
    count = slots * len(middle)
    here = pl.BlockSpec(memory_space=pltpu.VMEM)
    return pl.pallas_call(
        functools.partial(mlp_down_kernel, len(middle)),
        in_specs=[here] * (len(middle) + 3),
        out_specs=here,
        out_shape=jax.ShapeDtypeStruct((count, width), bf16),
        compiler_params=pltpu.CompilerParams(vmem_limit_bytes=4 * 2**20),
        cost_estimate=pl.CostEstimate(
            flops=MLP_COST * count * width * activated.shape[1],
            bytes_accessed=mlp_w.size + count * width * 10,
            transcendentals=0,
        ),
        name="mlp_down",
    )(activated, *middle, mlp_w, vecs)


def mlp_backward_kernel(pieces, first, turn_pieces, slope_ref, *refs):
    if turn_pieces:
        count = 1 + 2 * turn_pieces
        last = len(refs) - 2
        turn_kernel(turn_pieces, *refs[:count], *refs[last - 4 : last])
        refs = (*refs[count : last - 4], *refs[last:])
    upstream_refs, middle_refs, refs = refs[:pieces], refs[pieces : 2 * pieces], refs[2 * pieces :]
    (w_ref, vec_ref), refs = refs[:2], refs[2:]
    grad_middle_refs, branch_refs, refs = refs[:pieces], refs[pieces : 2 * pieces], refs[2 * pieces :]
    grad_pre_ref, sums_ref, up_sum_ref, ga_refs = refs[0], refs[1], refs[2], refs[3:]
    slots, width = upstream_refs[0].shape
    hidden = slope_ref.shape[1]
    half = w_ref.shape[1] // 2

    step = LEAD // 4 * half

    def multiply(at):
        weight = w_ref[at // half : (at + step) // half, half:, :].reshape(step, width)
        for piece, upstream_ref in enumerate(upstream_refs):
            ga_refs[at // step % 2][piece * slots : (piece + 1) * slots, :] = dot_nt(upstream_ref[...], weight)

    multiply(0)
    for at in range(0, hidden, step):
        if at + step < hidden:
            multiply(at + step)
        sums = jnp.zeros((1, step), f32)
        for start in range(0, slots * pieces, MLP_CHUNK):
            here = slice(start, start + MLP_CHUNK)
            slope = slope_ref[first * slots + start : first * slots + start + MLP_CHUNK, at : at + step]
            pre = (ga_refs[at // step % 2][here, :] * slope.astype(f32)).astype(bf16)
            grad_pre_ref[here, at : at + step] = pre
            sums += column_sum(pre.astype(f32))
        up_sum_ref[at // width, :, at % width : at % width + step] = sums
    gain = vec_ref[GAIN_TWO : GAIN_TWO + 1, :]
    sums = [jnp.zeros((1, width), f32)] * 3
    for piece in range(pieces):
        rows = slice(piece * slots, (piece + 1) * slots)
        total = None
        for chunk in range(hidden // width):
            weight = w_ref[:, chunk * width // LEAD : (chunk + 1) * width // LEAD, :].reshape(width, width)
            added = dot_nt(grad_pre_ref[rows, chunk * width : (chunk + 1) * width], weight)
            total = added if total is None else total + added
        ga_refs[piece % 2][:slots, :] = total
        for at in range(0, slots, MLP_CHUNK):
            here = slice(at, at + MLP_CHUNK)
            upstream = upstream_refs[piece][here, :].astype(f32)
            grad = ga_refs[piece % 2][here, :]
            grad_mid, gain_terms = norm_back(middle_refs[piece][here, :], gain, grad)
            whole = upstream + grad_mid
            grad_middle_refs[piece][here, :] = whole
            branch_refs[piece][here, :] = whole.astype(bf16)
            sums = [old + column_sum(new) for old, new in zip(sums, (upstream, gain_terms, grad))]
    for row, value in enumerate(sums):
        sums_ref[row : row + 1, :] = value


def mlp_backward(upstream, slope, middle, mlp_w, vecs, image=0, turn=()):
    slots, width = middle[0].shape
    pieces = len(middle)
    count = slots * pieces
    parts = mlp_w.shape[1] * LEAD // (2 * width)
    here = pl.BlockSpec(memory_space=pltpu.VMEM)
    turn_in, turn_out = turn_arrays(*turn) if turn else ([], [])
    outs = pl.pallas_call(
        functools.partial(mlp_backward_kernel, pieces, image, (len(turn_in) - 1) // 2 if turn else 0),
        in_specs=[here] * (2 * pieces + 3 + len(turn_in)),
        out_specs=[here] * (2 * pieces + 3 + len(turn_out)),
        out_shape=[jax.ShapeDtypeStruct((slots, width), f32)] * pieces
        + [jax.ShapeDtypeStruct((slots, width), bf16)] * pieces
        + [
            jax.ShapeDtypeStruct((count, width * parts), bf16),
            jax.ShapeDtypeStruct((8, width), f32),
            jax.ShapeDtypeStruct((parts, 1, width), f32),
        ]
        + turn_out,
        scratch_shapes=[pltpu.VMEM((count, width), f32)] * 2,
        compiler_params=pltpu.CompilerParams(vmem_limit_bytes=8 * 2**20),
        cost_estimate=pl.CostEstimate(
            flops=2 * MLP_COST * count * width * width * parts,
            bytes_accessed=mlp_w.size * 2 + count * width * (10 + 4 * parts),
            transcendentals=0,
        ),
        name="mlp_backward",
    )(slope, *turn_in, *upstream, *middle, mlp_w, vecs)
    return outs[:pieces], outs[pieces : 2 * pieces], *outs[2 * pieces :]


def attn_backward_kernel(
    grad_middle_ref, branch_ref, x_ref, q_ref, k_ref, v_ref, probs_ref, w_ref, vec_ref,
    grad_in_ref, grad_low_ref, gq_ref, gk_ref, gv_ref, sums_ref,
    ga_ref, gat_ref, qt_ref, kt_ref, gqt_ref, gkt_ref, gvt_ref,
):
    slots, width = x_ref.shape
    head_size = width // H
    scale = head_size ** (-0.5)
    ga = dot_nt(branch_ref[...], weight_part(w_ref, 3)).astype(bf16)
    ga_ref[...] = ga
    gat_ref[...] = ga.T
    qt_ref[...] = q_ref[...].T
    kt_ref[...] = k_ref[...].T
    for head in range(H):
        start, low = head_window(head, head_size, width)
        here = slice(head * head_size, (head + 1) * head_size)
        own = only_head(ga_ref[:, start : start + 256], low, head_size)
        grad_probs = dot_nt(v_ref[:, start : start + 256], own)
        pieces = []
        for at in range(0, slots, 128):
            probs = probs_ref[head, :, at : at + 128].astype(f32)
            grad = grad_probs[:, at : at + 128]
            total = jnp.sum(probs * grad, axis=0, keepdims=True)
            pieces.append((probs * (grad - total)).astype(bf16))
        grad_scores = jnp.concatenate(pieces, axis=1)
        gvt_ref[here, :] = dot_nt(gat_ref[here, :], probs_ref[head])
        gqt_ref[here, :] = dot(kt_ref[here, :], grad_scores) * scale
        gkt_ref[here, :] = dot_nt(qt_ref[here, :], grad_scores) * scale
    gq_ref[...] = gqt_ref[...].T.astype(bf16)
    gk_ref[...] = gkt_ref[...].T.astype(bf16)
    gv_ref[...] = gvt_ref[...].T.astype(bf16)
    grad_normed = dot_nt(gq_ref[...], weight_part(w_ref, 0))
    grad_normed += dot_nt(gk_ref[...], weight_part(w_ref, 1))
    grad_normed += dot_nt(gv_ref[...], weight_part(w_ref, 2))
    grad_in_ref[...] = grad_normed
    gain = vec_ref[GAIN_ONE : GAIN_ONE + 1, :]
    sums = [jnp.zeros((1, width), f32)] * 5
    for at in range(0, slots, MLP_CHUNK):
        rows = slice(at, at + MLP_CHUNK)
        grad = grad_in_ref[rows, :]
        grad_norm, gain_terms = norm_back(x_ref[rows, :].astype(f32), gain, grad)
        total = grad_middle_ref[rows, :] + grad_norm
        grad_in_ref[rows, :] = total
        grad_low_ref[rows, :] = total.astype(bf16)
        terms = (
            gq_ref[rows, :].astype(f32), gv_ref[rows, :].astype(f32), branch_ref[rows, :].astype(f32),
            gain_terms, grad,
        )
        sums = [old + column_sum(new) for old, new in zip(sums, terms)]

    for row, value in enumerate(sums):
        sums_ref[row : row + 1, :] = value


def attn_backward(grad_middle, branch, layer_input, saved, attn_w, vecs):
    queries, key_rows, values, probs = saved
    slots, width = layer_input.shape
    low = jax.ShapeDtypeStruct((slots, width), bf16)
    here = pl.BlockSpec(memory_space=pltpu.VMEM)
    flipped = pltpu.VMEM((width, slots), bf16)
    flipped_wide = pltpu.VMEM((width, slots), f32)
    return pl.pallas_call(
        attn_backward_kernel,
        in_specs=[here] * 9,
        out_specs=[here] * 6,
        out_shape=[jax.ShapeDtypeStruct((slots, width), f32)] + [low] * 4 + [jax.ShapeDtypeStruct((8, width), f32)],
        scratch_shapes=[pltpu.VMEM((slots, width), bf16)] + [flipped] * 3 + [flipped_wide] * 3,
        compiler_params=pltpu.CompilerParams(vmem_limit_bytes=8 * 2**20),
        cost_estimate=pl.CostEstimate(
            flops=ATTN_COST * slots * width * width, bytes_accessed=attn_w.size * 2, transcendentals=0
        ),
        name="attn_backward",
    )(grad_middle, branch, layer_input, queries, key_rows, values, probs, attn_w, vecs)


def ring_slot(owner, me):
    there, here = place_of(lax.div(owner, 2)), place_of(lax.div(me, 2))
    return lax.rem(there - here + RING, RING)


def store_block(own_ref, peer_ref, owner, core, rows, value):
    me = lax.axis_index("dp")
    slot = ring_slot(owner, me)

    @pl.when(lax.rem(me, 2) == core)
    def _():
        own_ref[slot, rows, :] = value

    @pl.when(lax.rem(me, 2) != core)
    def _():
        peer_ref[slot, rows, :] = value


def scatter_shapes(rows, width):
    return [jax.ShapeDtypeStruct((RING, rows, width), bf16)] * 2


def joined(refs, scratch_ref):
    slots = refs[0].shape[0]
    for piece, ref in enumerate(refs):
        scratch_ref[piece * slots : (piece + 1) * slots, :] = ref[...]


def flipped(refs, scratch_ref):
    slots = refs[0].shape[0]
    for piece, ref in enumerate(refs):
        scratch_ref[:, piece * slots : (piece + 1) * slots] = ref[...].T


def turn_kernel(pieces, act_ref, *refs):
    second_refs, attended_refs, outs = refs[:pieces], refs[pieces : 2 * pieces], refs[2 * pieces :]
    own_act, peer_act, own_small, peer_small = outs
    slots, width = second_refs[0].shape
    core = lax.rem(lax.axis_index("dp"), 2)
    rows, act_rows = own_small.shape[1] // 2, own_act.shape[1]

    def put(own_ref, peer_ref, owner, here, columns, value):
        @pl.when(core == owner % 2)
        def _():
            own_ref[owner // 2, here, columns] = value

        @pl.when(core != owner % 2)
        def _():
            peer_ref[owner // 2, here, columns] = value

    for piece in range(pieces):
        columns = slice(piece * slots, (piece + 1) * slots)
        for at in range(0, act_ref.shape[1], width):
            turned = act_ref[columns, at : at + width].T
            for first in range(0, width, act_rows):
                put(own_act, peer_act, (at + first) // act_rows, slice(None), columns, turned[first : first + act_rows])
        for part, side in enumerate((second_refs, attended_refs)):
            turned = side[piece][...].T
            for owner in range(LEAD):
                here = slice(part * rows, (part + 1) * rows)
                put(own_small, peer_small, owner, here, columns, turned[owner * rows : (owner + 1) * rows])


def turn_arrays(activated, second, attended):
    count, hidden = activated.shape
    width = second[0].shape[1]
    big = jax.ShapeDtypeStruct((RING, hidden // LEAD, count), bf16)
    small = jax.ShapeDtypeStruct((RING, 2 * width // LEAD, count), bf16)
    return [activated, *second, *attended], [big, big, small, small]


def grad_down_kernel(pieces, own_ref, got_ref, *refs):
    mine, theirs, (out_ref, right_ref, got_right_ref) = refs[:pieces], refs[pieces : 2 * pieces], refs[2 * pieces :]
    joined(mine, right_ref)
    joined(theirs, got_right_ref)
    me = lax.axis_index("dp")
    chips, rows, count = own_ref.shape
    for chip in range(0, chips, 2):
        left, got = (ref[chip : chip + 2].reshape(2 * rows, count) for ref in (own_ref, got_ref))
        value = (dot(left, right_ref[...]) + dot(got, got_right_ref[...])).astype(bf16)
        for at in range(2):
            out_ref[ring_slot(2 * (chip + at), me)] = value[at * rows : (at + 1) * rows]


def grad_down_blocks(own_act, got_act, upstream, got_upstream):
    slots, width = upstream[0].shape
    chips, rows, count = own_act.shape
    here = pl.BlockSpec(memory_space=pltpu.VMEM)
    return pl.pallas_call(
        functools.partial(grad_down_kernel, len(upstream)),
        in_specs=[here] * (2 + 2 * len(upstream)),
        out_specs=here,
        out_shape=jax.ShapeDtypeStruct((RING, rows, width), bf16),
        scratch_shapes=[pltpu.VMEM((count, width), bf16)] * 2,
        compiler_params=pltpu.CompilerParams(vmem_limit_bytes=8 * 2**20),
        cost_estimate=pl.CostEstimate(
            flops=MLP_COST * 2 * count * width * chips * rows, bytes_accessed=count * chips * rows * 4, transcendentals=0
        ),
        name="grad_down",
    )(own_act, got_act, *upstream, *got_upstream)


def grad_up_kernel(pieces, own_ref, got_ref, *refs):
    groups, (out_ref, left_ref, right_ref) = refs[: 4 * pieces], refs[4 * pieces :]
    pre_refs, branch_refs = groups[: 2 * pieces], groups[2 * pieces :]
    me = lax.axis_index("dp")
    chips, both_rows, count = own_ref.shape
    rows = both_rows // 2
    width = branch_refs[0].shape[1]
    parts = pre_refs[0].shape[1] // width
    slots = pre_refs[0].shape[0]

    def lefts(part):
        for at, ref in enumerate((own_ref, got_ref)):
            side = ref[:, part * rows : (part + 1) * rows, :].reshape(chips * rows, count)
            left_ref[:, at * count : (at + 1) * count] = side

    def store(part):
        value = dot(left_ref[...], right_ref[...]).astype(bf16)
        for chip in range(chips):
            here = slice(part * rows, (part + 1) * rows)
            out_ref[ring_slot(2 * chip, me), here, :] = value[chip * rows : (chip + 1) * rows]

    lefts(0)
    for part in range(parts):
        for piece, ref in enumerate(pre_refs):
            right_ref[piece * slots : (piece + 1) * slots, :] = ref[:, part * width : (part + 1) * width]
        store(part)
    lefts(1)
    joined(branch_refs, right_ref)
    store(parts)


def grad_up_blocks(own_small, got_small, grad_pre, branch):
    width = branch[0].shape[1]
    hidden = grad_pre[0].shape[1]
    chips, both_rows, count = own_small.shape
    rows = hidden // LEAD + both_rows // 2
    here = pl.BlockSpec(memory_space=pltpu.VMEM)
    return pl.pallas_call(
        functools.partial(grad_up_kernel, len(branch) // 2),
        in_specs=[here] * (2 + 2 * len(branch)),
        out_specs=here,
        out_shape=jax.ShapeDtypeStruct((RING, rows, width), bf16),
        scratch_shapes=[pltpu.VMEM((chips * both_rows // 2, 2 * count), bf16), pltpu.VMEM((2 * count, width), bf16)],
        compiler_params=pltpu.CompilerParams(vmem_limit_bytes=8 * 2**20),
        cost_estimate=pl.CostEstimate(
            flops=MLP_COST * count * width * hidden, bytes_accessed=count * hidden * 4, transcendentals=0
        ),
        name="grad_up",
    )(own_small, got_small, *grad_pre, *branch)


def grad_qkv_kernel(pieces, *refs):
    left_refs, rights = refs[:pieces], refs[pieces : 4 * pieces]
    attn_sums, mlp_sums, up_sums = (refs[at * pieces : (at + 1) * pieces] for at in (4, 5, 6))
    own_ref, peer_ref, left_ref, right_ref, vec_ref = refs[7 * pieces :]
    width = left_refs[0].shape[1]
    rows = width // LEAD
    flipped(left_refs, left_ref)
    for part in range(3):
        joined(rights[part * pieces : (part + 1) * pieces], right_ref)
        value = dot(left_ref[...], right_ref[...]).astype(bf16)
        for owner in range(LEAD):
            here = slice(part * rows, (part + 1) * rows)
            store_block(own_ref, peer_ref, owner, owner % 2, here, value[owner * rows : (owner + 1) * rows])
    vec_ref[...] = jnp.zeros_like(vec_ref)
    for name, refs_of, row in (
        (Q_BIAS, attn_sums, 0), (V_BIAS, attn_sums, 1), (OUT_BIAS, attn_sums, 2), (DOWN_BIAS, mlp_sums, 0),
        (GAIN_ONE, attn_sums, 3), (SHIFT_ONE, attn_sums, 4), (GAIN_TWO, mlp_sums, 1), (SHIFT_TWO, mlp_sums, 2),
    ):
        vec_ref[name : name + 1, :] = sum(ref[row : row + 1, :] for ref in refs_of)
    for part in range(up_sums[0].shape[0]):
        vec_ref[UP_BIAS + part : UP_BIAS + part + 1, :] = sum(ref[part] for ref in up_sums)
    vectors = vec_ref[...].astype(bf16)
    here = slice(3 * rows, 3 * rows + VEC_ROWS)
    for slot in range(RING):
        own_ref[slot, here, :] = vectors
        peer_ref[slot, here, :] = vectors


def grad_qkv_blocks(normed, rights, attn_sums, mlp_sums, up_sums):
    slots, width = normed[0].shape
    count = slots * len(normed)
    arrays = [*normed, *(piece for right in rights for piece in right), *attn_sums, *mlp_sums, *up_sums]
    rows = 3 * width // LEAD + VEC_ROWS
    return pl.pallas_call(
        functools.partial(grad_qkv_kernel, len(normed)),
        in_specs=[pl.BlockSpec(memory_space=pltpu.VMEM)] * len(arrays),
        out_specs=[pl.BlockSpec(memory_space=pltpu.VMEM)] * 2,
        out_shape=scatter_shapes(rows, width),
        scratch_shapes=[
            pltpu.VMEM((width, count), bf16), pltpu.VMEM((count, width), bf16), pltpu.VMEM((VEC_ROWS, width), f32)
        ],
        compiler_params=pltpu.CompilerParams(vmem_limit_bytes=6 * 2**20),
        cost_estimate=pl.CostEstimate(
            flops=3 * MLP_COST * count * width * width, bytes_accessed=len(arrays) * slots * width * 2, transcendentals=0
        ),
        name="grad_qkv",
    )(*arrays)


VECS = ("q_bias", "v_bias", "out_bias", "down_bias", "gain_one", "shift_one", "gain_two", "shift_two")


def solution(mesh):
    dp_size = mesh.shape["dp"]
    ringed = dp_size == 2 * RING

    def gathered_whole(qkv, out, up, down, vectors):
        width = out.shape[1]
        gathered = [lax.all_gather(w, "dp", axis=0, tiled=True) for w in (qkv, out, up, down)]
        blocked = [w.reshape(LEAD, -1, w.shape[1]) for w in gathered]
        fold = lambda w: w.reshape(LEAD, w.shape[1], -1, width).transpose(0, 2, 1, 3).reshape(LEAD, -1, width)
        first = jnp.concatenate([fold(blocked[0]), blocked[1], jnp.zeros((LEAD, VEC_ROWS, width), bf16)], 1)
        whole = lambda name: lax.all_gather(vectors[name], "dp", axis=0, tiled=True)
        vecs = jnp.concatenate([jnp.stack([whole(name) for name in VECS]), whole("up_bias").reshape(-1, width)])
        vecs = jnp.pad(vecs.astype(f32), ((0, VEC_ROWS - vecs.shape[0]), (0, 0)))
        return first, jnp.concatenate([fold(blocked[2]), blocked[3]], 1), vecs

    def own_vectors(block):
        me = lax.axis_index("dp")
        width = block.shape[1]
        rows = width // LEAD
        small = lax.dynamic_slice(block, (0, me * rows), (len(VECS), rows))
        parts = (3 * LEAD + LEAD) * rows // width
        size = parts * rows
        in_row = width // size
        own = {name: small[at] for at, name in enumerate(VECS)}
        own["up_bias"] = lax.dynamic_slice(block, (len(VECS) + me // in_row, me % in_row * size), (1, size))[0]
        return own

    def shards(
        tokens, cotangent, heights, widths, qkv_weight, out_weight, up_weight, down_weight,
        q_bias, v_bias, out_bias, up_bias, down_bias, gain_one, shift_one, gain_two, shift_two,
    ):
        leading = lax.axis_index("section") == 0
        width = tokens.shape[1]
        images = heights.shape[0]
        each = range(images)
        rows = width // LEAD
        cut = lambda array: jnp.split(array, images)
        vectors = dict(
            q_bias=q_bias[0], v_bias=v_bias[0], out_bias=out_bias[0], up_bias=up_bias[0], down_bias=down_bias[0],
            gain_one=gain_one[0], shift_one=shift_one[0], gain_two=gain_two[0], shift_two=shift_two[0],
        )
        inputs, cotangents = cut(tokens), cut(cotangent)

        attention = lambda x, image, keep: attn_forward(x, attn_w, vecs, heights, widths, image, keep)
        if ringed:
            small = jnp.stack([vectors[name] for name in VECS])
            one, two = pack_first(qkv_weight[0], out_weight[0], small, vectors["up_bias"][None])
            g, h = gather_start(one), gather_start(two)
            u, d = gather_start(pack_columns(up_weight[0], width)), gather_start(down_weight[0])
            for _ in range(RING // 2 - 1):
                g, h = gather_step(g), gather_step(h)
            g["mine"], u["mine"] = tie(g["mine"], u["mine"])
            h["mine"], d["mine"] = tie(h["mine"], d["mine"])
            g, h, u, d = (gather_step(state) for state in (g, h, u, d))
            attn_w, vecs = assemble([g, h], True)
            front = [attention(inputs[0], 0, False)]
            attn_w, front, u["mine"], d["mine"] = tie(attn_w, front, u["mine"], d["mine"])
            u, d = gather_step(u), gather_step(d)
            front += [attention(inputs[image], image, False) for image in each[1:]]
            front, u["mine"], d["mine"] = tie(front, u["mine"], d["mine"])
            for _ in range(u["step"], RING // 2):
                u, d = gather_step(u), gather_step(d)
            mlp_w = assemble([u, d])
        else:
            attn_w, mlp_w, vecs = gathered_whole(
                qkv_weight[0], out_weight[0], up_weight[0], down_weight[0], vectors
            )
            front = [attention(inputs[image], image, False) for image in each]
        received = []
        for image in each:
            (activated,) = mlp_up(front[image][1:], mlp_w, vecs, False)
            sent = mlp_down(activated, front[image][:1], mlp_w, vecs)
            front, sent = tie(front, sent)
            received.append(lax.ppermute(sent, "section", [(0, 1)]))

        layer_input, kept = [], []
        for image in each:
            layer_input.append(jnp.where(leading, inputs[image], received[image]))
            kept.append(attention(layer_input[image], image, True))
            kept, received = tie(kept, received)
        middle, second, normed, queries, key_rows, values, probs, attended = zip(*kept)
        activated, slope = mlp_up(second, mlp_w, vecs, True)

        back_attn = lambda grad, branch, image: attn_backward(
            grad[image], branch[image], layer_input[image],
            (queries[image], key_rows[image], values[image], probs[image]), attn_w, vecs,
        )
        grad_middle, branch = mlp_backward(cotangents, slope, middle, mlp_w, vecs)[:2]
        arriving = []
        for image in each:
            to_send = back_attn(grad_middle, branch, image)[1]
            grad_middle, branch, activated, to_send = tie(grad_middle, branch, activated, to_send)
            arriving.append(lax.ppermute(to_send, "section", [(1, 0)]))
        upstream, back = [jnp.where(leading, arriving[0], cotangents[0])], []

        def back_one(image, turn=()):
            outs = mlp_backward(upstream[image : image + 1], slope, middle[image : image + 1], mlp_w, vecs, image, turn)
            back.append(outs[:5])
            return outs[5:]

        turned = back_one(0, (activated, second, attended) if ringed else ())
        got_pre, got_branch = [], []

        def exchange(image):
            got_pre.append(across(back[image][2]))
            got_branch.append(across(back[image][1][0]))

        back, activated, arriving, turned = tie(back, activated, arriving, turned)
        if ringed:
            own_act, peer_act, own_small, peer_small = turned
            got_act, got_small = across(peer_act), across(peer_small)
        else:
            result = mlp_down(activated, middle, mlp_w, vecs)
        upstream += [jnp.where(leading, arriving[image], cotangents[image]) for image in each[1:]]
        if ringed:
            got_upstream = [across(array) for array in upstream]
            exchange(0)
            d = scatter_start(grad_down_blocks(own_act, got_act, upstream, got_upstream))
            d, upstream = scatter_step(d, upstream)
            for image in each[1:]:
                back_one(image)
            d, back, got_pre, got_branch = tie(d, back, got_pre, got_branch)
            d, back = scatter_step(d, back)
            grad_middle, branch, grad_pre, mlp_sums, up_sums = zip(*back)
            grad_middle, branch = [g for (g,) in grad_middle], [g for (g,) in branch]
            for image in each[1:]:
                exchange(image)
            held = (grad_middle, branch)
            attn_back = [back_attn(*held, 0)]
            d, attn_back, held, grad_pre, activated = tie(d, attn_back, held, grad_pre, activated)
            d, (grad_pre, activated) = scatter_step(d, (grad_pre, activated))
            result = mlp_down(activated, middle, mlp_w, vecs)
            u = scatter_start(grad_up_blocks(own_small, got_small, [*grad_pre, *got_pre], [*branch, *got_branch]))
            d, u, held, result = tie(d, u, held, result)
            u, held = scatter_step(u, held)
            d, held = scatter_step(d, held)
            attn_back += [back_attn(*held, image) for image in each[1:]]
            d, u, attn_back = tie(d, u, attn_back)
            u, attn_back = scatter_step(u, attn_back)
        else:
            for image in each[1:]:
                back_one(image)
            grad_middle, branch, grad_pre, mlp_sums, up_sums = zip(*back)
            grad_middle, branch = [g for (g,) in grad_middle], [g for (g,) in branch]
            attn_back = [back_attn(grad_middle, branch, image) for image in each]
            grad_whole = jnp.concatenate([each_back[0] for each_back in attn_back])
        grad_input, _, gq, gk, gv, attn_sums = zip(*attn_back)
        if ringed:
            q = scatter_start(*grad_qkv_blocks(normed, (gq, gk, gv), attn_sums, mlp_sums, up_sums))
            parts = mlp_w.shape[1] // rows - 4
            ends = RING // 2 + 1
            q = scatter_step(q)[0]
            (g_down,) = scatter_sum(d, [(0, d["own"].shape[1], 1)])
            grad_whole = jnp.concatenate(grad_input)
            q = scatter_step(q)[0]
            q, g_down = tie(q, g_down)
            q = scatter_step(q)[0]
            q, grad_whole = tie(q, grad_whole)
            q = scatter_step(q)[0]
            while u["step"] < ends:
                u = scatter_step(u)[0]
            g_up, g_out = scatter_sum(u, [(0, rows, parts), (parts * rows, rows, 1)])
            q = scatter_step(q)[0]
            g_qkv, vec_sums = scatter_sum(q, [(0, rows, 3), (3 * rows, VEC_ROWS, 1)])
            g_vecs = own_vectors(vec_sums)
        else:
            attn_sums = sum(attn_sums)
            sums = dict(zip(("q_bias", "v_bias", "out_bias", "gain_one", "shift_one"), attn_sums))
            sums |= dict(zip(("down_bias", "gain_two", "shift_two"), sum(mlp_sums)))
            sums["up_bias"] = sum(up_sums).reshape(-1)
            scatter = lambda a: lax.psum_scatter(a, "dp", scatter_dimension=0, tiled=True)
            whole = lambda pieces: jnp.concatenate(pieces)
            outer = lambda a, b: lax.dot_general(a, b, TN, preferred_element_type=f32)
            g_down = scatter(outer(activated, whole(upstream)))
            g_up = scatter(outer(whole(second), whole(grad_pre)))
            g_qkv = scatter(jnp.concatenate([outer(whole(normed), whole(part)) for part in (gq, gk, gv)], 1))
            g_out = scatter(outer(whole(attended), whole(branch)))
            g_vecs = {name: scatter(value) for name, value in sums.items()}
        return (
            result[None], grad_whole[None],
            g_qkv[None], g_out[None], g_up[None], g_down[None],
            *(
                g_vecs[name][None]
                for name in (
                    "q_bias", "v_bias", "out_bias", "up_bias", "down_bias",
                    "gain_one", "shift_one", "gain_two", "shift_two",
                )
            ),
        )

    rows_spec = P("dp", None)
    three, two = P("section", "dp", None), P("section", "dp")
    return jax.shard_map(
        shards,
        mesh=mesh,
        in_specs=(rows_spec, rows_spec, P("dp"), P("dp")) + (three,) * 4 + (two,) * 9,
        out_specs=(three,) * 6 + (two,) * 9,
        check_vma=False,
    )
```

```python
import functools

import jax
import jax.numpy as jnp
from jax import lax
from jax.experimental import pallas as pl
from jax.experimental.pallas import tpu as pltpu
from jax.sharding import PartitionSpec as P

H = 16
GRID = 16
LEAD = 16
RING = 8
VEC_ROWS = 16

f32 = jnp.float32
bf16 = jnp.bfloat16
eps_norm = 1e-05


def chip_at(place):
    if isinstance(place, int):
        return 2 * place if place < 4 else 2 * (7 - place) + 1
    return jnp.where(place < 4, 2 * place, 2 * (7 - place) + 1)


def place_of(chip):
    if isinstance(chip, int):
        return chip // 2 if chip % 2 == 0 else 7 - chip // 2
    return jnp.where(chip % 2 == 0, chip // 2, 7 - chip // 2)


def ring_route(step):
    return [
        (2 * chip_at(place) + core, 2 * chip_at((place + step) % RING) + core)
        for place in range(RING)
        for core in range(2)
    ]


CORE_ROUTE = [(index, index ^ 1) for index in range(2 * RING)]


def onward(block):
    return lax.ppermute(block, "dp", ring_route(1))


def backward(block):
    return lax.ppermute(block, "dp", ring_route(-1))


def across(block):
    return lax.ppermute(block, "dp", CORE_ROUTE)


def around(block):
    route = [(2 * chip_at(p) + core, 2 * chip_at((p + (-1) ** core) % RING) + core) for p in range(RING) for core in (0, 1)]
    return lax.ppermute(block, "dp", route)


def tie(*values):
    leaves, tree = jax.tree.flatten(values)
    arrays = iter(lax.optimization_barrier([leaf for leaf in leaves if isinstance(leaf, jax.Array)]))
    held = jax.tree.unflatten(tree, [next(arrays) if isinstance(leaf, jax.Array) else leaf for leaf in leaves])
    return held if len(held) > 1 else held[0]


def pack_first(qkv, out, vectors, ups):
    rows, width = out.shape
    chunks = qkv.shape[1] // width
    names, size = vectors.shape[0], ups.shape[1]

    def kernel(qkv_ref, out_ref, vec_ref, up_ref, one_ref, two_ref):
        me = lax.axis_index("dp")
        for chunk in range(chunks):
            packed_ref, at = (one_ref, chunk) if chunk < 2 else (two_ref, chunk - 2)
            packed_ref[at * rows : (at + 1) * rows, :] = qkv_ref[:, chunk * width : (chunk + 1) * width]
        two_ref[(chunks - 2) * rows : (chunks - 1) * rows, :] = out_ref[...]
        lane = lax.broadcasted_iota(jnp.int32, (names, width), 1)
        spread = jnp.concatenate([vec_ref[...].astype(f32)] * (width // rows), axis=1)
        small = jnp.where((lane >= me * rows) & (lane < (me + 1) * rows), spread, 0.0)
        lane = lax.broadcasted_iota(jnp.int32, (VEC_ROWS - names, width), 1)
        row = lax.broadcasted_iota(jnp.int32, (VEC_ROWS - names, width), 0)
        spread = jnp.concatenate([up_ref[...].astype(f32)] * (width // size), axis=1)
        at = row * width + lane
        last = jnp.where((at >= me * size) & (at < (me + 1) * size), spread, 0.0)
        two_ref[(chunks - 1) * rows :, :] = jnp.concatenate([small, last], axis=0).astype(bf16)

    return pl.pallas_call(
        kernel,
        out_shape=[
            jax.ShapeDtypeStruct((2 * rows, width), bf16),
            jax.ShapeDtypeStruct(((chunks - 1) * rows + VEC_ROWS, width), bf16),
        ],
        compiler_params=pltpu.CompilerParams(vmem_limit_bytes=4 * 2**20),
        name="pack_first",
    )(qkv, out, vectors, ups)


def pack_columns(weight, width):
    rows, columns = weight.shape
    chunks = columns // width

    def kernel(weight_ref, packed_ref):
        for chunk in range(chunks):
            packed_ref[chunk * rows : (chunk + 1) * rows, :] = weight_ref[:, chunk * width : (chunk + 1) * width]

    return pl.pallas_call(
        kernel,
        out_shape=jax.ShapeDtypeStruct((chunks * rows, width), bf16),
        compiler_params=pltpu.CompilerParams(vmem_limit_bytes=4 * 2**20),
        name="pack_columns",
    )(weight)


def half_of(rows):
    return rows // 32 * 16


def gather_start(shard):
    return {"step": 0, "rows": shard.shape[0], "mine": [jnp.concatenate([shard, across(shard)])], "theirs": []}


def gather_step(state):
    step, rows = state["step"] + 1, state["rows"]
    mine, theirs = list(state["mine"]), list(state["theirs"])
    if step > 2:
        mine[-1], theirs[-2] = tie(mine[-1], theirs[-2])
    came = around(mine[-1] if step < RING // 2 else mine[-1][:rows])
    return {"step": step, "rows": rows, "mine": [*mine, came], "theirs": [*theirs, across(came)]}


def assemble(states, vectors=False):
    width = states[0]["mine"][0].shape[1]
    arrays = [array for state in states for array in state["mine"] + state["theirs"]]
    count = len(arrays)
    total_rows = sum(state["rows"] for state in states)

    def kernel(*refs):
        blocks, out = refs[:count], refs[count]
        me = lax.axis_index("dp")
        core, place = lax.rem(me, 2), place_of(lax.div(me, 2))
        way = 1 - 2 * core
        at, start = 0, 0
        for state in states:
            rows = state["rows"]
            for steps, own_first in ((range(RING // 2 + 1), 1), (range(1, RING // 2 + 1), 0)):
                for step in steps:
                    toward = step * way if not own_first else -step * way
                    chip = chip_at(lax.rem(place + toward + RING, RING))
                    first = core if own_first else 1 - core
                    out[2 * chip + first, start : start + rows, :] = blocks[at][:rows, :]
                    if step < RING // 2:
                        out[2 * chip + 1 - first, start : start + rows, :] = blocks[at][rows:, :]
                    at += 1
            start += rows
        if vectors:
            total = jnp.zeros((VEC_ROWS, width), f32)
            for owner in range(2 * RING):
                total += out[owner, total_rows - VEC_ROWS :, :].astype(f32)
            refs[count + 1][...] = total

    shapes = [jax.ShapeDtypeStruct((2 * RING, total_rows, width), bf16)]
    if vectors:
        shapes.append(jax.ShapeDtypeStruct((VEC_ROWS, width), f32))
    outs = pl.pallas_call(
        kernel,
        out_shape=shapes,
        in_specs=[pl.BlockSpec(memory_space=pltpu.VMEM)] * count,
        out_specs=[pl.BlockSpec(memory_space=pltpu.VMEM)] * len(shapes),
        compiler_params=pltpu.CompilerParams(vmem_limit_bytes=2 * RING * total_rows * width + 2**21),
        name="assemble",
    )(*arrays)
    return outs if vectors else outs[0]


def scatter_start(own, peer=None):
    return {"step": 1 if peer is None else 0, "own": own, "peer": peer}


def hop_kernel(step, half, both, *refs):
    count = 2 if both else 1
    last = step == RING // 2
    ups, downs, befores = refs[:count], refs[count : 2 * count], refs[2 * count : -2]
    up_out, down_out = refs[-2:]
    if last:
        homes, befores, local_out = befores[:count], befores[count : count + 2], refs[-1]
        up_out, down_out = refs[-3:-1]
    top, bottom = slice(0, half), slice(half, None)

    def local(blocks, rows):
        return sum(block[0, rows, :].astype(f32) for block in blocks)

    if step == 1:
        up_out[...] = local(ups, top).astype(bf16)
        down_out[...] = local(downs, bottom).astype(bf16)
        return
    up_in, down_in = befores
    if step == 2:
        up_out[top, :] = (local(ups, top) + up_in[...].astype(f32)).astype(bf16)
        up_out[bottom, :] = local(ups, bottom).astype(bf16)
        down_out[top, :] = local(downs, top).astype(bf16)
        down_out[bottom, :] = (local(downs, bottom) + down_in[...].astype(f32)).astype(bf16)
        return
    up_out[...] = (local(ups, slice(None)) + up_in[...].astype(f32)).astype(bf16)
    down_out[...] = (local(downs, slice(None)) + down_in[...].astype(f32)).astype(bf16)
    if last:
        local_out[...] = local(homes, slice(None))


def scatter_step(state, held=()):
    step = state["step"]
    own, peer = state["own"], state["peer"]
    if step == 0:
        peer, held = tie(peer, held)
        return {"step": 1, "own": own, "peer": across(peer)}, held
    rows, width = own.shape[1:]
    half, far = half_of(rows), RING // 2
    at = lambda place: pl.BlockSpec((1, rows, width), lambda i: (place, 0, 0))
    whole = lambda size: pl.BlockSpec((size, width), lambda i: (0, 0))
    up_place, down_place = far + 1 - step, far - 1 + step
    before = [] if step == 1 else [state["up"], state["down"]]
    sizes = (half, rows - half) if step == 1 else (rows, rows)
    both = [own] if peer is None else [own, peer]
    places = [up_place, down_place]
    shapes = [jax.ShapeDtypeStruct((size, width), bf16) for size in sizes]
    if step == far:
        places.append(0)
        shapes.append(jax.ShapeDtypeStruct((rows, width), f32))
    outs = pl.pallas_call(
        functools.partial(hop_kernel, step, half, peer is not None),
        grid=(1,),
        in_specs=[at(place) for place in places for _ in both] + [whole(b.shape[0]) for b in before],
        out_specs=[whole(shape.shape[0]) for shape in shapes],
        out_shape=shapes,
        compiler_params=pltpu.CompilerParams(vmem_limit_bytes=8 * 2**20),
        name="hop",
    )(*both * len(places), *before)
    up, down, held = tie(*outs[:2], held)
    state = {"step": step + 1, "own": own, "peer": peer, "up": onward(up), "down": backward(down)}
    if step == far:
        state["local"] = outs[2]
    return state, held


def scatter_sum(state, cuts):
    rows, width = state["local"].shape
    shapes = [jax.ShapeDtypeStruct((count, chunks * width), f32) for _, count, chunks in cuts]

    def kernel(local_ref, up_ref, down_ref, *outs):
        for (first, count, chunks), out in zip(cuts, outs):
            for chunk in range(chunks):
                here = slice(first + chunk * count, first + (chunk + 1) * count)
                sent = up_ref[here, :].astype(f32) + down_ref[here, :].astype(f32)
                out[:, chunk * width : (chunk + 1) * width] = local_ref[here, :] + sent

    here = pl.BlockSpec(memory_space=pltpu.VMEM)
    return pl.pallas_call(
        kernel,
        in_specs=[here] * 3,
        out_specs=[here] * len(shapes),
        out_shape=shapes,
        compiler_params=pltpu.CompilerParams(vmem_limit_bytes=12 * 2**20),
        cost_estimate=pl.CostEstimate(flops=rows * width * 2000, bytes_accessed=rows * width * 10, transcendentals=0),
        name="scatter_sum",
    )(state["local"], state["up"], state["down"])


VMEM_LIMIT = 24 * 2**20
MLP_CHUNK = 32
TILE = 256
LOG2_E = 1.4426950408889634
ATTN_COST, MLP_COST = 24, 6
Q_BIAS, V_BIAS, OUT_BIAS, DOWN_BIAS, GAIN_ONE, SHIFT_ONE, GAIN_TWO, SHIFT_TWO, UP_BIAS = range(9)
NT = (((1,), (1,)), ((), ()))
TN = (((0,), (0,)), ((), ()))


def dot(first_mat, second_mat):
    return jnp.dot(first_mat, second_mat, preferred_element_type=f32)


def dot_nt(first_mat, second_mat):
    return lax.dot_general(first_mat, second_mat, NT, preferred_element_type=f32)


def dot_tn(first_mat, second_mat):
    return lax.dot_general(first_mat, second_mat, TN, preferred_element_type=f32)


def weight_part(w_ref, part):
    width = w_ref.shape[2]
    rows = width // LEAD
    return w_ref[:, part * rows : (part + 1) * rows, :].reshape(width, width)


def norm_parts(rows_in):
    average = jnp.mean(rows_in, axis=-1, keepdims=True)
    centred = rows_in - average
    inverse = lax.rsqrt(jnp.mean(centred * centred, axis=-1, keepdims=True) + eps_norm)
    return centred * inverse, inverse


def norm_back(rows_in, gain_row, grad_rows):
    unit, inverse = norm_parts(rows_in)
    scaled = grad_rows * gain_row
    mean_one = jnp.mean(scaled, axis=-1, keepdims=True)
    mean_two = jnp.mean(scaled * unit, axis=-1, keepdims=True)
    return (scaled - mean_one - unit * mean_two) * inverse, grad_rows * unit


def head_window(head, head_size, width):
    start = min(head * head_size // 128 * 128, width - 256)
    return start, head * head_size - start


def only_head(block, low, head_size):
    lane = lax.broadcasted_iota(jnp.int32, block.shape, 1)
    return jnp.where((lane >= low) & (lane < low + head_size), block, jnp.zeros_like(block))


def column_sum(rows_in):
    return jnp.sum(rows_in, axis=0, keepdims=True)


def attn_forward_kernel(
    image, heights_ref, widths_ref, x_ref, w_ref, vec_ref,
    middle_ref, second_ref, normed_ref, q_ref, k_ref, v_ref, probs_ref, attended_ref,
    vt_ref, at_ref,
):
    kept_heads = probs_ref.shape[0]
    slots, width = x_ref.shape
    head_size = width // H
    step = 64
    for at in range(0, slots, step):
        unit, _ = norm_parts(x_ref[at : at + step, :].astype(f32))
        normed_ref[at : at + step, :] = (
            unit * vec_ref[GAIN_ONE : GAIN_ONE + 1, :] + vec_ref[SHIFT_ONE : SHIFT_ONE + 1, :]
        ).astype(bf16)
    normed = normed_ref[...]
    q_ref[...] = (dot(normed, weight_part(w_ref, 0)) + vec_ref[Q_BIAS : Q_BIAS + 1, :]).astype(bf16)
    k_ref[...] = dot(normed, weight_part(w_ref, 1)).astype(bf16)
    values = dot(normed, weight_part(w_ref, 2)) + vec_ref[V_BIAS : V_BIAS + 1, :]
    v_ref[...] = values.astype(bf16)
    vt_ref[...] = values.astype(bf16).T
    slot = lax.broadcasted_iota(jnp.int32, (slots, 128), 0)
    valid = (slot // GRID < heights_ref[image]) & (slot % GRID < widths_ref[image])
    mask = jnp.where(valid, 0.0, -1e30).astype(f32)
    scale = head_size ** (-0.5)
    for head in range(H):
        start, low = head_window(head, head_size, width)
        queries = only_head(q_ref[:, start : start + 256], low, head_size)
        scores = dot_nt(k_ref[:, start : start + 256], queries)
        for at in range(0, slots, 128):
            part = scores[:, at : at + 128] * scale + mask
            exponent = jnp.exp(part - jnp.max(part, axis=0, keepdims=True))
            inverse = 1.0 / jnp.sum(exponent, axis=0, keepdims=True)
            probs_ref[head % kept_heads, :, at : at + 128] = (exponent * inverse).astype(bf16)
        here = slice(head * head_size, (head + 1) * head_size)
        at_ref[here, :] = dot(vt_ref[here, :], probs_ref[head % kept_heads])
    attended_ref[...] = at_ref[...].T.astype(bf16)
    branch = dot(attended_ref[...], weight_part(w_ref, 3))
    middle_ref[...] = x_ref[...].astype(f32) + (branch + vec_ref[OUT_BIAS : OUT_BIAS + 1, :])
    for at in range(0, slots, step):
        unit, _ = norm_parts(middle_ref[at : at + step, :])
        second_ref[at : at + step, :] = (
            unit * vec_ref[GAIN_TWO : GAIN_TWO + 1, :] + vec_ref[SHIFT_TWO : SHIFT_TWO + 1, :]
        ).astype(bf16)


def attn_forward(layer_input, attn_w, vecs, heights, widths, image, keep):
    slots, width = layer_input.shape
    wide = jax.ShapeDtypeStruct((slots, width), f32)
    low = jax.ShapeDtypeStruct((slots, width), bf16)
    probs = jax.ShapeDtypeStruct((H if keep else 4, slots, slots), bf16)
    here = pl.BlockSpec(memory_space=pltpu.VMEM)
    results = [wide, low, low, low, low, low, probs, low]
    outs = len(results) if keep else 2
    return pl.pallas_call(
        functools.partial(attn_forward_kernel, image),
        in_specs=[pl.BlockSpec(memory_space=pltpu.SMEM)] * 2 + [here] * 3,
        out_specs=[here] * outs,
        scratch_shapes=[pltpu.VMEM(r.shape, r.dtype) for r in results[outs:]]
        + [pltpu.VMEM((width, slots), bf16), pltpu.VMEM((width, slots), f32)],
        out_shape=results[:outs],
        compiler_params=pltpu.CompilerParams(vmem_limit_bytes=6 * 2**20),
        cost_estimate=pl.CostEstimate(
            flops=ATTN_COST * slots * width * width, bytes_accessed=attn_w.size * 2, transcendentals=slots * slots * H
        ),
        name="attn_forward",
    )(heights, widths, layer_input, attn_w, vecs)


def gelu_parts(pre):
    bell = jnp.exp2(pre * pre * (-0.5 * LOG2_E))
    scaled = 1.0 + jnp.abs(pre) * (0.3275911 * 0.5**0.5)
    near = pl.reciprocal(scaled, approx=True)
    near = near * (2.0 - scaled * near)
    tail = near * (0.5 * 1.061405429) - 0.5 * 1.453152027
    for coefficient in (1.421413741, -0.284496736, 0.254829592):
        tail = tail * near + 0.5 * coefficient
    tail = tail * near * bell
    return jnp.where(pre < 0.0, tail, 1.0 - tail), bell


def up_columns(w_ref, at):
    width = w_ref.shape[2]
    rows = width // LEAD
    chunk, column = at // width, at % width
    return w_ref[:, chunk * rows : (chunk + 1) * rows, column : column + TILE].reshape(width, TILE)


def mlp_up_kernel(keep_slope, pieces, *refs):
    second_refs, (w_ref, vec_ref, act_ref) = refs[:pieces], refs[pieces : pieces + 3]
    slope_ref = refs[pieces + 3] if keep_slope else None
    pre_refs = refs[-2:]
    slots, width = second_refs[0].shape
    hidden = act_ref.shape[1]

    def multiply(at):
        weight = up_columns(w_ref, at)
        for piece, second_ref in enumerate(second_refs):
            pre_refs[at // TILE % 2][piece * slots : (piece + 1) * slots, :] = dot(second_ref[...], weight)

    multiply(0)
    for at in range(0, hidden, TILE):
        if at + TILE < hidden:
            multiply(at + TILE)
        columns = slice(at, at + TILE)
        row = UP_BIAS + at // width
        bias = vec_ref[row : row + 1, at % width : at % width + TILE]
        for start in range(0, slots * pieces, MLP_CHUNK):
            here = slice(start, start + MLP_CHUNK)
            pre = pre_refs[at // TILE % 2][here, :] + bias
            below, bell = gelu_parts(pre)
            act_ref[here, columns] = (pre * below).astype(bf16)
            if keep_slope:
                slope_ref[here, columns] = (below + pre * bell * (0.5 / jnp.pi) ** 0.5).astype(bf16)


def mlp_up(second, mlp_w, vecs, keep_slope):
    slots, width = second[0].shape
    count = slots * len(second)
    hidden = mlp_w.shape[1] * LEAD // 2
    outs = 2 if keep_slope else 1
    here = pl.BlockSpec(memory_space=pltpu.VMEM)
    return pl.pallas_call(
        functools.partial(mlp_up_kernel, keep_slope, len(second)),
        in_specs=[here] * (len(second) + 2),
        out_specs=[here] * outs,
        out_shape=[jax.ShapeDtypeStruct((count, hidden), bf16)] * outs,
        scratch_shapes=[pltpu.VMEM((count, TILE), f32)] * 2,
        compiler_params=pltpu.CompilerParams(vmem_limit_bytes=6 * 2**20),
        cost_estimate=pl.CostEstimate(
            flops=MLP_COST * count * width * hidden,
            bytes_accessed=mlp_w.size + count * hidden * 4,
            transcendentals=2 * count * hidden,
        ),
        name="mlp_up",
    )(*second, mlp_w, vecs)


def mlp_down_kernel(pieces, act_ref, *refs):
    middle_refs, (w_ref, vec_ref, result_ref) = refs[:pieces], refs[pieces:]
    slots, width = middle_refs[0].shape
    hidden = act_ref.shape[1]
    bias = vec_ref[DOWN_BIAS : DOWN_BIAS + 1, :]
    for column in range(0, width, TILE):
        columns = slice(column, column + TILE)
        weight = w_ref[:, w_ref.shape[1] // 2 :, columns].reshape(hidden, TILE)
        for piece, middle_ref in enumerate(middle_refs):
            here = slice(piece * slots, (piece + 1) * slots)
            added = dot(act_ref[here, :], weight)
            result_ref[here, columns] = (added + (middle_ref[:, columns] + bias[:, columns])).astype(bf16)


def mlp_down(activated, middle, mlp_w, vecs):
    slots, width = middle[0].shape
    count = slots * len(middle)
    here = pl.BlockSpec(memory_space=pltpu.VMEM)
    return pl.pallas_call(
        functools.partial(mlp_down_kernel, len(middle)),
        in_specs=[here] * (len(middle) + 3),
        out_specs=here,
        out_shape=jax.ShapeDtypeStruct((count, width), bf16),
        compiler_params=pltpu.CompilerParams(vmem_limit_bytes=4 * 2**20),
        cost_estimate=pl.CostEstimate(
            flops=MLP_COST * count * width * activated.shape[1],
            bytes_accessed=mlp_w.size + count * width * 10,
            transcendentals=0,
        ),
        name="mlp_down",
    )(activated, *middle, mlp_w, vecs)


def mlp_backward_kernel(pieces, first, turn_pieces, slope_ref, *refs):
    if turn_pieces:
        count = 1 + 2 * turn_pieces
        last = len(refs) - 2
        turn_kernel(turn_pieces, *refs[:count], *refs[last - 4 : last])
        refs = (*refs[count : last - 4], *refs[last:])
    upstream_refs, middle_refs, refs = refs[:pieces], refs[pieces : 2 * pieces], refs[2 * pieces :]
    (w_ref, vec_ref), refs = refs[:2], refs[2:]
    grad_middle_refs, branch_refs, refs = refs[:pieces], refs[pieces : 2 * pieces], refs[2 * pieces :]
    grad_pre_ref, sums_ref, up_sum_ref, ga_refs = refs[0], refs[1], refs[2], refs[3:]
    slots, width = upstream_refs[0].shape
    hidden = slope_ref.shape[1]
    half = w_ref.shape[1] // 2

    step = LEAD // 4 * half

    def multiply(at):
        weight = w_ref[at // half : (at + step) // half, half:, :].reshape(step, width)
        for piece, upstream_ref in enumerate(upstream_refs):
            ga_refs[at // step % 2][piece * slots : (piece + 1) * slots, :] = dot_nt(upstream_ref[...], weight)

    multiply(0)
    for at in range(0, hidden, step):
        if at + step < hidden:
            multiply(at + step)
        sums = jnp.zeros((1, step), f32)
        for start in range(0, slots * pieces, MLP_CHUNK):
            here = slice(start, start + MLP_CHUNK)
            slope = slope_ref[first * slots + start : first * slots + start + MLP_CHUNK, at : at + step]
            pre = (ga_refs[at // step % 2][here, :] * slope.astype(f32)).astype(bf16)
            grad_pre_ref[here, at : at + step] = pre
            sums += column_sum(pre.astype(f32))
        up_sum_ref[at // width, :, at % width : at % width + step] = sums
    gain = vec_ref[GAIN_TWO : GAIN_TWO + 1, :]
    sums = [jnp.zeros((1, width), f32)] * 3
    for piece in range(pieces):
        rows = slice(piece * slots, (piece + 1) * slots)
        total = None
        for chunk in range(hidden // width):
            weight = w_ref[:, chunk * width // LEAD : (chunk + 1) * width // LEAD, :].reshape(width, width)
            added = dot_nt(grad_pre_ref[rows, chunk * width : (chunk + 1) * width], weight)
            total = added if total is None else total + added
        ga_refs[piece % 2][:slots, :] = total
        for at in range(0, slots, MLP_CHUNK):
            here = slice(at, at + MLP_CHUNK)
            upstream = upstream_refs[piece][here, :].astype(f32)
            grad = ga_refs[piece % 2][here, :]
            grad_mid, gain_terms = norm_back(middle_refs[piece][here, :], gain, grad)
            whole = upstream + grad_mid
            grad_middle_refs[piece][here, :] = whole
            branch_refs[piece][here, :] = whole.astype(bf16)
            sums = [old + column_sum(new) for old, new in zip(sums, (upstream, gain_terms, grad))]
    for row, value in enumerate(sums):
        sums_ref[row : row + 1, :] = value


def mlp_backward(upstream, slope, middle, mlp_w, vecs, image=0, turn=()):
    slots, width = middle[0].shape
    pieces = len(middle)
    count = slots * pieces
    parts = mlp_w.shape[1] * LEAD // (2 * width)
    here = pl.BlockSpec(memory_space=pltpu.VMEM)
    turn_in, turn_out = turn_arrays(*turn) if turn else ([], [])
    outs = pl.pallas_call(
        functools.partial(mlp_backward_kernel, pieces, image, (len(turn_in) - 1) // 2 if turn else 0),
        in_specs=[here] * (2 * pieces + 3 + len(turn_in)),
        out_specs=[here] * (2 * pieces + 3 + len(turn_out)),
        out_shape=[jax.ShapeDtypeStruct((slots, width), f32)] * pieces
        + [jax.ShapeDtypeStruct((slots, width), bf16)] * pieces
        + [
            jax.ShapeDtypeStruct((count, width * parts), bf16),
            jax.ShapeDtypeStruct((8, width), f32),
            jax.ShapeDtypeStruct((parts, 1, width), f32),
        ]
        + turn_out,
        scratch_shapes=[pltpu.VMEM((count, width), f32)] * 2,
        compiler_params=pltpu.CompilerParams(vmem_limit_bytes=8 * 2**20),
        cost_estimate=pl.CostEstimate(
            flops=2 * MLP_COST * count * width * width * parts,
            bytes_accessed=mlp_w.size * 2 + count * width * (10 + 4 * parts),
            transcendentals=0,
        ),
        name="mlp_backward",
    )(slope, *turn_in, *upstream, *middle, mlp_w, vecs)
    return outs[:pieces], outs[pieces : 2 * pieces], *outs[2 * pieces :]


def attn_backward_kernel(
    grad_middle_ref, branch_ref, x_ref, q_ref, k_ref, v_ref, probs_ref, w_ref, vec_ref,
    grad_in_ref, grad_low_ref, gq_ref, gk_ref, gv_ref, sums_ref,
    ga_ref, gat_ref, qt_ref, kt_ref, gqt_ref, gkt_ref, gvt_ref,
):
    slots, width = x_ref.shape
    head_size = width // H
    scale = head_size ** (-0.5)
    ga = dot_nt(branch_ref[...], weight_part(w_ref, 3)).astype(bf16)
    ga_ref[...] = ga
    gat_ref[...] = ga.T
    qt_ref[...] = q_ref[...].T
    kt_ref[...] = k_ref[...].T
    for head in range(H):
        start, low = head_window(head, head_size, width)
        here = slice(head * head_size, (head + 1) * head_size)
        own = only_head(ga_ref[:, start : start + 256], low, head_size)
        grad_probs = dot_nt(v_ref[:, start : start + 256], own)
        pieces = []
        for at in range(0, slots, 128):
            probs = probs_ref[head, :, at : at + 128].astype(f32)
            grad = grad_probs[:, at : at + 128]
            total = jnp.sum(probs * grad, axis=0, keepdims=True)
            pieces.append((probs * (grad - total)).astype(bf16))
        grad_scores = jnp.concatenate(pieces, axis=1)
        gvt_ref[here, :] = dot_nt(gat_ref[here, :], probs_ref[head])
        gqt_ref[here, :] = dot(kt_ref[here, :], grad_scores) * scale
        gkt_ref[here, :] = dot_nt(qt_ref[here, :], grad_scores) * scale
    gq_ref[...] = gqt_ref[...].T.astype(bf16)
    gk_ref[...] = gkt_ref[...].T.astype(bf16)
    gv_ref[...] = gvt_ref[...].T.astype(bf16)
    grad_normed = dot_nt(gq_ref[...], weight_part(w_ref, 0))
    grad_normed += dot_nt(gk_ref[...], weight_part(w_ref, 1))
    grad_normed += dot_nt(gv_ref[...], weight_part(w_ref, 2))
    grad_in_ref[...] = grad_normed
    gain = vec_ref[GAIN_ONE : GAIN_ONE + 1, :]
    sums = [jnp.zeros((1, width), f32)] * 5
    for at in range(0, slots, MLP_CHUNK):
        rows = slice(at, at + MLP_CHUNK)
        grad = grad_in_ref[rows, :]
        grad_norm, gain_terms = norm_back(x_ref[rows, :].astype(f32), gain, grad)
        total = grad_middle_ref[rows, :] + grad_norm
        grad_in_ref[rows, :] = total
        grad_low_ref[rows, :] = total.astype(bf16)
        terms = (
            gq_ref[rows, :].astype(f32), gv_ref[rows, :].astype(f32), branch_ref[rows, :].astype(f32),
            gain_terms, grad,
        )
        sums = [old + column_sum(new) for old, new in zip(sums, terms)]

    for row, value in enumerate(sums):
        sums_ref[row : row + 1, :] = value


def attn_backward(grad_middle, branch, layer_input, saved, attn_w, vecs):
    queries, key_rows, values, probs = saved
    slots, width = layer_input.shape
    low = jax.ShapeDtypeStruct((slots, width), bf16)
    here = pl.BlockSpec(memory_space=pltpu.VMEM)
    flipped = pltpu.VMEM((width, slots), bf16)
    flipped_wide = pltpu.VMEM((width, slots), f32)
    return pl.pallas_call(
        attn_backward_kernel,
        in_specs=[here] * 9,
        out_specs=[here] * 6,
        out_shape=[jax.ShapeDtypeStruct((slots, width), f32)] + [low] * 4 + [jax.ShapeDtypeStruct((8, width), f32)],
        scratch_shapes=[pltpu.VMEM((slots, width), bf16)] + [flipped] * 3 + [flipped_wide] * 3,
        compiler_params=pltpu.CompilerParams(vmem_limit_bytes=8 * 2**20),
        cost_estimate=pl.CostEstimate(
            flops=ATTN_COST * slots * width * width, bytes_accessed=attn_w.size * 2, transcendentals=0
        ),
        name="attn_backward",
    )(grad_middle, branch, layer_input, queries, key_rows, values, probs, attn_w, vecs)


def ring_slot(owner, me):
    there, here = place_of(lax.div(owner, 2)), place_of(lax.div(me, 2))
    return lax.rem(there - here + RING, RING)


def store_block(own_ref, peer_ref, owner, core, rows, value):
    me = lax.axis_index("dp")
    slot = ring_slot(owner, me)

    @pl.when(lax.rem(me, 2) == core)
    def _():
        own_ref[slot, rows, :] = value

    @pl.when(lax.rem(me, 2) != core)
    def _():
        peer_ref[slot, rows, :] = value


def scatter_shapes(rows, width):
    return [jax.ShapeDtypeStruct((RING, rows, width), bf16)] * 2


def joined(refs, scratch_ref):
    slots = refs[0].shape[0]
    for piece, ref in enumerate(refs):
        scratch_ref[piece * slots : (piece + 1) * slots, :] = ref[...]


def flipped(refs, scratch_ref):
    slots = refs[0].shape[0]
    for piece, ref in enumerate(refs):
        scratch_ref[:, piece * slots : (piece + 1) * slots] = ref[...].T


def turn_kernel(pieces, act_ref, *refs):
    second_refs, attended_refs, outs = refs[:pieces], refs[pieces : 2 * pieces], refs[2 * pieces :]
    own_act, peer_act, own_small, peer_small = outs
    slots, width = second_refs[0].shape
    core = lax.rem(lax.axis_index("dp"), 2)
    rows, act_rows = own_small.shape[1] // 2, own_act.shape[1]

    def put(own_ref, peer_ref, owner, here, columns, value):
        @pl.when(core == owner % 2)
        def _():
            own_ref[owner // 2, here, columns] = value

        @pl.when(core != owner % 2)
        def _():
            peer_ref[owner // 2, here, columns] = value

    for piece in range(pieces):
        columns = slice(piece * slots, (piece + 1) * slots)
        for at in range(0, act_ref.shape[1], width):
            turned = act_ref[columns, at : at + width].T
            for first in range(0, width, act_rows):
                put(own_act, peer_act, (at + first) // act_rows, slice(None), columns, turned[first : first + act_rows])
        for part, side in enumerate((second_refs, attended_refs)):
            turned = side[piece][...].T
            for owner in range(LEAD):
                here = slice(part * rows, (part + 1) * rows)
                put(own_small, peer_small, owner, here, columns, turned[owner * rows : (owner + 1) * rows])


def turn_arrays(activated, second, attended):
    count, hidden = activated.shape
    width = second[0].shape[1]
    big = jax.ShapeDtypeStruct((RING, hidden // LEAD, count), bf16)
    small = jax.ShapeDtypeStruct((RING, 2 * width // LEAD, count), bf16)
    return [activated, *second, *attended], [big, big, small, small]


def grad_down_kernel(pieces, own_ref, got_ref, *refs):
    mine, theirs, (out_ref, right_ref, got_right_ref) = refs[:pieces], refs[pieces : 2 * pieces], refs[2 * pieces :]
    joined(mine, right_ref)
    joined(theirs, got_right_ref)
    me = lax.axis_index("dp")
    chips, rows, count = own_ref.shape
    for chip in range(0, chips, 2):
        left, got = (ref[chip : chip + 2].reshape(2 * rows, count) for ref in (own_ref, got_ref))
        value = (dot(left, right_ref[...]) + dot(got, got_right_ref[...])).astype(bf16)
        for at in range(2):
            out_ref[ring_slot(2 * (chip + at), me)] = value[at * rows : (at + 1) * rows]


def grad_down_blocks(own_act, got_act, upstream, got_upstream):
    slots, width = upstream[0].shape
    chips, rows, count = own_act.shape
    here = pl.BlockSpec(memory_space=pltpu.VMEM)
    return pl.pallas_call(
        functools.partial(grad_down_kernel, len(upstream)),
        in_specs=[here] * (2 + 2 * len(upstream)),
        out_specs=here,
        out_shape=jax.ShapeDtypeStruct((RING, rows, width), bf16),
        scratch_shapes=[pltpu.VMEM((count, width), bf16)] * 2,
        compiler_params=pltpu.CompilerParams(vmem_limit_bytes=8 * 2**20),
        cost_estimate=pl.CostEstimate(
            flops=MLP_COST * 2 * count * width * chips * rows, bytes_accessed=count * chips * rows * 4, transcendentals=0
        ),
        name="grad_down",
    )(own_act, got_act, *upstream, *got_upstream)


def grad_up_kernel(pieces, own_ref, got_ref, *refs):
    groups, (out_ref, left_ref, right_ref) = refs[: 4 * pieces], refs[4 * pieces :]
    pre_refs, branch_refs = groups[: 2 * pieces], groups[2 * pieces :]
    me = lax.axis_index("dp")
    chips, both_rows, count = own_ref.shape
    rows = both_rows // 2
    width = branch_refs[0].shape[1]
    parts = pre_refs[0].shape[1] // width
    slots = pre_refs[0].shape[0]

    def lefts(part):
        for at, ref in enumerate((own_ref, got_ref)):
            side = ref[:, part * rows : (part + 1) * rows, :].reshape(chips * rows, count)
            left_ref[:, at * count : (at + 1) * count] = side

    def store(part):
        value = dot(left_ref[...], right_ref[...]).astype(bf16)
        for chip in range(chips):
            here = slice(part * rows, (part + 1) * rows)
            out_ref[ring_slot(2 * chip, me), here, :] = value[chip * rows : (chip + 1) * rows]

    lefts(0)
    for part in range(parts):
        for piece, ref in enumerate(pre_refs):
            right_ref[piece * slots : (piece + 1) * slots, :] = ref[:, part * width : (part + 1) * width]
        store(part)
    lefts(1)
    joined(branch_refs, right_ref)
    store(parts)


def grad_up_blocks(own_small, got_small, grad_pre, branch):
    width = branch[0].shape[1]
    hidden = grad_pre[0].shape[1]
    chips, both_rows, count = own_small.shape
    rows = hidden // LEAD + both_rows // 2
    here = pl.BlockSpec(memory_space=pltpu.VMEM)
    return pl.pallas_call(
        functools.partial(grad_up_kernel, len(branch) // 2),
        in_specs=[here] * (2 + 2 * len(branch)),
        out_specs=here,
        out_shape=jax.ShapeDtypeStruct((RING, rows, width), bf16),
        scratch_shapes=[pltpu.VMEM((chips * both_rows // 2, 2 * count), bf16), pltpu.VMEM((2 * count, width), bf16)],
        compiler_params=pltpu.CompilerParams(vmem_limit_bytes=8 * 2**20),
        cost_estimate=pl.CostEstimate(
            flops=MLP_COST * count * width * hidden, bytes_accessed=count * hidden * 4, transcendentals=0
        ),
        name="grad_up",
    )(own_small, got_small, *grad_pre, *branch)


def grad_qkv_kernel(pieces, *refs):
    left_refs, rights = refs[:pieces], refs[pieces : 4 * pieces]
    attn_sums, mlp_sums, up_sums = (refs[at * pieces : (at + 1) * pieces] for at in (4, 5, 6))
    own_ref, peer_ref, left_ref, right_ref, vec_ref = refs[7 * pieces :]
    width = left_refs[0].shape[1]
    rows = width // LEAD
    flipped(left_refs, left_ref)
    for part in range(3):
        joined(rights[part * pieces : (part + 1) * pieces], right_ref)
        value = dot(left_ref[...], right_ref[...]).astype(bf16)
        for owner in range(LEAD):
            here = slice(part * rows, (part + 1) * rows)
            store_block(own_ref, peer_ref, owner, owner % 2, here, value[owner * rows : (owner + 1) * rows])
    vec_ref[...] = jnp.zeros_like(vec_ref)
    for name, refs_of, row in (
        (Q_BIAS, attn_sums, 0), (V_BIAS, attn_sums, 1), (OUT_BIAS, attn_sums, 2), (DOWN_BIAS, mlp_sums, 0),
        (GAIN_ONE, attn_sums, 3), (SHIFT_ONE, attn_sums, 4), (GAIN_TWO, mlp_sums, 1), (SHIFT_TWO, mlp_sums, 2),
    ):
        vec_ref[name : name + 1, :] = sum(ref[row : row + 1, :] for ref in refs_of)
    for part in range(up_sums[0].shape[0]):
        vec_ref[UP_BIAS + part : UP_BIAS + part + 1, :] = sum(ref[part] for ref in up_sums)
    vectors = vec_ref[...].astype(bf16)
    here = slice(3 * rows, 3 * rows + VEC_ROWS)
    for slot in range(RING):
        own_ref[slot, here, :] = vectors
        peer_ref[slot, here, :] = vectors


def grad_qkv_blocks(normed, rights, attn_sums, mlp_sums, up_sums):
    slots, width = normed[0].shape
    count = slots * len(normed)
    arrays = [*normed, *(piece for right in rights for piece in right), *attn_sums, *mlp_sums, *up_sums]
    rows = 3 * width // LEAD + VEC_ROWS
    return pl.pallas_call(
        functools.partial(grad_qkv_kernel, len(normed)),
        in_specs=[pl.BlockSpec(memory_space=pltpu.VMEM)] * len(arrays),
        out_specs=[pl.BlockSpec(memory_space=pltpu.VMEM)] * 2,
        out_shape=scatter_shapes(rows, width),
        scratch_shapes=[
            pltpu.VMEM((width, count), bf16), pltpu.VMEM((count, width), bf16), pltpu.VMEM((VEC_ROWS, width), f32)
        ],
        compiler_params=pltpu.CompilerParams(vmem_limit_bytes=6 * 2**20),
        cost_estimate=pl.CostEstimate(
            flops=3 * MLP_COST * count * width * width, bytes_accessed=len(arrays) * slots * width * 2, transcendentals=0
        ),
        name="grad_qkv",
    )(*arrays)


VECS = ("q_bias", "v_bias", "out_bias", "down_bias", "gain_one", "shift_one", "gain_two", "shift_two")


def solution(mesh):
    dp_size = mesh.shape["dp"]
    ringed = dp_size == 2 * RING

    def gathered_whole(qkv, out, up, down, vectors):
        width = out.shape[1]
        gathered = [lax.all_gather(w, "dp", axis=0, tiled=True) for w in (qkv, out, up, down)]
        blocked = [w.reshape(LEAD, -1, w.shape[1]) for w in gathered]
        fold = lambda w: w.reshape(LEAD, w.shape[1], -1, width).transpose(0, 2, 1, 3).reshape(LEAD, -1, width)
        first = jnp.concatenate([fold(blocked[0]), blocked[1], jnp.zeros((LEAD, VEC_ROWS, width), bf16)], 1)
        whole = lambda name: lax.all_gather(vectors[name], "dp", axis=0, tiled=True)
        vecs = jnp.concatenate([jnp.stack([whole(name) for name in VECS]), whole("up_bias").reshape(-1, width)])
        vecs = jnp.pad(vecs.astype(f32), ((0, VEC_ROWS - vecs.shape[0]), (0, 0)))
        return first, jnp.concatenate([fold(blocked[2]), blocked[3]], 1), vecs

    def own_vectors(block):
        me = lax.axis_index("dp")
        width = block.shape[1]
        rows = width // LEAD
        small = lax.dynamic_slice(block, (0, me * rows), (len(VECS), rows))
        parts = (3 * LEAD + LEAD) * rows // width
        size = parts * rows
        in_row = width // size
        own = {name: small[at] for at, name in enumerate(VECS)}
        own["up_bias"] = lax.dynamic_slice(block, (len(VECS) + me // in_row, me % in_row * size), (1, size))[0]
        return own

    def shards(
        tokens, cotangent, heights, widths, qkv_weight, out_weight, up_weight, down_weight,
        q_bias, v_bias, out_bias, up_bias, down_bias, gain_one, shift_one, gain_two, shift_two,
    ):
        leading = lax.axis_index("section") == 0
        width = tokens.shape[1]
        images = heights.shape[0]
        each = range(images)
        rows = width // LEAD
        cut = lambda array: jnp.split(array, images)
        vectors = dict(
            q_bias=q_bias[0], v_bias=v_bias[0], out_bias=out_bias[0], up_bias=up_bias[0], down_bias=down_bias[0],
            gain_one=gain_one[0], shift_one=shift_one[0], gain_two=gain_two[0], shift_two=shift_two[0],
        )
        inputs, cotangents = cut(tokens), cut(cotangent)

        attention = lambda x, image, keep: attn_forward(x, attn_w, vecs, heights, widths, image, keep)
        if ringed:
            small = jnp.stack([vectors[name] for name in VECS])
            one, two = pack_first(qkv_weight[0], out_weight[0], small, vectors["up_bias"][None])
            g, h = gather_start(one), gather_start(two)
            u, d = gather_start(pack_columns(up_weight[0], width)), gather_start(down_weight[0])
            for _ in range(RING // 2 - 2):
                g, h = gather_step(g), gather_step(h)
            g["mine"], u["mine"] = tie(g["mine"], u["mine"])
            h["mine"], d["mine"] = tie(h["mine"], d["mine"])
            g, h = gather_step(g), gather_step(h)
            g, h, u, d = (gather_step(state) for state in (g, h, u, d))
            attn_w, vecs = assemble([g, h], True)
            front = [attention(inputs[0], 0, False)]
            attn_w, front, u["mine"], d["mine"] = tie(attn_w, front, u["mine"], d["mine"])
            u, d = gather_step(u), gather_step(d)
            front += [attention(inputs[image], image, False) for image in each[1:]]
            front, u["mine"], d["mine"] = tie(front, u["mine"], d["mine"])
            for _ in range(u["step"], RING // 2):
                u, d = gather_step(u), gather_step(d)
            mlp_w = assemble([u, d])
        else:
            attn_w, mlp_w, vecs = gathered_whole(
                qkv_weight[0], out_weight[0], up_weight[0], down_weight[0], vectors
            )
            front = [attention(inputs[image], image, False) for image in each]
        received = []
        for image in each:
            (activated,) = mlp_up(front[image][1:], mlp_w, vecs, False)
            sent = mlp_down(activated, front[image][:1], mlp_w, vecs)
            front, sent = tie(front, sent)
            received.append(lax.ppermute(sent, "section", [(0, 1)]))

        layer_input, kept = [], []
        for image in each:
            layer_input.append(jnp.where(leading, inputs[image], received[image]))
            kept.append(attention(layer_input[image], image, True))
            kept, received = tie(kept, received)
        middle, second, normed, queries, key_rows, values, probs, attended = zip(*kept)
        activated, slope = mlp_up(second, mlp_w, vecs, True)

        back_attn = lambda grad, branch, image: attn_backward(
            grad[image], branch[image], layer_input[image],
            (queries[image], key_rows[image], values[image], probs[image]), attn_w, vecs,
        )
        grad_middle, branch = mlp_backward(cotangents, slope, middle, mlp_w, vecs)[:2]
        arriving = []
        for image in each:
            to_send = back_attn(grad_middle, branch, image)[1]
            grad_middle, branch, activated, to_send = tie(grad_middle, branch, activated, to_send)
            arriving.append(lax.ppermute(to_send, "section", [(1, 0)]))
        upstream, back = [jnp.where(leading, arriving[0], cotangents[0])], []

        def back_one(image, turn=()):
            outs = mlp_backward(upstream[image : image + 1], slope, middle[image : image + 1], mlp_w, vecs, image, turn)
            back.append(outs[:5])
            return outs[5:]

        turned = back_one(0, (activated, second, attended) if ringed else ())
        got_pre, got_branch = [], []

        def exchange(image):
            got_pre.append(across(back[image][2]))
            got_branch.append(across(back[image][1][0]))

        back, activated, arriving, turned = tie(back, activated, arriving, turned)
        if ringed:
            own_act, peer_act, own_small, peer_small = turned
            got_act, got_small = across(peer_act), across(peer_small)
        else:
            result = mlp_down(activated, middle, mlp_w, vecs)
        upstream += [jnp.where(leading, arriving[image], cotangents[image]) for image in each[1:]]
        if ringed:
            got_upstream = [across(array) for array in upstream]
            exchange(0)
            d = scatter_start(grad_down_blocks(own_act, got_act, upstream, got_upstream))
            d, upstream = scatter_step(d, upstream)
            for image in each[1:]:
                back_one(image)
            d, back, got_pre, got_branch = tie(d, back, got_pre, got_branch)
            d, back = scatter_step(d, back)
            grad_middle, branch, grad_pre, mlp_sums, up_sums = zip(*back)
            grad_middle, branch = [g for (g,) in grad_middle], [g for (g,) in branch]
            for image in each[1:]:
                exchange(image)
            held = (grad_middle, branch)
            attn_back = [back_attn(*held, 0)]
            d, attn_back, held, grad_pre, activated = tie(d, attn_back, held, grad_pre, activated)
            d, (grad_pre, activated) = scatter_step(d, (grad_pre, activated))
            result = mlp_down(activated, middle, mlp_w, vecs)
            u = scatter_start(grad_up_blocks(own_small, got_small, [*grad_pre, *got_pre], [*branch, *got_branch]))
            d, u, held, result = tie(d, u, held, result)
            u, held = scatter_step(u, held)
            d, held = scatter_step(d, held)
            attn_back += [back_attn(*held, image) for image in each[1:]]
            d, u, attn_back = tie(d, u, attn_back)
            u, attn_back = scatter_step(u, attn_back)
        else:
            for image in each[1:]:
                back_one(image)
            grad_middle, branch, grad_pre, mlp_sums, up_sums = zip(*back)
            grad_middle, branch = [g for (g,) in grad_middle], [g for (g,) in branch]
            attn_back = [back_attn(grad_middle, branch, image) for image in each]
            grad_whole = jnp.concatenate([each_back[0] for each_back in attn_back])
        grad_input, _, gq, gk, gv, attn_sums = zip(*attn_back)
        if ringed:
            q = scatter_start(*grad_qkv_blocks(normed, (gq, gk, gv), attn_sums, mlp_sums, up_sums))
            parts = mlp_w.shape[1] // rows - 4
            ends = RING // 2 + 1
            q = scatter_step(q)[0]
            (g_down,) = scatter_sum(d, [(0, d["own"].shape[1], 1)])
            grad_whole = jnp.concatenate(grad_input)
            q = scatter_step(q)[0]
            q, g_down = tie(q, g_down)
            q = scatter_step(q)[0]
            q, grad_whole = tie(q, grad_whole)
            q = scatter_step(q)[0]
            while u["step"] < ends:
                u = scatter_step(u)[0]
            g_up, g_out = scatter_sum(u, [(0, rows, parts), (parts * rows, rows, 1)])
            q = scatter_step(q)[0]
            g_qkv, vec_sums = scatter_sum(q, [(0, rows, 3), (3 * rows, VEC_ROWS, 1)])
            g_vecs = own_vectors(vec_sums)
        else:
            attn_sums = sum(attn_sums)
            sums = dict(zip(("q_bias", "v_bias", "out_bias", "gain_one", "shift_one"), attn_sums))
            sums |= dict(zip(("down_bias", "gain_two", "shift_two"), sum(mlp_sums)))
            sums["up_bias"] = sum(up_sums).reshape(-1)
            scatter = lambda a: lax.psum_scatter(a, "dp", scatter_dimension=0, tiled=True)
            whole = lambda pieces: jnp.concatenate(pieces)
            outer = lambda a, b: lax.dot_general(a, b, TN, preferred_element_type=f32)
            g_down = scatter(outer(activated, whole(upstream)))
            g_up = scatter(outer(whole(second), whole(grad_pre)))
            g_qkv = scatter(jnp.concatenate([outer(whole(normed), whole(part)) for part in (gq, gk, gv)], 1))
            g_out = scatter(outer(whole(attended), whole(branch)))
            g_vecs = {name: scatter(value) for name, value in sums.items()}
        return (
            result[None], grad_whole[None],
            g_qkv[None], g_out[None], g_up[None], g_down[None],
            *(
                g_vecs[name][None]
                for name in (
                    "q_bias", "v_bias", "out_bias", "up_bias", "down_bias",
                    "gain_one", "shift_one", "gain_two", "shift_two",
                )
            ),
        )

    rows_spec = P("dp", None)
    three, two = P("section", "dp", None), P("section", "dp")
    return jax.shard_map(
        shards,
        mesh=mesh,
        in_specs=(rows_spec, rows_spec, P("dp"), P("dp")) + (three,) * 4 + (two,) * 9,
        out_specs=(three,) * 6 + (two,) * 9,
        check_vma=False,
    )
```
